128 devices in a mesh: dp: 4 (over z), rows: 8 (over x, core), cols: 4 (over y).
Axes of the slice: x: 4, y: 4, z: 4, core: 2. Of those that a mesh axis runs over, the one named last changes fastest.
Arguments:
- gated_hidden_input: bfloat16 [1024, 28672], P('dp', 'rows'), may hold values from -6 to 6
- output_gradient: bfloat16 [1024, 8192], P('dp', 'cols'), may hold values from -6 to 6
- frozen_down_weight: bfloat16 [28672, 8192], P('rows', 'cols'), may hold values from -8 to 8
- input_side_factor: bfloat16 [28672, 64], P('rows'), may hold values from -0.03125 to 0.03125
- output_side_factor: bfloat16 [64, 8192], P(None, 'cols'), may hold values from -0.375 to 0.375
- magnitude: float32 [8192], P('cols'), may hold values from 0.3 to 3
Outputs:
- input_grad: bfloat16 [28672, 1024], P(('rows', 'cols'), 'dp')
- lora_a_grad: float32 [28672, 64], P('rows')
- lora_b_grad: float32 [64, 8192], P(None, 'cols')
- magnitude_grad: float32 [8192], P('cols')
The draws below stay inside these ranges and needn't reach their ends.
All inputs are finite; a program needn't handle non-finite values.
Results may differ from the reference program's by a relative error of at most 0.0032.
Values sent between devices are 32-bit elements; how exact they have to be, the bound alone decides.
No kernel may reach another device: no remote copies, remote signals or barrier semaphores. Data moves between devices by JAX's collectives and lax.ppermute only.
A program may use at most 192 MiB of HBM per device.

```python
import math
import jax
import jax.numpy as jnp
from jax import lax

MODEL_WIDTH = 8192
HIDDEN_UNITS = 28672
ADAPTER_RANK = 64
TOK_DEV = 256
TOKENS = 1024
N_DP = 4


def common_factors(key):
    key_tok, key_row, key_col = jax.random.split(key, 3)
    position = jnp.arange(TOKENS, dtype=jnp.float32) / TOKENS
    token_factor = jax.random.normal(key_tok, (TOKENS,), jnp.float32) * jnp.power(3.0, 0.5 * position)
    row_factor = jax.random.normal(key_row, (HIDDEN_UNITS,), jnp.float32)
    col_factor = jax.random.normal(key_col, (MODEL_WIDTH,), jnp.float32)
    return (token_factor, row_factor, col_factor)


def noise_field(key, shape):
    return jax.random.normal(key, shape, jnp.float32)


def draw_gated_hidden_input(key, part):
    token_factor, row_factor, col_factor = common_factors(key)
    key = jax.random.fold_in(key, 21)
    mixing = 0.6324555 * float(TOK_DEV) ** (-0.25)
    base = noise_field(key, (TOKENS, HIDDEN_UNITS))
    values = base + mixing * token_factor[:, None] * row_factor[None, :]
    return jnp.clip(values, -6.0, 6.0).astype(jnp.bfloat16)


def draw_output_gradient(key, part):
    token_factor, row_factor, col_factor = common_factors(key)
    key = jax.random.fold_in(key, 31)
    mixing = 0.6324555 * float(TOK_DEV) ** (-0.25)
    base = noise_field(key, (TOKENS, MODEL_WIDTH))
    values = base + mixing * token_factor[:, None] * col_factor[None, :]
    return jnp.clip(values, -6.0, 6.0).astype(jnp.bfloat16)


def draw_frozen_down_weight(key, part):
    token_factor, row_factor, col_factor = common_factors(key)
    key = jax.random.fold_in(key, 11)
    key_base, key_rows, key_cols = jax.random.split(key, 3)
    position = jnp.arange(HIDDEN_UNITS, dtype=jnp.float32) / HIDDEN_UNITS
    row_scale = jnp.power(10.0, position) * jnp.exp(jax.random.uniform(key_rows, (HIDDEN_UNITS,), jnp.float32, -0.7, 0.7))
    col_scale = jnp.exp(jax.random.uniform(key_cols, (MODEL_WIDTH,), jnp.float32, 0.0, 2.302585))
    base = jax.random.normal(key_base, (HIDDEN_UNITS, MODEL_WIDTH), jnp.float32)
    base = base + row_factor[:, None] * col_factor[None, :]
    base = jnp.clip(base, -6.0, 6.0)
    values = base * row_scale[:, None] * col_scale[None, :] / jnp.sqrt(43.0 * HIDDEN_UNITS)
    return jnp.clip(values, -8.0, 8.0).astype(jnp.bfloat16)


def steps_of(key, shape, cuts, least, largest):
    level, own = 1.0, jax.random.fold_in(key, 6)
    for dim, parts in cuts:
        heights = jnp.exp(jax.random.uniform(jax.random.fold_in(own, dim), (parts,), jnp.float32, least / len(cuts), largest / len(cuts)))
        level = level * jnp.repeat(heights, shape[dim] // parts).reshape([-1 if axis == dim else 1 for axis in range(len(shape))])
    return level


def gaussian(own_key, extent, width, bound, cuts=(), kind=jnp.bfloat16):
    level = steps_of(own_key, extent, cuts, -0.22, 0.18) if cuts else 1.0
    array = jax.random.normal(own_key, extent, jnp.float32) * width * level
    return jnp.minimum(jnp.maximum(array, -bound), bound).astype(kind)


def setup_inputs(seed: int = 0) -> dict:
    keys = jax.random.split(jax.random.key(seed), 7)
    gated_hidden_input = draw_gated_hidden_input(jax.random.fold_in(keys[6], 71), 0)
    output_gradient = draw_output_gradient(jax.random.fold_in(keys[6], 71), 0)
    frozen_down_weight = draw_frozen_down_weight(jax.random.fold_in(keys[6], 71), 0)
    input_side_factor = gaussian(keys[3], (HIDDEN_UNITS, ADAPTER_RANK), HIDDEN_UNITS ** -0.5, 0.03125, ((0, 8),))
    output_side_factor = gaussian(keys[4], (ADAPTER_RANK, MODEL_WIDTH), (4 * ADAPTER_RANK) ** -0.5, 0.375, ((1, 4),))
    magnitude = jnp.clip(jnp.exp(math.log(3.0) - 2.3025851 * jax.random.uniform(keys[5], (MODEL_WIDTH,), jnp.float32) ** steps_of(keys[5], (MODEL_WIDTH,), ((0, 4),), -0.2, 0.2)), 0.3, 3.0)
    return dict(gated_hidden_input=gated_hidden_input, output_gradient=output_gradient, frozen_down_weight=frozen_down_weight, input_side_factor=input_side_factor, output_side_factor=output_side_factor, magnitude=magnitude)


EPS = 1e-06

def reference(gated_hidden_input, output_gradient, frozen_down_weight, input_side_factor, output_side_factor, magnitude):
    low_rank_product = jnp.dot(input_side_factor, output_side_factor, preferred_element_type=jnp.float32)
    merged = (frozen_down_weight.astype(jnp.float32) + 2.0 * low_rank_product).astype(jnp.bfloat16)
    merged_wide = merged.astype(jnp.float32)
    squares = lax.optimization_barrier(jnp.sum(merged_wide * merged_wide, axis=0)) + EPS
    norms = jnp.sqrt(squares)
    scale = magnitude / norms
    scaled = (output_gradient.astype(jnp.float32) * scale).astype(jnp.bfloat16)
    input_grad = lax.dot_general(merged, scaled, (((1,), (1,)), ((), ())), preferred_element_type=jnp.float32).astype(jnp.bfloat16)
    projected = jnp.dot(gated_hidden_input, merged, preferred_element_type=jnp.float32)
    inner = lax.optimization_barrier(jnp.sum(projected * output_gradient.astype(jnp.float32), axis=0))
    gamma = float(TOKENS) ** (-0.5)
    magnitude_grad = gamma * inner / (norms * float(HIDDEN_UNITS) ** 0.5)
    correction = merged_wide * (inner / (N_DP * squares))
    input_factor_total = jnp.zeros((HIDDEN_UNITS, ADAPTER_RANK), jnp.float32)
    output_factor_total = jnp.zeros((ADAPTER_RANK, MODEL_WIDTH), jnp.float32)
    for group in range(N_DP):
        acts_group = gated_hidden_input[group * TOK_DEV:(group + 1) * TOK_DEV]
        grads_group = output_gradient[group * TOK_DEV:(group + 1) * TOK_DEV]
        weight_grad = lax.dot_general(acts_group, grads_group, (((0,), (0,)), ((), ())), preferred_element_type=jnp.float32)
        direction_gradient = (scale * (weight_grad - correction)).astype(jnp.bfloat16)
        input_factor_total = input_factor_total + lax.dot_general(direction_gradient, output_side_factor, (((1,), (1,)), ((), ())), preferred_element_type=jnp.float32)
        output_factor_total = output_factor_total + lax.dot_general(input_side_factor, direction_gradient, (((0,), (0,)), ((), ())), preferred_element_type=jnp.float32)
    return (input_grad, 2.0 * gamma * input_factor_total, 2.0 * gamma * output_factor_total, magnitude_grad)
```

```python
import functools

import jax
import jax.numpy as jnp
from jax import lax
from jax.experimental import pallas as pl
from jax.experimental.pallas import tpu as pltpu
from jax.sharding import PartitionSpec as P

EPS = 1e-06
F32 = jnp.float32
BF16 = jnp.bfloat16
MIB = 1024 * 1024

ANY = pl.BlockSpec(memory_space=pl.ANY)
VMEM = pl.BlockSpec(memory_space=pltpu.VMEM)


def nn(a, b):
    return lax.dot_general(a, b, (((1,), (0,)), ((), ())), preferred_element_type=F32)


def nt(a, b):
    return lax.dot_general(a, b, (((1,), (1,)), ((), ())), preferred_element_type=F32)


def tn(a, b):
    return lax.dot_general(a, b, (((0,), (0,)), ((), ())), preferred_element_type=F32)


def hi_lo(value):
    hi = value.astype(BF16)
    lo = (value - hi.astype(F32)).astype(BF16)
    return jnp.concatenate([hi, lo], axis=0)


def fold(value):
    half = value.shape[0] // 2
    return value[:half] + value[half:]


def call(kernel, outs, specs, *args, scratch=(), vmem=16, flops=0, data=0):
    return pl.pallas_call(
        kernel,
        out_shape=outs,
        in_specs=specs,
        out_specs=[VMEM for _ in outs],
        scratch_shapes=list(scratch),
        compiler_params=pltpu.CompilerParams(vmem_limit_bytes=vmem * MIB),
        cost_estimate=pl.CostEstimate(flops=flops, bytes_accessed=data, transcendentals=0),
    )(*args)


def out(shape, dtype=F32):
    return jax.ShapeDtypeStruct(shape, dtype)


def merge_kernel(
    steps, w_ref, x_ref, a_ref, b_ref, dy_ref, m_ref, stat_ref, bq_ref, am_ref,
    xa, b2, dy, acc, qt, sq, w_sem, x_sem, a_sem, b_sem, dy_sem,
):
    rows, cols = w_ref.shape
    toks = x_ref.shape[0]
    step = rows // steps
    tile = 256
    b_copy = pltpu.make_async_copy(b_ref, b2, b_sem)
    dy_copy = pltpu.make_async_copy(dy_ref, dy, dy_sem)
    a_copy = pltpu.make_async_copy(a_ref, xa.at[toks:], a_sem)

    def w_copy(i):
        part = pl.ds(pl.multiple_of(i * step, step), step)
        return pltpu.make_async_copy(w_ref.at[part], m_ref.at[part], w_sem.at[i])

    def x_copy(i):
        part = pl.ds(pl.multiple_of(i * step, step), step)
        return pltpu.make_async_copy(x_ref.at[:, part], xa.at[:toks, part], x_sem.at[i])

    b_copy.start()
    a_copy.start()
    for i in range(steps):
        w_copy(i).start()
        x_copy(i).start()
    dy_copy.start()
    acc[...] = jnp.zeros_like(acc)
    qt[...] = jnp.zeros_like(qt)
    sq[...] = jnp.zeros_like(sq)
    b_copy.wait()
    a_copy.wait()
    b2[...] = b2[...] + b2[...]

    @pl.loop(0, steps)
    def _(i):
        w_copy(i).wait()
        x_copy(i).wait()
        part = pl.ds(pl.multiple_of(i * step, step), step)
        xa_part = xa[:, part]
        a_part = xa_part[toks:]
        for c in range(cols // tile):
            at = slice(c * tile, (c + 1) * tile)
            m = (m_ref[part, at].astype(F32) + tn(a_part, b2[:, at])).astype(BF16)
            m_ref[part, at] = m
            wide = m.astype(F32)
            sq[:, at] += jnp.sum((wide * wide).reshape(step // 8, 8, tile), axis=0)
            acc[:, at] += nn(xa_part, m)
        qt[...] += nt(a_part, xa_part[:toks])

    dy_copy.wait()
    am_ref[...] = acc[toks:]
    stat_ref[0:1] = jnp.sum(sq[...], axis=0, keepdims=True)
    stat_ref[1:2] = jnp.sum(acc[:toks] * dy[...].astype(F32), axis=0, keepdims=True)
    bq_ref[...] = fold(nn(hi_lo(qt[...]), dy[...]))


def merge(w, x, a_t, b, dy):
    rows, cols = w.shape
    toks = x.shape[0]
    rank = b.shape[0]
    steps = rows // 512
    dma = pltpu.SemaphoreType.DMA
    return call(
        functools.partial(merge_kernel, steps),
        [pltpu.VMEM((rows, cols), BF16), out((2, cols)), out((rank, cols)), out((rank, cols))],
        [ANY] * 5,
        w, x, a_t, b, dy,
        scratch=[
            pltpu.VMEM((toks + rank, rows), BF16),
            pltpu.VMEM((rank, cols), BF16),
            pltpu.VMEM((toks, cols), BF16),
            pltpu.VMEM((toks + rank, cols), F32),
            pltpu.VMEM((rank, toks), F32),
            pltpu.VMEM((8, cols), F32),
            dma((steps,)), dma((steps,)), dma, dma, dma,
        ],
        vmem=24,
        flops=2 * rows * cols * (toks + 2 * rank),
        data=rows * cols * 2,
    )


def block(m_ref, index, half=None, count=4):
    size = m_ref.shape[0] // count
    start = lax.rem(index + count, count) * size
    if half is not None:
        size //= 2
        start += half * size
    return m_ref[pl.ds(pl.multiple_of(start, 64), size)]


def far_kernel(stat_ref, r1_ref, r2_ref, r3_ref, mag_ref, dy_ref, m_ref, vec_ref, scaled_ref, h0_ref, h1_ref):
    total = (stat_ref[...] + r2_ref[...]) + (r1_ref[...] + r3_ref[...])
    squares = total[0:1] + EPS
    norms = jnp.sqrt(squares)
    scale = mag_ref[...] / norms
    vec_ref[...] = jnp.concatenate([squares, norms, scale, total[1:2]], axis=0)
    scaled = (dy_ref[...].astype(F32) * scale).astype(BF16)
    scaled_ref[...] = scaled
    y = lax.axis_index("cols")
    h0_ref[...] = nt(block(m_ref, y + 2, 0), scaled)
    h1_ref[...] = nt(block(m_ref, y + 2, 1), scaled)


def near_kernel(m_ref, scaled_ref, up_ref, down_ref):
    y = lax.axis_index("cols")
    up_ref[...] = nt(block(m_ref, y + 1, 1), scaled_ref[...])
    down_ref[...] = nt(block(m_ref, y - 1, 0), scaled_ref[...])


def relay_kernel(m_ref, scaled_ref, u0_ref, u1_ref, up_ref, down_ref):
    y = lax.axis_index("cols")
    up_ref[...] = u0_ref[...] + nt(block(m_ref, y + 1, 0), scaled_ref[...])
    down_ref[...] = u1_ref[...] + nt(block(m_ref, y - 1, 1), scaled_ref[...])


def own_kernel(m_ref, scaled_ref, own_ref):
    own_ref[...] = nt(block(m_ref, lax.axis_index("cols")), scaled_ref[...])


def finish_kernel(own_ref, v0_ref, v1_ref, w0_ref, w1_ref, out_ref):
    half = own_ref.shape[0] // 2
    out_ref[:half] = (own_ref[:half] + (w0_ref[...] + v1_ref[...])).astype(BF16)
    out_ref[half:] = (own_ref[half:] + (w1_ref[...] + v0_ref[...])).astype(BF16)


def a_kernel(factor, vec_ref, dy_ref, b_ref, x_ref, m_ref, *refs):
    outs, whole = refs[:-1], refs[-1]
    scale = vec_ref[2:3] * factor
    wide = b_ref[...].astype(F32) * scale
    p_t = fold(nt(hi_lo(wide), dy_ref[...]))
    left = hi_lo(p_t)
    right = hi_lo(wide * (vec_ref[3:4] / vec_ref[0:1]))
    rows = m_ref.shape[0]
    tile = 512
    for r in range(rows // tile):
        at = slice(r * tile, (r + 1) * tile)
        whole[:, at] = fold(nn(left, x_ref[:, at]) - nt(right, m_ref[at]))
    split(whole, outs, lax.axis_index("dp"), 1)


def split(whole, outs, index, axis):
    count = len(outs)
    size = whole.shape[axis] // count
    for k, ref in enumerate(outs):
        at = pl.ds(pl.multiple_of(lax.rem(index + k, count) * size, 128 if axis else 8), size)
        ref[...] = whole[:, at] if axis else whole[at]


def sum_split_kernel(position, axis, parts, *refs):
    ins, outs, whole = refs[:parts], refs[parts:-1], refs[-1]
    whole[...] = functools.reduce(jnp.add, [ref[...] for ref in ins])
    split(whole, outs, position(), axis)


def sum_split(ins, position, axis, count):
    shape = ins[0].shape
    piece = list(shape)
    piece[axis] //= count
    return call(
        functools.partial(sum_split_kernel, position, axis, len(ins)),
        [out(tuple(piece))] * count,
        [VMEM] * len(ins),
        *ins,
        scratch=[pltpu.VMEM(shape, F32)],
        data=4 * 5 * shape[0] * shape[1],
    )


def join_kernel(position, axis, *refs):
    ins, whole = refs[:-1], refs[-1]
    count = len(ins)
    size = ins[0].shape[axis]
    for k, ref in enumerate(ins):
        start = lax.rem(position() + count - k, count) * size
        at = pl.ds(pl.multiple_of(start, 128 if axis else 8), size)
        if axis:
            whole[:, at] = ref[...]
        else:
            whole[at] = ref[...]


def join(ins, position, axis):
    shape = list(ins[0].shape)
    shape[axis] *= len(ins)
    return call(
        functools.partial(join_kernel, position, axis),
        [out(tuple(shape))],
        [VMEM] * len(ins),
        *ins,
        data=4 * 2 * shape[0] * shape[1],
    )[0]


def b_kernel(factor, vec_ref, bq_ref, am_ref, keep_ref, send_ref, whole):
    ratio = vec_ref[3:4] / vec_ref[0:1]
    whole[...] = (vec_ref[2:3] * factor) * (bq_ref[...] - ratio * am_ref[...])
    split(whole, [keep_ref, send_ref], core_index(), 0)


def b_dp_kernel(vec_ref, *refs):
    ins, outs, whole = refs[:4], refs[4:-1], refs[-1]
    rows = ins[0].shape[0]
    whole[:rows] = functools.reduce(jnp.add, [ref[...] for ref in ins])
    whole[rows:] = jnp.broadcast_to(vec_ref[3:4], (whole.shape[0] - rows, whole.shape[1]))
    split(whole, outs, lax.axis_index("dp"), 1)


def b_join_kernel(factor, vec_ref, i0_ref, i1_ref, i2_ref, i3_ref, b_out_ref, mag_ref, whole):
    join_kernel(dp_index, 1, i0_ref, i1_ref, i2_ref, i3_ref, whole)
    rows = b_out_ref.shape[0]
    b_out_ref[...] = whole[:rows]
    mag_ref[...] = factor * whole[rows:rows + 1] / vec_ref[1:2]


def core_index():
    return lax.rem(lax.axis_index("rows"), 2)


def x_index():
    return lax.div(lax.axis_index("rows"), 2)


def dp_index():
    return lax.axis_index("dp")


def cols_index():
    return lax.axis_index("cols")


def ring(value, axis, k, count=4):
    return lax.ppermute(value, axis, [(i, (i + k) % count) for i in range(count)])


def ring_x(value, k, count=8):
    return lax.ppermute(value, "rows", [(i, (i + 2 * k) % count) for i in range(count)])


def swap_core(value, count=8):
    return lax.ppermute(value, "rows", [(i, i ^ 1) for i in range(count)])


def shards(x, dy, w, a, b, mag):
    rows, cols = w.shape
    toks, rank = x.shape[0], a.shape[1]
    groups, full_rows = 4, rows * 8
    gamma = float(toks * groups) ** (-0.5)
    mag = mag.reshape(1, cols)
    m, stat, bq, am = merge(w, x, a.T, b, dy)

    m = pltpu.with_memory_space_constraint(m, pltpu.VMEM)
    stat = stat + swap_core(stat)
    far = rows // 8
    vec, scaled, h0, h1 = call(
        far_kernel,
        [out((4, cols)), out((toks, cols), BF16), out((far, toks)), out((far, toks))],
        [VMEM] * 7,
        stat, ring_x(stat, 1), ring_x(stat, 2), ring_x(stat, 3), mag, dy, m,
        flops=2 * 2 * far * toks * cols,
    )
    u0, u1 = ring(h0, "cols", 1), ring(h1, "cols", 3)
    up, down = call(near_kernel, [out((far, toks))] * 2, [VMEM] * 2, m, scaled, flops=2 * 2 * far * toks * cols)
    v0, v1 = ring(up, "cols", 1), ring(down, "cols", 3)

    pieces = call(
        functools.partial(a_kernel, 2.0 * gamma),
        [out((rank, rows // 4))] * 4,
        [VMEM] * 5,
        vec, dy, b, x, m,
        scratch=[pltpu.VMEM((rank, rows), F32)],
        flops=2 * 2 * rank * rows * (cols + toks),
    )
    pieces = [pieces[0]] + [ring(pieces[k], "dp", k) for k in (1, 2, 3)]

    keep, send = call(
        functools.partial(b_kernel, 2.0 * gamma),
        [out((rank // 2, cols))] * 2,
        [VMEM] * 3,
        vec, bq, am,
        scratch=[pltpu.VMEM((rank, cols), F32)],
    )
    send = swap_core(send)

    up, down = call(
        relay_kernel, [out((far, toks))] * 2, [VMEM] * 4, m, scaled, u0, u1, flops=2 * 2 * far * toks * cols
    )
    w0, w1 = ring(up, "cols", 1), ring(down, "cols", 3)
    own = call(own_kernel, [out((rows // 4, toks))], [VMEM] * 2, m, scaled, flops=2 * 2 * far * toks * cols)[0]

    pieces = sum_split(pieces, cols_index, 0, 4)
    pieces = [pieces[0]] + [ring(pieces[k], "cols", k) for k in (1, 2, 3)]
    piece = (pieces[0] + pieces[2]) + (pieces[1] + pieces[3])
    piece = join([piece] + [ring(piece, "cols", k) for k in (1, 2, 3)], cols_index, 0)
    a_grad = join([piece] + [ring(piece, "dp", k) for k in (1, 2, 3)], dp_index, 1)

    pieces = sum_split([keep, send], x_index, 0, 4)
    pieces = [pieces[0]] + [ring_x(pieces[k], k) for k in (1, 2, 3)]
    pieces = call(
        b_dp_kernel,
        [out((rank // 4, cols // 4))] * 4,
        [VMEM] * 5,
        vec, *pieces,
        scratch=[pltpu.VMEM((rank // 4, cols), F32)],
    )
    pieces = [pieces[0]] + [ring(pieces[k], "dp", k) for k in (1, 2, 3)]
    piece = (pieces[0] + pieces[2]) + (pieces[1] + pieces[3])
    b_part, mag_grad = call(
        functools.partial(b_join_kernel, gamma / float(full_rows) ** 0.5),
        [out((rank // 8, cols)), out((1, cols))],
        [VMEM] * 5,
        vec, piece, ring(piece, "dp", 1), ring(piece, "dp", 2), ring(piece, "dp", 3),
        scratch=[pltpu.VMEM((rank // 4, cols), F32)],
    )
    b_part = join([b_part] + [ring_x(b_part, k) for k in (1, 2, 3)], x_index, 0)
    b_grad = join([b_part, swap_core(b_part)], core_index, 0)

    grad = call(finish_kernel, [out((rows // 4, toks), BF16)], [VMEM] * 5, own, v0, v1, w0, w1)[0]
    return grad, a_grad.T, b_grad, mag_grad.reshape(cols)


def solution(mesh):
    return jax.shard_map(
        shards,
        mesh=mesh,
        in_specs=(
            P("dp", "rows"),
            P("dp", "cols"),
            P("rows", "cols"),
            P("rows", None),
            P(None, "cols"),
            P("cols"),
        ),
        out_specs=(P(("rows", "cols"), "dp"), P("rows", None), P(None, "cols"), P("cols")),
        check_vma=False,
    )
```

```python
import functools

import jax
import jax.numpy as jnp
from jax import lax
from jax.experimental import pallas as pl
from jax.experimental.pallas import tpu as pltpu
from jax.sharding import PartitionSpec as P

EPS = 1e-06
F32 = jnp.float32
BF16 = jnp.bfloat16
MIB = 1024 * 1024

ANY = pl.BlockSpec(memory_space=pl.ANY)
VMEM = pl.BlockSpec(memory_space=pltpu.VMEM)
HBM = pl.BlockSpec(memory_space=pltpu.HBM)


def nn(a, b):
    return lax.dot_general(a, b, (((1,), (0,)), ((), ())), preferred_element_type=F32)


def nt(a, b):
    return lax.dot_general(a, b, (((1,), (1,)), ((), ())), preferred_element_type=F32)


def tn(a, b):
    return lax.dot_general(a, b, (((0,), (0,)), ((), ())), preferred_element_type=F32)


def hi_lo(value):
    hi = value.astype(BF16)
    lo = (value - hi.astype(F32)).astype(BF16)
    return jnp.concatenate([hi, lo], axis=0)


def fold(value):
    half = value.shape[0] // 2
    return value[:half] + value[half:]


def call(kernel, outs, specs, *args, scratch=(), vmem=16, flops=1, data=1, after=()):
    used = len(args)

    def body(*refs):
        kernel(*refs[:used], *refs[used + len(after):])

    return pl.pallas_call(
        body,
        out_shape=outs,
        in_specs=list(specs) + [ANY] * len(after),
        out_specs=[VMEM for _ in outs],
        scratch_shapes=list(scratch),
        compiler_params=pltpu.CompilerParams(vmem_limit_bytes=vmem * MIB),
        cost_estimate=pl.CostEstimate(flops=flops, bytes_accessed=data, transcendentals=0),
    )(*args, *after)


def out(shape, dtype=F32):
    return jax.ShapeDtypeStruct(shape, dtype)


def merge_kernel(
    steps, w_ref, x_ref, a_ref, b_ref, dy_ref, m_ref, stat_ref, bq_ref, am_ref,
    xa, b2, dy, acc, qt, sq, w_sem, x_sem, a_sem, b_sem, dy_sem,
):
    rows, cols = w_ref.shape
    toks = x_ref.shape[0]
    step = rows // steps
    tile = 2048
    b_copy = pltpu.make_async_copy(b_ref, b2, b_sem)
    dy_copy = pltpu.make_async_copy(dy_ref, dy, dy_sem)
    a_copy = pltpu.make_async_copy(a_ref, xa.at[toks:], a_sem)

    def w_copy(i):
        part = pl.ds(pl.multiple_of(i * step, step), step)
        return pltpu.make_async_copy(w_ref.at[part], m_ref.at[part], w_sem.at[i])

    x_copy = pltpu.make_async_copy(x_ref, xa.at[:toks], x_sem)
    b_copy.start()
    a_copy.start()
    w_copy(0).start()
    x_copy.start()
    for i in range(1, steps):
        w_copy(i).start()
    dy_copy.start()
    acc[...] = jnp.zeros_like(acc)
    qt[...] = jnp.zeros_like(qt)
    sq[...] = jnp.zeros_like(sq)
    b_copy.wait()
    a_copy.wait()
    x_copy.wait()
    b2[...] = b2[...] + b2[...]

    @pl.loop(0, steps)
    def _(i):
        w_copy(i).wait()
        part = pl.ds(pl.multiple_of(i * step, step), step)
        xa_part = xa[:, part]
        a_part = xa_part[toks:]
        for c in range(cols // tile):
            at = slice(c * tile, (c + 1) * tile)
            m = (m_ref[part, at].astype(F32) + tn(a_part, b2[:, at])).astype(BF16)
            m_ref[part, at] = m
            wide = m.astype(F32)
            sq[:, at] += jnp.sum((wide * wide).reshape(step // 8, 8, tile), axis=0)
            acc[:, at] += nn(xa_part, m)
        qt[...] += nt(a_part, xa_part[:toks])

    dy_copy.wait()
    am_ref[...] = acc[toks:]
    stat_ref[0:1] = jnp.sum(sq[...], axis=0, keepdims=True)
    stat_ref[1:2] = jnp.sum(acc[:toks] * dy[...].astype(F32), axis=0, keepdims=True)
    bq_ref[...] = fold(nn(hi_lo(qt[...]), dy[...]))


def merge(w, x, a_t, b, dy):
    rows, cols = w.shape
    toks = x.shape[0]
    rank = b.shape[0]
    steps = rows // 512
    dma = pltpu.SemaphoreType.DMA
    return call(
        functools.partial(merge_kernel, steps),
        [pltpu.VMEM((rows, cols), BF16), out((2, cols)), out((rank, cols)), out((rank, cols))],
        [HBM] * 5,
        *[pltpu.with_memory_space_constraint(value, pltpu.HBM) for value in (w, x, a_t, b, dy)],
        scratch=[
            pltpu.VMEM((toks + rank, rows), BF16),
            pltpu.VMEM((rank, cols), BF16),
            pltpu.VMEM((toks, cols), BF16),
            pltpu.VMEM((toks + rank, cols), F32),
            pltpu.VMEM((rank, toks), F32),
            pltpu.VMEM((8, cols), F32),
            dma((steps,)), dma, dma, dma, dma,
        ],
        vmem=32,
        flops=2 * rows * cols * (toks + 2 * rank),
        data=rows * cols * 2,
    )


def block(m_ref, index, half=None, count=4):
    size = m_ref.shape[0] // count
    start = lax.rem(index + count, count) * size
    if half is not None:
        size //= 2
        start += half * size
    return m_ref[pl.ds(pl.multiple_of(start, 64), size)]


def far_kernel(stat_ref, r1_ref, r2_ref, r3_ref, mag_ref, dy_ref, m_ref, vec_ref, scaled_ref, h0_ref, h1_ref):
    total = (stat_ref[...] + r2_ref[...]) + (r1_ref[...] + r3_ref[...])
    squares = total[0:1] + EPS
    norms = jnp.sqrt(squares)
    scale = mag_ref[...] / norms
    vec_ref[...] = jnp.concatenate([squares, norms, scale, total[1:2]], axis=0)
    scaled = (dy_ref[...].astype(F32) * scale).astype(BF16)
    scaled_ref[...] = scaled
    y = lax.axis_index("cols")
    h0_ref[...] = nt(block(m_ref, y + 2, 0), scaled)
    h1_ref[...] = nt(block(m_ref, y + 2, 1), scaled)


def near_kernel(m_ref, scaled_ref, up_ref, down_ref):
    y = lax.axis_index("cols")
    up_ref[...] = nt(block(m_ref, y + 1, 1), scaled_ref[...])
    down_ref[...] = nt(block(m_ref, y - 1, 0), scaled_ref[...])


def relay_kernel(m_ref, scaled_ref, u0_ref, u1_ref, up_ref, down_ref):
    y = lax.axis_index("cols")
    up_ref[...] = u0_ref[...] + nt(block(m_ref, y + 1, 0), scaled_ref[...])
    down_ref[...] = u1_ref[...] + nt(block(m_ref, y - 1, 1), scaled_ref[...])


def own_kernel(m_ref, scaled_ref, own_ref):
    own_ref[...] = nt(block(m_ref, lax.axis_index("cols")), scaled_ref[...])


def direct_kernel(own_ref, v0_ref, v1_ref, sum_ref):
    half = own_ref.shape[0] // 2
    sum_ref[:half] = own_ref[:half] + v1_ref[...]
    sum_ref[half:] = own_ref[half:] + v0_ref[...]


def finish_kernel(own_ref, w0_ref, w1_ref, out_ref):
    half = own_ref.shape[0] // 2
    out_ref[:half] = (own_ref[:half] + w0_ref[...]).astype(BF16)
    out_ref[half:] = (own_ref[half:] + w1_ref[...]).astype(BF16)


def a_kernel(factor, vec_ref, dy_ref, b_ref, x_ref, m_ref, *refs):
    outs, whole = refs[:-1], refs[-1]
    scale = vec_ref[2:3] * factor
    wide = b_ref[...].astype(F32) * scale
    p_t = fold(nt(hi_lo(wide), dy_ref[...]))
    left = hi_lo(p_t)
    right = hi_lo(wide * (vec_ref[3:4] / vec_ref[0:1]))
    rows = m_ref.shape[0]
    tile = 512
    for r in range(rows // tile):
        at = slice(r * tile, (r + 1) * tile)
        whole[:, at] = fold(nn(left, x_ref[:, at]) - nt(right, m_ref[at]))
    split(whole, outs, lax.axis_index("dp"), 1)


def split(whole, outs, index, axis):
    count = len(outs)
    size = whole.shape[axis] // count
    for k, ref in enumerate(outs):
        at = pl.ds(pl.multiple_of(lax.rem(index + k, count) * size, 128 if axis else 8), size)
        ref[...] = whole[:, at] if axis else whole[at]


def sum_kernel(*refs):
    refs[-1][...] = functools.reduce(jnp.add, [ref[...] for ref in refs[:-1]])


def add(*ins, after=()):
    return call(sum_kernel, [out(ins[0].shape)], [VMEM] * len(ins), *ins, after=after)[0]


def halve_kernel(position, left_ref, right_ref, keep_ref, send_ref, whole):
    whole[...] = left_ref[...] + right_ref[...]
    split(whole, [keep_ref, send_ref], position(), 0)


def halve(left, right, position, after=()):
    rows, cols = left.shape
    return call(
        functools.partial(halve_kernel, position),
        [out((rows // 2, cols))] * 2,
        [VMEM] * 2,
        left, right,
        scratch=[pltpu.VMEM((rows, cols), F32)],
        after=after,
    )


def join_kernel(position, axis, *refs):
    ins, whole = refs[:-1], refs[-1]
    count = len(ins)
    size = ins[0].shape[axis]
    for k, ref in enumerate(ins):
        start = lax.rem(position() + count - k, count) * size
        at = pl.ds(pl.multiple_of(start, 128 if axis else 8), size)
        if axis:
            whole[:, at] = ref[...]
        else:
            whole[at] = ref[...]


def join(ins, position, axis, after=()):
    shape = list(ins[0].shape)
    shape[axis] *= len(ins)
    return call(
        functools.partial(join_kernel, position, axis),
        [out(tuple(shape))],
        [VMEM] * len(ins),
        *ins,
        after=after,
    )[0]


def b_kernel(factor, vec_ref, bq_ref, am_ref, keep_ref, send_ref, whole):
    ratio = vec_ref[3:4] / vec_ref[0:1]
    whole[...] = (vec_ref[2:3] * factor) * (bq_ref[...] - ratio * am_ref[...])
    split(whole, [keep_ref, send_ref], core_bit(), 0)


def b_stack_kernel(left_ref, right_ref, vec_ref, out_ref):
    rows = left_ref.shape[0]
    out_ref[:rows] = left_ref[...] + right_ref[...]
    out_ref[rows:] = jnp.broadcast_to(vec_ref[3:4], left_ref.shape)


def b_unstack_kernel(factor, left_ref, right_ref, vec_ref, b_ref, mag_ref):
    rows = b_ref.shape[0]
    total = left_ref[...] + right_ref[...]
    b_ref[...] = total[:rows]
    mag_ref[...] = factor * total[rows:rows + 1] / vec_ref[1:2]


def core_bit():
    return lax.rem(lax.axis_index("rows"), 2)


def near_bit():
    return lax.rem(lax.div(lax.div(lax.axis_index("rows"), 2) + 1, 2), 2)


def far_bit():
    return lax.div(lax.axis_index("rows"), 4)


def dp_index():
    return lax.axis_index("dp")


def ring(value, axis, k, count=4):
    return lax.ppermute(value, axis, [(i, (i + k) % count) for i in range(count)])


def ring_x(value, k, count=8):
    return lax.ppermute(value, "rows", [(i, (i + 2 * k) % count) for i in range(count)])


def swap(value, axis, step):
    return lax.ppermute(value, axis, [(i, i ^ 1 if step == 0 else 3 - i) for i in range(4)])


def swap_x(value, step):
    return lax.ppermute(value, "rows", [(i, i ^ 2 if step == 0 else 6 - 2 * (i // 2) + i % 2) for i in range(8)])


def swap_core(value, count=8):
    return lax.ppermute(value, "rows", [(i, i ^ 1) for i in range(count)])


def shards(x, dy, w, a, b, mag):
    rows, cols = w.shape
    toks, rank = x.shape[0], a.shape[1]
    groups, full_rows = 4, rows * 8
    gamma = float(toks * groups) ** (-0.5)
    mag = mag.reshape(1, cols)
    m, stat, bq, am = merge(w, x, a.T, b, dy)

    m = pltpu.with_memory_space_constraint(m, pltpu.VMEM)
    stat = stat + swap_core(stat)
    far = rows // 8
    vec, scaled, h0, h1 = call(
        far_kernel,
        [out((4, cols)), out((toks, cols), BF16), out((far, toks)), out((far, toks))],
        [VMEM] * 7,
        stat, ring_x(stat, 1), ring_x(stat, 2), ring_x(stat, 3), mag, dy, m,
    )
    u0, u1 = ring(h0, "cols", 1), ring(h1, "cols", 3)
    up, down = call(near_kernel, [out((far, toks))] * 2, [VMEM] * 2, m, scaled)
    v0, v1 = ring(up, "cols", 1), ring(down, "cols", 3)

    pieces = call(
        functools.partial(a_kernel, 2.0 * gamma),
        [out((rank, rows // 4))] * 4,
        [VMEM] * 5,
        vec, dy, b, x, m,
        scratch=[pltpu.VMEM((rank, rows), F32)],
        after=[up],
    )
    pieces = [pieces[0]] + [ring(pieces[k], "dp", k) for k in (1, 2, 3)]

    keep, send = call(
        functools.partial(b_kernel, 2.0 * gamma),
        [out((rank // 2, cols))] * 2,
        [VMEM] * 3,
        vec, bq, am,
        scratch=[pltpu.VMEM((rank, cols), F32)],
        after=[pieces[0]],
    )
    keep, send = halve(keep, swap_core(send), near_bit)
    own = call(own_kernel, [out((rows // 4, toks))], [VMEM] * 2, m, scaled, after=[send])[0]
    up, down = call(relay_kernel, [out((far, toks))] * 2, [VMEM] * 4, m, scaled, u0, u1, after=[own])
    w0, w1 = ring(up, "cols", 1), ring(down, "cols", 3)

    keep, send = halve(keep, swap_x(send, 0), far_bit, after=[up])
    stack = call(
        b_stack_kernel, [out((rank // 4, cols))], [VMEM] * 3, keep, swap_x(send, 1), vec, after=[keep]
    )[0]
    own = call(direct_kernel, [out((rows // 4, toks))], [VMEM] * 3, own, v0, v1, after=[stack])[0]

    piece = add(*pieces, after=[own])
    stack = add(stack, swap(stack, "dp", 0), after=[piece])
    piece = add(piece, swap(piece, "cols", 0), after=[stack])
    b_part, mag_grad = call(
        functools.partial(b_unstack_kernel, gamma / float(full_rows) ** 0.5),
        [out((rank // 8, cols)), out((1, cols))],
        [VMEM] * 3,
        stack, swap(stack, "dp", 1), vec,
        after=[piece],
    )
    piece = add(piece, swap(piece, "cols", 1), after=[b_part])
    grad = call(
        finish_kernel, [out((rows // 4, toks), BF16)], [VMEM] * 3, own, w0, w1, after=[piece]
    )[0]
    b_part = join([b_part, swap_x(b_part, 1)], far_bit, 0)
    b_part = join([b_part, swap_x(b_part, 0)], near_bit, 0)
    b_grad = join([b_part, swap_core(b_part)], core_bit, 0, after=[grad])
    a_grad = join([piece] + [ring(piece, "dp", k) for k in (1, 2, 3)], dp_index, 1, after=[b_grad])
    return grad, a_grad.T, b_grad, mag_grad.reshape(cols)


def solution(mesh):
    return jax.shard_map(
        shards,
        mesh=mesh,
        in_specs=(
            P("dp", "rows"),
            P("dp", "cols"),
            P("rows", "cols"),
            P("rows", None),
            P(None, "cols"),
            P("cols"),
        ),
        out_specs=(P(("rows", "cols"), "dp"), P("rows", None), P(None, "cols"), P("cols")),
        check_vma=False,
    )
```

```python
import functools

import jax
import jax.numpy as jnp
from jax import lax
from jax.experimental import pallas as pl
from jax.experimental.pallas import tpu as pltpu
from jax.sharding import PartitionSpec as P

EPS = 1e-06
F32 = jnp.float32
BF16 = jnp.bfloat16
MIB = 1024 * 1024

ANY = pl.BlockSpec(memory_space=pl.ANY)
VMEM = pl.BlockSpec(memory_space=pltpu.VMEM)
HBM = pl.BlockSpec(memory_space=pltpu.HBM)


def nn(a, b):
    return lax.dot_general(a, b, (((1,), (0,)), ((), ())), preferred_element_type=F32)


def nt(a, b):
    return lax.dot_general(a, b, (((1,), (1,)), ((), ())), preferred_element_type=F32)


def tn(a, b):
    return lax.dot_general(a, b, (((0,), (0,)), ((), ())), preferred_element_type=F32)


def hi_lo(value):
    hi = value.astype(BF16)
    lo = (value - hi.astype(F32)).astype(BF16)
    return jnp.concatenate([hi, lo], axis=0)


def fold(value):
    half = value.shape[0] // 2
    return value[:half] + value[half:]


def call(kernel, outs, specs, *args, scratch=(), vmem=16, flops=1, data=1, after=()):
    used = len(args)

    def body(*refs):
        kernel(*refs[:used], *refs[used + len(after):])

    return pl.pallas_call(
        body,
        out_shape=outs,
        in_specs=list(specs) + [ANY] * len(after),
        out_specs=[VMEM for _ in outs],
        scratch_shapes=list(scratch),
        compiler_params=pltpu.CompilerParams(vmem_limit_bytes=vmem * MIB),
        cost_estimate=pl.CostEstimate(flops=flops, bytes_accessed=data, transcendentals=0),
    )(*args, *after)


def out(shape, dtype=F32):
    return jax.ShapeDtypeStruct(shape, dtype)


def merge_kernel(
    steps, w_ref, x_ref, a_ref, b_ref, dy_ref, m_ref, stat_ref, bq_ref, am_ref,
    xa, b2, dy, acc, qt, sq, w_sem, x_sem, a_sem, b_sem, dy_sem,
):
    rows, cols = w_ref.shape
    toks = x_ref.shape[0]
    step = rows // steps
    tile = 2048
    b_copy = pltpu.make_async_copy(b_ref, b2, b_sem)
    dy_copy = pltpu.make_async_copy(dy_ref, dy, dy_sem)
    a_copy = pltpu.make_async_copy(a_ref, xa.at[toks:], a_sem)

    def w_copy(i):
        part = pl.ds(pl.multiple_of(i * step, step), step)
        return pltpu.make_async_copy(w_ref.at[part], m_ref.at[part], w_sem.at[i])

    x_copy = pltpu.make_async_copy(x_ref, xa.at[:toks], x_sem)
    b_copy.start()
    a_copy.start()
    w_copy(0).start()
    x_copy.start()
    for i in range(1, steps):
        w_copy(i).start()
    dy_copy.start()
    acc[...] = jnp.zeros_like(acc)
    qt[...] = jnp.zeros_like(qt)
    sq[...] = jnp.zeros_like(sq)
    b_copy.wait()
    a_copy.wait()
    x_copy.wait()
    b2[...] = b2[...] + b2[...]

    @pl.loop(0, steps)
    def _(i):
        w_copy(i).wait()
        part = pl.ds(pl.multiple_of(i * step, step), step)
        xa_part = xa[:, part]
        a_part = xa_part[toks:]
        for c in range(cols // tile):
            at = slice(c * tile, (c + 1) * tile)
            m = (m_ref[part, at].astype(F32) + tn(a_part, b2[:, at])).astype(BF16)
            m_ref[part, at] = m
            wide = m.astype(F32)
            sq[:, at] += jnp.sum((wide * wide).reshape(step // 8, 8, tile), axis=0)
            acc[:, at] += nn(xa_part, m)
        qt[...] += nt(a_part, xa_part[:toks])

    dy_copy.wait()
    am_ref[...] = acc[toks:]
    stat_ref[0:1] = jnp.sum(sq[...], axis=0, keepdims=True)
    stat_ref[1:2] = jnp.sum(acc[:toks] * dy[...].astype(F32), axis=0, keepdims=True)
    bq_ref[...] = fold(nn(hi_lo(qt[...]), dy[...]))


def merge(w, x, a_t, b, dy):
    rows, cols = w.shape
    toks = x.shape[0]
    rank = b.shape[0]
    steps = rows // 512
    dma = pltpu.SemaphoreType.DMA
    return call(
        functools.partial(merge_kernel, steps),
        [pltpu.VMEM((rows, cols), BF16), out((2, cols)), out((rank, cols)), out((rank, cols))],
        [HBM] * 5,
        *[pltpu.with_memory_space_constraint(value, pltpu.HBM) for value in (w, x, a_t, b, dy)],
        scratch=[
            pltpu.VMEM((toks + rank, rows), BF16),
            pltpu.VMEM((rank, cols), BF16),
            pltpu.VMEM((toks, cols), BF16),
            pltpu.VMEM((toks + rank, cols), F32),
            pltpu.VMEM((rank, toks), F32),
            pltpu.VMEM((8, cols), F32),
            dma((steps,)), dma, dma, dma, dma,
        ],
        vmem=32,
        flops=2 * rows * cols * (toks + 2 * rank),
        data=rows * cols * 2,
    )


def block(m_ref, index, half=None, count=4):
    size = m_ref.shape[0] // count
    start = lax.rem(index + count, count) * size
    if half is not None:
        size //= 2
        start += half * size
    return m_ref[pl.ds(pl.multiple_of(start, 64), size)]


def far_kernel(stat_ref, r1_ref, r2_ref, r3_ref, mag_ref, dy_ref, m_ref, vec_ref, scaled_ref, h0_ref, h1_ref):
    total = (stat_ref[...] + r2_ref[...]) + (r1_ref[...] + r3_ref[...])
    squares = total[0:1] + EPS
    norms = jnp.sqrt(squares)
    scale = mag_ref[...] / norms
    vec_ref[...] = jnp.concatenate([squares, norms, scale, total[1:2]], axis=0)
    scaled = (dy_ref[...].astype(F32) * scale).astype(BF16)
    scaled_ref[...] = scaled
    y = lax.axis_index("cols")
    h0_ref[...] = nt(block(m_ref, y + 2, 0), scaled)
    h1_ref[...] = nt(block(m_ref, y + 2, 1), scaled)


def near_kernel(m_ref, scaled_ref, up_ref, down_ref):
    y = lax.axis_index("cols")
    up_ref[...] = nt(block(m_ref, y + 1), scaled_ref[...])
    down_ref[...] = nt(block(m_ref, y - 1), scaled_ref[...])


def relay_kernel(near_up_ref, near_down_ref, u0_ref, u1_ref, up_ref, down_ref):
    half = u0_ref.shape[0]
    up_ref[:half] = near_up_ref[:half] + u0_ref[...]
    up_ref[half:] = near_up_ref[half:]
    down_ref[:half] = near_down_ref[:half]
    down_ref[half:] = near_down_ref[half:] + u1_ref[...]


def own_kernel(m_ref, scaled_ref, own_ref):
    own_ref[...] = nt(block(m_ref, lax.axis_index("cols")), scaled_ref[...])


def finish_kernel(own_ref, up_ref, down_ref, out_ref, done_ref):
    out_ref[...] = (own_ref[...] + (up_ref[...] + down_ref[...])).astype(BF16)
    done_ref[...] = jnp.zeros_like(done_ref)


def a_kernel(factor, vec_ref, dy_ref, b_ref, x_ref, m_ref, *refs):
    outs, whole = refs[:-1], refs[-1]
    scale = vec_ref[2:3] * factor
    wide = b_ref[...].astype(F32) * scale
    p_t = fold(nt(hi_lo(wide), dy_ref[...]))
    left = hi_lo(p_t)
    right = hi_lo(wide * (vec_ref[3:4] / vec_ref[0:1]))
    rows = m_ref.shape[0]
    tile = 512
    for r in range(rows // tile):
        at = slice(r * tile, (r + 1) * tile)
        whole[:, at] = fold(nn(left, x_ref[:, at]) - nt(right, m_ref[at]))
    split(whole, outs, lax.axis_index("dp"), 1)


def split(whole, outs, index, axis):
    count = len(outs)
    size = whole.shape[axis] // count
    for k, ref in enumerate(outs):
        at = pl.ds(pl.multiple_of(lax.rem(index + k, count) * size, 128 if axis else 8), size)
        ref[...] = whole[:, at] if axis else whole[at]


def sum_kernel(*refs):
    refs[-1][...] = functools.reduce(jnp.add, [ref[...] for ref in refs[:-1]])


def add(*ins, after=()):
    return call(sum_kernel, [out(ins[0].shape)], [VMEM] * len(ins), *ins, after=after)[0]


def halve_kernel(position, left_ref, right_ref, keep_ref, send_ref, whole):
    whole[...] = left_ref[...] + right_ref[...]
    split(whole, [keep_ref, send_ref], position(), 0)


def halve(left, right, position, after=()):
    rows, cols = left.shape
    return call(
        functools.partial(halve_kernel, position),
        [out((rows // 2, cols))] * 2,
        [VMEM] * 2,
        left, right,
        scratch=[pltpu.VMEM((rows, cols), F32)],
        after=after,
    )


def join_kernel(position, axis, *refs):
    ins, whole = refs[:-1], refs[-1]
    count = len(ins)
    size = ins[0].shape[axis]
    for k, ref in enumerate(ins):
        start = lax.rem(position() + count - k, count) * size
        at = pl.ds(pl.multiple_of(start, 128 if axis else 8), size)
        if axis:
            whole[:, at] = ref[...]
        else:
            whole[at] = ref[...]


def join(ins, position, axis, after=()):
    shape = list(ins[0].shape)
    shape[axis] *= len(ins)
    return call(
        functools.partial(join_kernel, position, axis),
        [out(tuple(shape))],
        [VMEM] * len(ins),
        *ins,
        after=after,
    )[0]


def b_kernel(factor, vec_ref, bq_ref, am_ref, keep_ref, send_ref, whole):
    ratio = vec_ref[3:4] / vec_ref[0:1]
    whole[...] = (vec_ref[2:3] * factor) * (bq_ref[...] - ratio * am_ref[...])
    split(whole, [keep_ref, send_ref], core_bit(), 0)


def b_stack_kernel(left_ref, right_ref, vec_ref, out_ref):
    rows = left_ref.shape[0]
    out_ref[:rows] = left_ref[...] + right_ref[...]
    out_ref[rows:] = jnp.broadcast_to(vec_ref[3:4], left_ref.shape)


def b_unstack_kernel(factor, left_ref, right_ref, vec_ref, b_ref, mag_ref):
    rows = b_ref.shape[0]
    total = left_ref[...] + right_ref[...]
    b_ref[...] = total[:rows]
    mag_ref[...] = factor * total[rows:rows + 1] / vec_ref[1:2]


def core_bit():
    return lax.rem(lax.axis_index("rows"), 2)


def near_bit():
    return lax.rem(lax.div(lax.div(lax.axis_index("rows"), 2) + 1, 2), 2)


def far_bit():
    return lax.div(lax.axis_index("rows"), 4)


def dp_index():
    return lax.axis_index("dp")


def ring(value, axis, k, count=4):
    return lax.ppermute(value, axis, [(i, (i + k) % count) for i in range(count)])


def ring_x(value, k, count=8):
    return lax.ppermute(value, "rows", [(i, (i + 2 * k) % count) for i in range(count)])


def swap(value, axis, step):
    return lax.ppermute(value, axis, [(i, i ^ 1 if step == 0 else 3 - i) for i in range(4)])


def swap_x(value, step):
    return lax.ppermute(value, "rows", [(i, i ^ 2 if step == 0 else 6 - 2 * (i // 2) + i % 2) for i in range(8)])


def swap_core(value, count=8):
    return lax.ppermute(value, "rows", [(i, i ^ 1) for i in range(count)])


def shards(x, dy, w, a, b, mag):
    rows, cols = w.shape
    toks, rank = x.shape[0], a.shape[1]
    groups, full_rows = 4, rows * 8
    gamma = float(toks * groups) ** (-0.5)
    mag = mag.reshape(1, cols)
    m, stat, bq, am = merge(w, x, a.T, b, dy)

    m = pltpu.with_memory_space_constraint(m, pltpu.VMEM)
    stat = stat + swap_core(stat)
    far = rows // 8
    vec, scaled, h0, h1 = call(
        far_kernel,
        [out((4, cols)), out((toks, cols), BF16), out((far, toks)), out((far, toks))],
        [VMEM] * 7,
        stat, ring_x(stat, 1), ring_x(stat, 2), ring_x(stat, 3), mag, dy, m,
    )
    u0, u1 = ring(h0, "cols", 1), ring(h1, "cols", 3)
    keep, send = call(
        functools.partial(b_kernel, 2.0 * gamma),
        [out((rank // 2, cols))] * 2,
        [VMEM] * 3,
        vec, bq, am,
        scratch=[pltpu.VMEM((rank, cols), F32)],
    )
    pieces = call(
        functools.partial(a_kernel, 2.0 * gamma),
        [out((rank, rows // 4))] * 4,
        [VMEM] * 5,
        vec, dy, b, x, m,
        scratch=[pltpu.VMEM((rank, rows), F32)],
        after=[send],
    )
    keep, send = halve(keep, swap_core(send), near_bit, after=[pieces[0]])
    pieces = [pieces[0]] + [ring(pieces[k], "dp", k) for k in (2, 1, 3)]
    up, down = call(near_kernel, [out((rows // 4, toks))] * 2, [VMEM] * 2, m, scaled, after=[send])
    own = call(own_kernel, [out((rows // 4, toks))], [VMEM] * 2, m, scaled, after=[up])[0]

    piece = add(*pieces, after=[own])
    up, down = call(
        relay_kernel, [out((rows // 4, toks))] * 2, [VMEM] * 4, up, down, u0, u1, after=[piece]
    )
    w0, w1 = ring(up, "cols", 1), ring(down, "cols", 3)
    keep, send = halve(keep, swap_x(send, 0), far_bit, after=[up])
    stack = call(b_stack_kernel, [out((rank // 4, cols))], [VMEM] * 3, keep, swap_x(send, 1), vec)[0]
    piece = add(piece, swap(piece, "cols", 0), after=[stack])
    stack = add(stack, swap(stack, "dp", 0), after=[piece])
    b_part, mag_grad = call(
        functools.partial(b_unstack_kernel, gamma / float(full_rows) ** 0.5),
        [out((rank // 8, cols)), out((1, cols))],
        [VMEM] * 3,
        stack, swap(stack, "dp", 1), vec,
    )
    grad, done = call(
        finish_kernel,
        [out((rows // 4, toks), BF16), out((8, 128))],
        [VMEM] * 3,
        own, w0, w1,
        after=[b_part],
    )
    piece = add(piece, swap(piece, "cols", 1), after=[done])
    b_part = join([b_part, swap_x(b_part, 1)], far_bit, 0, after=[piece])
    b_part = join([b_part, swap_x(b_part, 0)], near_bit, 0)
    b_grad = join([b_part, swap_core(b_part)], core_bit, 0)
    a_grad = join([piece] + [ring(piece, "dp", k) for k in (1, 2, 3)], dp_index, 1, after=[b_part])
    return grad, a_grad.T, b_grad, mag_grad.reshape(cols)


def solution(mesh):
    return jax.shard_map(
        shards,
        mesh=mesh,
        in_specs=(
            P("dp", "rows"),
            P("dp", "cols"),
            P("rows", "cols"),
            P("rows", None),
            P(None, "cols"),
            P("cols"),
        ),
        out_specs=(P(("rows", "cols"), "dp"), P("rows", None), P(None, "cols"), P("cols")),
        check_vma=False,
    )
```

```python
import functools

import jax
import jax.numpy as jnp
from jax import lax
from jax.experimental import pallas as pl
from jax.experimental.pallas import tpu as pltpu
from jax.sharding import PartitionSpec as P

EPS = 1e-06
F32 = jnp.float32
BF16 = jnp.bfloat16
MIB = 1024 * 1024

ANY = pl.BlockSpec(memory_space=pl.ANY)
VMEM = pl.BlockSpec(memory_space=pltpu.VMEM)
HBM = pl.BlockSpec(memory_space=pltpu.HBM)


def nn(a, b):
    return lax.dot_general(a, b, (((1,), (0,)), ((), ())), preferred_element_type=F32)


def nt(a, b):
    return lax.dot_general(a, b, (((1,), (1,)), ((), ())), preferred_element_type=F32)


def tn(a, b):
    return lax.dot_general(a, b, (((0,), (0,)), ((), ())), preferred_element_type=F32)


def hi_lo(value):
    hi = value.astype(BF16)
    lo = (value - hi.astype(F32)).astype(BF16)
    return jnp.concatenate([hi, lo], axis=0)


def fold(value):
    half = value.shape[0] // 2
    return value[:half] + value[half:]


def call(kernel, outs, specs, *args, scratch=(), vmem=16, flops=1, data=1, after=()):
    used = len(args)

    def body(*refs):
        kernel(*refs[:used], *refs[used + len(after):])

    return pl.pallas_call(
        body,
        out_shape=outs,
        in_specs=list(specs) + [ANY] * len(after),
        out_specs=[VMEM for _ in outs],
        scratch_shapes=list(scratch),
        compiler_params=pltpu.CompilerParams(vmem_limit_bytes=vmem * MIB),
        cost_estimate=pl.CostEstimate(flops=flops, bytes_accessed=data, transcendentals=0),
    )(*args, *after)


def out(shape, dtype=F32):
    return jax.ShapeDtypeStruct(shape, dtype)


def merge_kernel(
    steps, w_ref, x_ref, a_ref, b_ref, dy_ref, m_ref, stat_ref, bq_ref, am_ref,
    xa, b2, dy, acc, qt, sq, w_sem, x_sem, a_sem, b_sem, dy_sem,
):
    rows, cols = w_ref.shape
    toks = x_ref.shape[0]
    step = rows // steps
    tile = 2048
    b_copy = pltpu.make_async_copy(b_ref, b2, b_sem)
    dy_copy = pltpu.make_async_copy(dy_ref, dy, dy_sem)
    a_copy = pltpu.make_async_copy(a_ref, xa.at[toks:], a_sem)

    def w_copy(i):
        part = pl.ds(pl.multiple_of(i * step, step), step)
        return pltpu.make_async_copy(w_ref.at[part], m_ref.at[part], w_sem.at[i])

    x_copy = pltpu.make_async_copy(x_ref, xa.at[:toks], x_sem)
    b_copy.start()
    a_copy.start()
    w_copy(0).start()
    x_copy.start()
    for i in range(1, steps):
        w_copy(i).start()
    dy_copy.start()
    acc[...] = jnp.zeros_like(acc)
    qt[...] = jnp.zeros_like(qt)
    sq[...] = jnp.zeros_like(sq)
    b_copy.wait()
    a_copy.wait()
    x_copy.wait()
    b2[...] = b2[...] + b2[...]

    @pl.loop(0, steps)
    def _(i):
        w_copy(i).wait()
        part = pl.ds(pl.multiple_of(i * step, step), step)
        xa_part = xa[:, part]
        a_part = xa_part[toks:]
        for c in range(cols // tile):
            at = slice(c * tile, (c + 1) * tile)
            m = (m_ref[part, at].astype(F32) + tn(a_part, b2[:, at])).astype(BF16)
            m_ref[part, at] = m
            wide = m.astype(F32)
            sq[:, at] += jnp.sum((wide * wide).reshape(step // 8, 8, tile), axis=0)
            acc[:, at] += nn(xa_part, m)
        qt[...] += nt(a_part, xa_part[:toks])

    dy_copy.wait()
    am_ref[...] = acc[toks:]
    stat_ref[0:1] = jnp.sum(sq[...], axis=0, keepdims=True)
    stat_ref[1:2] = jnp.sum(acc[:toks] * dy[...].astype(F32), axis=0, keepdims=True)
    bq_ref[...] = fold(nn(hi_lo(qt[...]), dy[...]))


def merge(w, x, a_t, b, dy):
    rows, cols = w.shape
    toks = x.shape[0]
    rank = b.shape[0]
    steps = rows // 512
    dma = pltpu.SemaphoreType.DMA
    return call(
        functools.partial(merge_kernel, steps),
        [pltpu.VMEM((rows, cols), BF16), out((2, cols)), out((rank, cols)), out((rank, cols))],
        [HBM] * 5,
        *[pltpu.with_memory_space_constraint(value, pltpu.HBM) for value in (w, x, a_t, b, dy)],
        scratch=[
            pltpu.VMEM((toks + rank, rows), BF16),
            pltpu.VMEM((rank, cols), BF16),
            pltpu.VMEM((toks, cols), BF16),
            pltpu.VMEM((toks + rank, cols), F32),
            pltpu.VMEM((rank, toks), F32),
            pltpu.VMEM((8, cols), F32),
            dma((steps,)), dma, dma, dma, dma,
        ],
        vmem=32,
        flops=2 * rows * cols * (toks + 2 * rank),
        data=rows * cols * 2,
    )


def block(m_ref, index, half=None, count=4):
    size = m_ref.shape[0] // count
    start = lax.rem(index + count, count) * size
    if half is not None:
        size //= 2
        start += half * size
    return m_ref[pl.ds(pl.multiple_of(start, 64), size)]


def far_kernel(stat_ref, r1_ref, r2_ref, r3_ref, mag_ref, dy_ref, m_ref, vec_ref, scaled_ref, h0_ref, h1_ref):
    total = (stat_ref[...] + r2_ref[...]) + (r1_ref[...] + r3_ref[...])
    squares = total[0:1] + EPS
    norms = jnp.sqrt(squares)
    scale = mag_ref[...] / norms
    vec_ref[...] = jnp.concatenate([squares, norms, scale, total[1:2]], axis=0)
    scaled = (dy_ref[...].astype(F32) * scale).astype(BF16)
    scaled_ref[...] = scaled
    y = lax.axis_index("cols")
    h0_ref[...] = nt(block(m_ref, y + 2, 0), scaled)
    h1_ref[...] = nt(block(m_ref, y + 2, 1), scaled)


def near_kernel(m_ref, scaled_ref, up_ref, down_ref):
    y = lax.axis_index("cols")
    up_ref[...] = nt(block(m_ref, y + 1, 1), scaled_ref[...])
    down_ref[...] = nt(block(m_ref, y - 1, 0), scaled_ref[...])


def relay_kernel(m_ref, scaled_ref, u0_ref, u1_ref, up_ref, down_ref):
    y = lax.axis_index("cols")
    up_ref[...] = u0_ref[...] + nt(block(m_ref, y + 1, 0), scaled_ref[...])
    down_ref[...] = u1_ref[...] + nt(block(m_ref, y - 1, 1), scaled_ref[...])


def own_kernel(m_ref, scaled_ref, own_ref):
    own_ref[...] = nt(block(m_ref, lax.axis_index("cols")), scaled_ref[...])


def gather_kernel(own_ref, v0_ref, v1_ref, sum_ref):
    half = own_ref.shape[0] // 2
    sum_ref[:half] = own_ref[:half] + v1_ref[...]
    sum_ref[half:] = own_ref[half:] + v0_ref[...]


def finish_kernel(own_ref, w0_ref, w1_ref, out_ref, done_ref):
    half = own_ref.shape[0] // 2
    out_ref[:half] = (own_ref[:half] + w0_ref[...]).astype(BF16)
    out_ref[half:] = (own_ref[half:] + w1_ref[...]).astype(BF16)
    done_ref[...] = jnp.zeros_like(done_ref)


def a_kernel(factor, vec_ref, dy_ref, b_ref, x_ref, m_ref, *refs):
    outs, whole = refs[:-1], refs[-1]
    scale = vec_ref[2:3] * factor
    wide = b_ref[...].astype(F32) * scale
    p_t = fold(nt(hi_lo(wide), dy_ref[...]))
    left = hi_lo(p_t)
    right = hi_lo(wide * (vec_ref[3:4] / vec_ref[0:1]))
    rows = m_ref.shape[0]
    tile = 512
    for r in range(rows // tile):
        at = slice(r * tile, (r + 1) * tile)
        whole[:, at] = fold(nn(left, x_ref[:, at]) - nt(right, m_ref[at]))
    split(whole, outs, lax.axis_index("dp"), 1)


def split(whole, outs, index, axis):
    count = len(outs)
    size = whole.shape[axis] // count
    for k, ref in enumerate(outs):
        at = pl.ds(pl.multiple_of(lax.rem(index + k, count) * size, 128 if axis else 8), size)
        ref[...] = whole[:, at] if axis else whole[at]


def sum_kernel(*refs):
    refs[-1][...] = functools.reduce(jnp.add, [ref[...] for ref in refs[:-1]])


def add(*ins, after=()):
    return call(sum_kernel, [out(ins[0].shape)], [VMEM] * len(ins), *ins, after=after)[0]


def halve_kernel(position, left_ref, right_ref, keep_ref, send_ref, whole):
    whole[...] = left_ref[...] + right_ref[...]
    split(whole, [keep_ref, send_ref], position(), 0)


def halve(left, right, position, after=()):
    rows, cols = left.shape
    return call(
        functools.partial(halve_kernel, position),
        [out((rows // 2, cols))] * 2,
        [VMEM] * 2,
        left, right,
        scratch=[pltpu.VMEM((rows, cols), F32)],
        after=after,
    )


def join_kernel(position, axis, *refs):
    ins, whole = refs[:-1], refs[-1]
    count = len(ins)
    size = ins[0].shape[axis]
    for k, ref in enumerate(ins):
        start = lax.rem(position() + count - k, count) * size
        at = pl.ds(pl.multiple_of(start, 128 if axis else 8), size)
        if axis:
            whole[:, at] = ref[...]
        else:
            whole[at] = ref[...]


def join(ins, position, axis, after=()):
    shape = list(ins[0].shape)
    shape[axis] *= len(ins)
    return call(
        functools.partial(join_kernel, position, axis),
        [out(tuple(shape))],
        [VMEM] * len(ins),
        *ins,
        after=after,
    )[0]


def b_kernel(factor, vec_ref, bq_ref, am_ref, keep_ref, send_ref, whole):
    ratio = vec_ref[3:4] / vec_ref[0:1]
    whole[...] = (vec_ref[2:3] * factor) * (bq_ref[...] - ratio * am_ref[...])
    split(whole, [keep_ref, send_ref], core_bit(), 0)


def add_halves_kernel(left_ref, right_ref, top_ref, bottom_ref):
    half = top_ref.shape[0]
    top_ref[...] = left_ref[:half] + right_ref[:half]
    bottom_ref[...] = left_ref[half:] + right_ref[half:]


def pair_kernel(top_ref, top_more_ref, bottom_ref, bottom_more_ref, top_out_ref, bottom_out_ref):
    half = top_ref.shape[0]
    top_out_ref[:half] = top_ref[...]
    top_out_ref[half:] = top_more_ref[...]
    bottom_out_ref[:half] = bottom_ref[...]
    bottom_out_ref[half:] = bottom_more_ref[...]


def a_join_kernel(top_ref, top_more_ref, bottom_ref, bottom_more_ref, whole, done_ref):
    done_ref[...] = jnp.zeros_like(done_ref)
    z = dp_index()
    first = z + 1 - 2 * lax.rem(z, 2)
    second = 3 - z
    half, size = top_ref.shape[0] // 2, top_ref.shape[1]
    for row, ref, near, far in (
        (0, top_ref, z, second),
        (0, top_more_ref, first, 3 - first),
        (half, bottom_ref, z, first),
        (half, bottom_more_ref, second, 3 - first),
    ):
        whole[row:row + half, pl.ds(pl.multiple_of(near * size, 128), size)] = ref[:half]
        whole[row:row + half, pl.ds(pl.multiple_of(far * size, 128), size)] = ref[half:]


def b_stack_kernel(left_ref, right_ref, vec_ref, out_ref):
    rows = left_ref.shape[0]
    out_ref[:rows] = left_ref[...] + right_ref[...]
    out_ref[rows:] = jnp.broadcast_to(vec_ref[3:4], left_ref.shape)


def b_unstack_kernel(factor, left_ref, right_ref, vec_ref, b_ref, mag_ref):
    rows = b_ref.shape[0]
    total = left_ref[...] + right_ref[...]
    b_ref[...] = total[:rows]
    mag_ref[...] = factor * total[rows:rows + 1] / vec_ref[1:2]


def core_bit():
    return lax.rem(lax.axis_index("rows"), 2)


def near_bit():
    return lax.rem(lax.div(lax.div(lax.axis_index("rows"), 2) + 1, 2), 2)


def far_bit():
    return lax.div(lax.axis_index("rows"), 4)


def dp_index():
    return lax.axis_index("dp")


def ring(value, axis, k, count=4):
    return lax.ppermute(value, axis, [(i, (i + k) % count) for i in range(count)])


def ring_x(value, k, count=8):
    return lax.ppermute(value, "rows", [(i, (i + 2 * k) % count) for i in range(count)])


def swap(value, axis, step):
    return lax.ppermute(value, axis, [(i, i ^ 1 if step == 0 else 3 - i) for i in range(4)])


def swap_x(value, step):
    return lax.ppermute(value, "rows", [(i, i ^ 2 if step == 0 else 6 - 2 * (i // 2) + i % 2) for i in range(8)])


def swap_core(value, count=8):
    return lax.ppermute(value, "rows", [(i, i ^ 1) for i in range(count)])


def shards(x, dy, w, a, b, mag):
    rows, cols = w.shape
    toks, rank = x.shape[0], a.shape[1]
    groups, full_rows = 4, rows * 8
    gamma = float(toks * groups) ** (-0.5)
    mag = mag.reshape(1, cols)
    m, stat, bq, am = merge(w, x, a.T, b, dy)

    m = pltpu.with_memory_space_constraint(m, pltpu.VMEM)
    stat = stat + swap_core(stat)
    far = rows // 8
    vec, scaled, h0, h1 = call(
        far_kernel,
        [out((4, cols)), out((toks, cols), BF16), out((far, toks)), out((far, toks))],
        [VMEM] * 7,
        stat, ring_x(stat, 1), ring_x(stat, 2), ring_x(stat, 3), mag, dy, m,
    )
    u0, u1 = ring(h0, "cols", 1), ring(h1, "cols", 3)
    keep, send = call(
        functools.partial(b_kernel, 2.0 * gamma),
        [out((rank // 2, cols))] * 2,
        [VMEM] * 3,
        vec, bq, am,
        scratch=[pltpu.VMEM((rank, cols), F32)],
    )
    half = [out((far, toks))] * 2
    up, down = call(near_kernel, half, [VMEM] * 2, m, scaled, after=[send])
    v0, v1 = ring(up, "cols", 1), ring(down, "cols", 3)
    keep, send = halve(keep, swap_core(send), near_bit, after=[up])
    pieces = call(
        functools.partial(a_kernel, 2.0 * gamma),
        [out((rank, rows // 4))] * 4,
        [VMEM] * 5,
        vec, dy, b, x, m,
        scratch=[pltpu.VMEM((rank, rows), F32)],
        after=[send],
    )
    keep, send = halve(keep, swap_x(send, 0), far_bit, after=[pieces[0]])
    pieces = [pieces[0]] + [ring(pieces[k], "dp", k) for k in (2, 1, 3)]
    own = call(own_kernel, [out((rows // 4, toks))], [VMEM] * 2, m, scaled, after=[send, u0, u1])[0]

    own = call(gather_kernel, [out((rows // 4, toks))], [VMEM] * 3, own, v0, v1)[0]
    piece = add(*pieces, after=[own])
    stack = call(
        b_stack_kernel, [out((rank // 4, cols))], [VMEM] * 3, keep, swap_x(send, 1), vec, after=[piece]
    )[0]
    piece = add(piece, swap(piece, "cols", 0), after=[stack])
    last = (piece, swap(piece, "cols", 1))
    stack = add(stack, swap(stack, "dp", 0), after=[piece])
    piece = [out((rank // 2, rows // 4))] * 2
    top, bottom = call(add_halves_kernel, piece, [VMEM] * 2, *last, after=[stack])
    up, down = call(relay_kernel, half, [VMEM] * 4, m, scaled, u0, u1, after=[top])
    w0, w1 = ring(up, "cols", 1), ring(down, "cols", 3)
    b_part, mag_grad = call(
        functools.partial(b_unstack_kernel, gamma / float(full_rows) ** 0.5),
        [out((rank // 8, cols)), out((1, cols))],
        [VMEM] * 3,
        stack, swap(stack, "dp", 1), vec,
        after=[up],
    )
    top, bottom = call(
        pair_kernel,
        [out((rank, rows // 4))] * 2,
        [VMEM] * 4,
        top, swap(top, "dp", 1), bottom, swap(bottom, "dp", 0),
        after=[b_part],
    )
    b_part = join([b_part, swap_x(b_part, 1)], far_bit, 0, after=[top])
    grad, done = call(
        finish_kernel,
        [out((rows // 4, toks), BF16), out((8, 128))],
        [VMEM] * 3,
        own, w0, w1,
        after=[b_part],
    )
    a_grad, done = call(
        a_join_kernel,
        [out((rank, rows)), out((8, 128))],
        [VMEM] * 4,
        top, swap(top, "dp", 0), bottom, swap(bottom, "dp", 1),
        after=[done],
    )
    b_part = join([b_part, swap_x(b_part, 0)], near_bit, 0, after=[done])
    b_grad = join([b_part, swap_core(b_part)], core_bit, 0)
    return grad, a_grad.T, b_grad, mag_grad.reshape(cols)


def solution(mesh):
    return jax.shard_map(
        shards,
        mesh=mesh,
        in_specs=(
            P("dp", "rows"),
            P("dp", "cols"),
            P("rows", "cols"),
            P("rows", None),
            P(None, "cols"),
            P("cols"),
        ),
        out_specs=(P(("rows", "cols"), "dp"), P("rows", None), P(None, "cols"), P("cols")),
        check_vma=False,
    )
```

```python
import functools

import jax
import jax.numpy as jnp
from jax import lax
from jax.experimental import pallas as pl
from jax.experimental.pallas import tpu as pltpu
from jax.sharding import PartitionSpec as P

EPS = 1e-06
F32 = jnp.float32
BF16 = jnp.bfloat16
MIB = 1024 * 1024

ANY = pl.BlockSpec(memory_space=pl.ANY)
VMEM = pl.BlockSpec(memory_space=pltpu.VMEM)
HBM = pl.BlockSpec(memory_space=pltpu.HBM)


def nn(a, b):
    return lax.dot_general(a, b, (((1,), (0,)), ((), ())), preferred_element_type=F32)


def nt(a, b):
    return lax.dot_general(a, b, (((1,), (1,)), ((), ())), preferred_element_type=F32)


def tn(a, b):
    return lax.dot_general(a, b, (((0,), (0,)), ((), ())), preferred_element_type=F32)


def hi_lo(value):
    hi = value.astype(BF16)
    lo = (value - hi.astype(F32)).astype(BF16)
    return jnp.concatenate([hi, lo], axis=0)


def fold(value):
    half = value.shape[0] // 2
    return value[:half] + value[half:]


def call(kernel, outs, specs, *args, scratch=(), vmem=16, flops=1, data=1, after=()):
    used = len(args)

    def body(*refs):
        kernel(*refs[:used], *refs[used + len(after):])

    return pl.pallas_call(
        body,
        out_shape=outs,
        in_specs=list(specs) + [ANY] * len(after),
        out_specs=[VMEM for _ in outs],
        scratch_shapes=list(scratch),
        compiler_params=pltpu.CompilerParams(vmem_limit_bytes=vmem * MIB),
        cost_estimate=pl.CostEstimate(flops=flops, bytes_accessed=data, transcendentals=0),
    )(*args, *after)


def hold(values, after):
    count = len(values)
    return pl.pallas_call(
        lambda *refs: None,
        out_shape=[out(value.shape, value.dtype) for value in values],
        in_specs=[ANY] * (count + len(after)),
        out_specs=[ANY] * count,
        input_output_aliases={k: k for k in range(count)},
        compiler_params=pltpu.CompilerParams(vmem_limit_bytes=MIB),
    )(*values, *after)


def out(shape, dtype=F32):
    return jax.ShapeDtypeStruct(shape, dtype)


def merge_kernel(
    steps, w_ref, x_ref, a_ref, b_ref, dy_ref, m_ref, stat_ref, bq_ref, am_ref,
    xa, b2, dy, acc, qt, sq, w_sem, x_sem, a_sem, b_sem, dy_sem,
):
    rows, cols = w_ref.shape
    toks = x_ref.shape[0]
    step = rows // steps
    tile = 2048
    b_copy = pltpu.make_async_copy(b_ref, b2, b_sem)
    dy_copy = pltpu.make_async_copy(dy_ref, dy, dy_sem)
    a_copy = pltpu.make_async_copy(a_ref, xa.at[toks:], a_sem)

    def w_copy(i):
        part = pl.ds(pl.multiple_of(i * step, step), step)
        return pltpu.make_async_copy(w_ref.at[part], m_ref.at[part], w_sem.at[i])

    x_copy = pltpu.make_async_copy(x_ref, xa.at[:toks], x_sem)
    b_copy.start()
    a_copy.start()
    w_copy(0).start()
    x_copy.start()
    for i in range(1, steps):
        w_copy(i).start()
    dy_copy.start()
    acc[...] = jnp.zeros_like(acc)
    qt[...] = jnp.zeros_like(qt)
    sq[...] = jnp.zeros_like(sq)
    b_copy.wait()
    a_copy.wait()
    x_copy.wait()
    b2[...] = b2[...] + b2[...]

    @pl.loop(0, steps)
    def _(i):
        w_copy(i).wait()
        part = pl.ds(pl.multiple_of(i * step, step), step)
        xa_part = xa[:, part]
        a_part = xa_part[toks:]
        for c in range(cols // tile):
            at = slice(c * tile, (c + 1) * tile)
            m = (m_ref[part, at].astype(F32) + tn(a_part, b2[:, at])).astype(BF16)
            m_ref[part, at] = m
            wide = m.astype(F32)
            sq[:, at] += jnp.sum((wide * wide).reshape(step // 8, 8, tile), axis=0)
            acc[:, at] += nn(xa_part, m)
        qt[...] += nt(a_part, xa_part[:toks])

    dy_copy.wait()
    am_ref[...] = acc[toks:]
    stat_ref[0:1] = jnp.sum(sq[...], axis=0, keepdims=True)
    stat_ref[1:2] = jnp.sum(acc[:toks] * dy[...].astype(F32), axis=0, keepdims=True)
    bq_ref[...] = fold(nn(hi_lo(qt[...]), dy[...]))


def merge(w, x, a_t, b, dy):
    rows, cols = w.shape
    toks = x.shape[0]
    rank = b.shape[0]
    steps = rows // 512
    dma = pltpu.SemaphoreType.DMA
    return call(
        functools.partial(merge_kernel, steps),
        [pltpu.VMEM((rows, cols), BF16), out((2, cols)), out((rank, cols)), out((rank, cols))],
        [HBM] * 5,
        *[pltpu.with_memory_space_constraint(value, pltpu.HBM) for value in (w, x, a_t, b, dy)],
        scratch=[
            pltpu.VMEM((toks + rank, rows), BF16),
            pltpu.VMEM((rank, cols), BF16),
            pltpu.VMEM((toks, cols), BF16),
            pltpu.VMEM((toks + rank, cols), F32),
            pltpu.VMEM((rank, toks), F32),
            pltpu.VMEM((8, cols), F32),
            dma((steps,)), dma, dma, dma, dma,
        ],
        vmem=32,
        flops=2 * rows * cols * (toks + 2 * rank),
        data=rows * cols * 2,
    )


def block(m_ref, index, half=None, count=4):
    size = m_ref.shape[0] // count
    start = lax.rem(index + count, count) * size
    if half is not None:
        size //= 2
        start += half * size
    return m_ref[pl.ds(pl.multiple_of(start, 64), size)]


def far_kernel(stat_ref, r1_ref, r2_ref, r3_ref, mag_ref, dy_ref, m_ref, vec_ref, scaled_ref, h0_ref, h1_ref):
    total = (stat_ref[...] + r2_ref[...]) + (r1_ref[...] + r3_ref[...])
    squares = total[0:1] + EPS
    norms = jnp.sqrt(squares)
    scale = mag_ref[...] / norms
    vec_ref[...] = jnp.concatenate([squares, norms, scale, total[1:2]], axis=0)
    scaled = (dy_ref[...].astype(F32) * scale).astype(BF16)
    scaled_ref[...] = scaled
    y = lax.axis_index("cols")
    h0_ref[...] = nt(block(m_ref, y + 2, 0), scaled)
    h1_ref[...] = nt(block(m_ref, y + 2, 1), scaled)


def near_kernel(m_ref, scaled_ref, up_ref, down_ref):
    y = lax.axis_index("cols")
    up_ref[...] = nt(block(m_ref, y + 1, 1), scaled_ref[...])
    down_ref[...] = nt(block(m_ref, y - 1, 0), scaled_ref[...])


def relay_kernel(m_ref, scaled_ref, u0_ref, u1_ref, up_ref, down_ref):
    y = lax.axis_index("cols")
    up_ref[...] = u0_ref[...] + nt(block(m_ref, y + 1, 0), scaled_ref[...])
    down_ref[...] = u1_ref[...] + nt(block(m_ref, y - 1, 1), scaled_ref[...])


def own_kernel(m_ref, scaled_ref, own_ref):
    own_ref[...] = nt(block(m_ref, lax.axis_index("cols")), scaled_ref[...])


def gather_kernel(own_ref, v0_ref, v1_ref, sum_ref):
    half = own_ref.shape[0] // 2
    sum_ref[:half] = own_ref[:half] + v1_ref[...]
    sum_ref[half:] = own_ref[half:] + v0_ref[...]


def finish_kernel(own_ref, w0_ref, w1_ref, out_ref):
    half = own_ref.shape[0] // 2
    out_ref[:half] = (own_ref[:half] + w0_ref[...]).astype(BF16)
    out_ref[half:] = (own_ref[half:] + w1_ref[...]).astype(BF16)


def a_kernel(factor, vec_ref, dy_ref, b_ref, x_ref, m_ref, *refs):
    outs, whole = refs[:-1], refs[-1]
    scale = vec_ref[2:3] * factor
    wide = b_ref[...].astype(F32) * scale
    p_t = fold(nt(hi_lo(wide), dy_ref[...]))
    left = hi_lo(p_t)
    right = hi_lo(wide * (vec_ref[3:4] / vec_ref[0:1]))
    rows = m_ref.shape[0]
    tile = 512
    for r in range(rows // tile):
        at = slice(r * tile, (r + 1) * tile)
        whole[:, at] = fold(nn(left, x_ref[:, at]) - nt(right, m_ref[at]))
    split(whole, outs, lax.axis_index("dp"), 1)


def split(whole, outs, index, axis):
    count = len(outs)
    size = whole.shape[axis] // count
    for k, ref in enumerate(outs):
        at = pl.ds(pl.multiple_of(lax.rem(index + k, count) * size, 128 if axis else 8), size)
        ref[...] = whole[:, at] if axis else whole[at]


def sum_kernel(*refs):
    refs[-1][...] = functools.reduce(jnp.add, [ref[...] for ref in refs[:-1]])


def add(*ins, after=()):
    return call(sum_kernel, [out(ins[0].shape)], [VMEM] * len(ins), *ins, after=after)[0]


def halve_kernel(position, left_ref, right_ref, keep_ref, send_ref, whole):
    whole[...] = left_ref[...] + right_ref[...]
    split(whole, [keep_ref, send_ref], position(), 0)


def halve(left, right, position, after=()):
    rows, cols = left.shape
    return call(
        functools.partial(halve_kernel, position),
        [out((rows // 2, cols))] * 2,
        [VMEM] * 2,
        left, right,
        scratch=[pltpu.VMEM((rows, cols), F32)],
        after=after,
    )


def join_kernel(position, axis, *refs):
    ins, whole = refs[:-1], refs[-1]
    count = len(ins)
    size = ins[0].shape[axis]
    for k, ref in enumerate(ins):
        start = lax.rem(position() + count - k, count) * size
        at = pl.ds(pl.multiple_of(start, 128 if axis else 8), size)
        if axis:
            whole[:, at] = ref[...]
        else:
            whole[at] = ref[...]


def join(ins, position, axis, after=()):
    shape = list(ins[0].shape)
    shape[axis] *= len(ins)
    return call(
        functools.partial(join_kernel, position, axis),
        [out(tuple(shape))],
        [VMEM] * len(ins),
        *ins,
        after=after,
    )[0]


def b_kernel(factor, vec_ref, bq_ref, am_ref, keep_ref, send_ref, whole):
    ratio = vec_ref[3:4] / vec_ref[0:1]
    whole[...] = (vec_ref[2:3] * factor) * (bq_ref[...] - ratio * am_ref[...])
    split(whole, [keep_ref, send_ref], core_bit(), 0)


def add_halves_kernel(left_ref, right_ref, top_ref, bottom_ref):
    half = top_ref.shape[0]
    top_ref[...] = left_ref[:half] + right_ref[:half]
    bottom_ref[...] = left_ref[half:] + right_ref[half:]


def pair_kernel(top_ref, top_more_ref, bottom_ref, bottom_more_ref, top_out_ref, bottom_out_ref):
    half = top_ref.shape[0]
    top_out_ref[:half] = top_ref[...]
    top_out_ref[half:] = top_more_ref[...]
    bottom_out_ref[:half] = bottom_ref[...]
    bottom_out_ref[half:] = bottom_more_ref[...]


def a_join_kernel(top_ref, top_more_ref, bottom_ref, bottom_more_ref, whole, done_ref):
    done_ref[...] = jnp.zeros_like(done_ref)
    z = dp_index()
    first = z + 1 - 2 * lax.rem(z, 2)
    second = 3 - z
    half, size = top_ref.shape[0] // 2, top_ref.shape[1]
    for row, ref, near, far in (
        (0, top_ref, z, second),
        (0, top_more_ref, first, 3 - first),
        (half, bottom_ref, z, first),
        (half, bottom_more_ref, second, 3 - first),
    ):
        whole[row:row + half, pl.ds(pl.multiple_of(near * size, 128), size)] = ref[:half]
        whole[row:row + half, pl.ds(pl.multiple_of(far * size, 128), size)] = ref[half:]


def b_stack_kernel(left_ref, right_ref, vec_ref, out_ref):
    rows = left_ref.shape[0]
    out_ref[:rows] = left_ref[...] + right_ref[...]
    out_ref[rows:] = jnp.broadcast_to(vec_ref[3:4], left_ref.shape)


def b_unstack_kernel(factor, left_ref, right_ref, vec_ref, b_ref, mag_ref):
    rows = b_ref.shape[0]
    total = left_ref[...] + right_ref[...]
    b_ref[...] = total[:rows]
    mag_ref[...] = factor * total[rows:rows + 1] / vec_ref[1:2]


def core_bit():
    return lax.rem(lax.axis_index("rows"), 2)


def near_bit():
    return lax.rem(lax.div(lax.div(lax.axis_index("rows"), 2) + 1, 2), 2)


def far_bit():
    return lax.div(lax.axis_index("rows"), 4)


def dp_index():
    return lax.axis_index("dp")


def ring(value, axis, k, count=4):
    return lax.ppermute(value, axis, [(i, (i + k) % count) for i in range(count)])


def ring_x(value, k, count=8):
    return lax.ppermute(value, "rows", [(i, (i + 2 * k) % count) for i in range(count)])


def swap(value, axis, step):
    return lax.ppermute(value, axis, [(i, i ^ 1 if step == 0 else 3 - i) for i in range(4)])


def swap_x(value, step):
    return lax.ppermute(value, "rows", [(i, i ^ 2 if step == 0 else 6 - 2 * (i // 2) + i % 2) for i in range(8)])


def swap_core(value, count=8):
    return lax.ppermute(value, "rows", [(i, i ^ 1) for i in range(count)])


def shards(x, dy, w, a, b, mag):
    rows, cols = w.shape
    toks, rank = x.shape[0], a.shape[1]
    groups, full_rows = 4, rows * 8
    gamma = float(toks * groups) ** (-0.5)
    mag = mag.reshape(1, cols)
    m, stat, bq, am = merge(w, x, a.T, b, dy)

    m = pltpu.with_memory_space_constraint(m, pltpu.VMEM)
    stat = stat + swap_core(stat)
    far = rows // 8
    vec, scaled, h0, h1 = call(
        far_kernel,
        [out((4, cols)), out((toks, cols), BF16), out((far, toks)), out((far, toks))],
        [VMEM] * 7,
        stat, ring_x(stat, 1), ring_x(stat, 2), ring_x(stat, 3), mag, dy, m,
    )
    u0, u1 = ring(h0, "cols", 1), ring(h1, "cols", 3)
    keep, send = call(
        functools.partial(b_kernel, 2.0 * gamma),
        [out((rank // 2, cols))] * 2,
        [VMEM] * 3,
        vec, bq, am,
        scratch=[pltpu.VMEM((rank, cols), F32)],
    )
    pieces = call(
        functools.partial(a_kernel, 2.0 * gamma),
        [out((rank, rows // 4))] * 4,
        [VMEM] * 5,
        vec, dy, b, x, m,
        scratch=[pltpu.VMEM((rank, rows), F32)],
        after=[send],
    )
    keep, send = halve(keep, swap_core(send), near_bit, after=[pieces[0]])
    pieces = [pieces[0]] + [ring(pieces[k], "dp", k) for k in (2, 1, 3)]
    half = [out((far, toks))] * 2
    up, down = call(near_kernel, half, [VMEM] * 2, m, scaled, after=[send])
    own = call(own_kernel, [out((rows // 4, toks))], [VMEM] * 2, m, scaled, after=[up])[0]
    up, down = hold([up, down], [own, u0, u1])
    v0, v1 = ring(up, "cols", 1), ring(down, "cols", 3)
    w_up, w_down = call(relay_kernel, half, [VMEM] * 4, m, scaled, u0, u1, after=[up])

    piece = add(*pieces, after=[w_up])
    keep, send = halve(keep, swap_x(send, 0), far_bit, after=[piece])
    own = call(gather_kernel, [out((rows // 4, toks))], [VMEM] * 3, own, v0, v1, after=[send])[0]
    stack = call(
        b_stack_kernel, [out((rank // 4, cols))], [VMEM] * 3, keep, swap_x(send, 1), vec, after=[own]
    )[0]
    piece = add(piece, swap(piece, "cols", 0), after=[stack])
    last = (piece, swap(piece, "cols", 1))
    stack = add(stack, swap(stack, "dp", 0), after=[piece])
    piece = [out((rank // 2, rows // 4))] * 2
    top, bottom = call(add_halves_kernel, piece, [VMEM] * 2, *last, after=[stack])
    b_part, mag_grad = call(
        functools.partial(b_unstack_kernel, gamma / float(full_rows) ** 0.5),
        [out((rank // 8, cols)), out((1, cols))],
        [VMEM] * 3,
        stack, swap(stack, "dp", 1), vec,
        after=[top],
    )
    b_part = join([b_part, swap_x(b_part, 1)], far_bit, 0)
    top, bottom = call(
        pair_kernel,
        [out((rank, rows // 4))] * 2,
        [VMEM] * 4,
        top, swap(top, "dp", 1), bottom, swap(bottom, "dp", 0),
        after=[b_part],
    )
    w_up, w_down = hold([w_up, w_down], [top])
    w0, w1 = ring(w_up, "cols", 1), ring(w_down, "cols", 3)
    a_grad, done = call(
        a_join_kernel,
        [out((rank, rows)), out((8, 128))],
        [VMEM] * 4,
        top, swap(top, "dp", 0), bottom, swap(bottom, "dp", 1),
        after=[w_up],
    )
    b_part = join([b_part, swap_x(b_part, 0)], near_bit, 0, after=[done])
    grad = call(finish_kernel, [out((rows // 4, toks), BF16)], [VMEM] * 3, own, w0, w1, after=[b_part])[0]
    b_grad = join([b_part, swap_core(b_part)], core_bit, 0)
    return grad, a_grad.T, b_grad, mag_grad.reshape(cols)


def solution(mesh):
    return jax.shard_map(
        shards,
        mesh=mesh,
        in_specs=(
            P("dp", "rows"),
            P("dp", "cols"),
            P("rows", "cols"),
            P("rows", None),
            P(None, "cols"),
            P("cols"),
        ),
        out_specs=(P(("rows", "cols"), "dp"), P("rows", None), P(None, "cols"), P("cols")),
        check_vma=False,
    )
```

```python
import functools

import jax
import jax.numpy as jnp
from jax import lax
from jax.experimental import pallas as pl
from jax.experimental.pallas import tpu as pltpu
from jax.sharding import PartitionSpec as P

EPS = 1e-06
F32 = jnp.float32
BF16 = jnp.bfloat16
MIB = 1024 * 1024

ANY = pl.BlockSpec(memory_space=pl.ANY)
VMEM = pl.BlockSpec(memory_space=pltpu.VMEM)
HBM = pl.BlockSpec(memory_space=pltpu.HBM)


def nn(a, b):
    return lax.dot_general(a, b, (((1,), (0,)), ((), ())), preferred_element_type=F32)


def nt(a, b):
    return lax.dot_general(a, b, (((1,), (1,)), ((), ())), preferred_element_type=F32)


def tn(a, b):
    return lax.dot_general(a, b, (((0,), (0,)), ((), ())), preferred_element_type=F32)


def hi_lo(value):
    hi = value.astype(BF16)
    lo = (value - hi.astype(F32)).astype(BF16)
    return jnp.concatenate([hi, lo], axis=0)


def fold(value):
    half = value.shape[0] // 2
    return value[:half] + value[half:]


def call(kernel, outs, specs, *args, scratch=(), vmem=16, flops=1, data=1, after=()):
    used = len(args)

    def body(*refs):
        kernel(*refs[:used], *refs[used + len(after):])

    return pl.pallas_call(
        body,
        out_shape=outs,
        in_specs=list(specs) + [ANY] * len(after),
        out_specs=[VMEM for _ in outs],
        scratch_shapes=list(scratch),
        compiler_params=pltpu.CompilerParams(vmem_limit_bytes=vmem * MIB),
        cost_estimate=pl.CostEstimate(flops=flops, bytes_accessed=data, transcendentals=0),
    )(*args, *after)


def hold(values, after):
    count = len(values)
    return pl.pallas_call(
        lambda *refs: None,
        out_shape=[out(value.shape, value.dtype) for value in values],
        in_specs=[ANY] * (count + len(after)),
        out_specs=[ANY] * count,
        input_output_aliases={k: k for k in range(count)},
        compiler_params=pltpu.CompilerParams(vmem_limit_bytes=MIB),
    )(*values, *after)


def out(shape, dtype=F32):
    return jax.ShapeDtypeStruct(shape, dtype)


def merge_kernel(
    steps, w_ref, x_ref, a_ref, b_ref, dy_ref, m_ref, stat_ref, bq_ref, am_ref,
    xa, b2, dy, acc, qt, sq, w_sem, x_sem, a_sem, b_sem, dy_sem,
):
    rows, cols = w_ref.shape
    toks = x_ref.shape[0]
    step = rows // steps
    tile = 2048
    b_copy = pltpu.make_async_copy(b_ref, b2, b_sem)
    dy_copy = pltpu.make_async_copy(dy_ref, dy, dy_sem)
    a_copy = pltpu.make_async_copy(a_ref, xa.at[toks:], a_sem)

    def w_copy(i):
        part = pl.ds(pl.multiple_of(i * step, step), step)
        return pltpu.make_async_copy(w_ref.at[part], m_ref.at[part], w_sem.at[i])

    x_copy = pltpu.make_async_copy(x_ref, xa.at[:toks], x_sem)
    b_copy.start()
    a_copy.start()
    w_copy(0).start()
    x_copy.start()
    for i in range(1, steps):
        w_copy(i).start()
    dy_copy.start()
    acc[...] = jnp.zeros_like(acc)
    qt[...] = jnp.zeros_like(qt)
    sq[...] = jnp.zeros_like(sq)
    b_copy.wait()
    a_copy.wait()
    x_copy.wait()
    b2[...] = b2[...] + b2[...]

    @pl.loop(0, steps)
    def _(i):
        w_copy(i).wait()
        part = pl.ds(pl.multiple_of(i * step, step), step)
        xa_part = xa[:, part]
        a_part = xa_part[toks:]
        for c in range(cols // tile):
            at = slice(c * tile, (c + 1) * tile)
            m = (m_ref[part, at].astype(F32) + tn(a_part, b2[:, at])).astype(BF16)
            m_ref[part, at] = m
            wide = m.astype(F32)
            sq[:, at] += jnp.sum((wide * wide).reshape(step // 8, 8, tile), axis=0)
            acc[:, at] += nn(xa_part, m)
        qt[...] += nt(a_part, xa_part[:toks])

    dy_copy.wait()
    am_ref[...] = acc[toks:]
    stat_ref[0:1] = jnp.sum(sq[...], axis=0, keepdims=True)
    stat_ref[1:2] = jnp.sum(acc[:toks] * dy[...].astype(F32), axis=0, keepdims=True)
    bq_ref[...] = fold(nn(hi_lo(qt[...]), dy[...]))


def merge(w, x, a_t, b, dy):
    rows, cols = w.shape
    toks = x.shape[0]
    rank = b.shape[0]
    steps = rows // 512
    dma = pltpu.SemaphoreType.DMA
    return call(
        functools.partial(merge_kernel, steps),
        [pltpu.VMEM((rows, cols), BF16), out((2, cols)), out((rank, cols)), out((rank, cols))],
        [HBM] * 5,
        *[pltpu.with_memory_space_constraint(value, pltpu.HBM) for value in (w, x, a_t, b, dy)],
        scratch=[
            pltpu.VMEM((toks + rank, rows), BF16),
            pltpu.VMEM((rank, cols), BF16),
            pltpu.VMEM((toks, cols), BF16),
            pltpu.VMEM((toks + rank, cols), F32),
            pltpu.VMEM((rank, toks), F32),
            pltpu.VMEM((8, cols), F32),
            dma((steps,)), dma, dma, dma, dma,
        ],
        vmem=32,
        flops=2 * rows * cols * (toks + 2 * rank),
        data=rows * cols * 2,
    )


def block(m_ref, index, half=None, count=4):
    size = m_ref.shape[0] // count
    start = lax.rem(index + count, count) * size
    if half is not None:
        size //= 2
        start += half * size
    return m_ref[pl.ds(pl.multiple_of(start, 64), size)]


def far_kernel(stat_ref, r1_ref, r2_ref, r3_ref, mag_ref, dy_ref, m_ref, vec_ref, scaled_ref, h0_ref, h1_ref):
    total = (stat_ref[...] + r2_ref[...]) + (r1_ref[...] + r3_ref[...])
    squares = total[0:1] + EPS
    norms = jnp.sqrt(squares)
    scale = mag_ref[...] / norms
    vec_ref[...] = jnp.concatenate([squares, norms, scale, total[1:2]], axis=0)
    scaled = (dy_ref[...].astype(F32) * scale).astype(BF16)
    scaled_ref[...] = scaled
    y = lax.axis_index("cols")
    h0_ref[...] = nt(block(m_ref, y + 2, 0), scaled)
    h1_ref[...] = nt(block(m_ref, y + 2, 1), scaled)


def near_kernel(m_ref, scaled_ref, up_ref, down_ref):
    y = lax.axis_index("cols")
    up_ref[...] = nt(block(m_ref, y + 1, 1), scaled_ref[...])
    down_ref[...] = nt(block(m_ref, y - 1, 0), scaled_ref[...])


def relay_kernel(m_ref, scaled_ref, u0_ref, u1_ref, up_ref, down_ref):
    y = lax.axis_index("cols")
    up_ref[...] = u0_ref[...] + nt(block(m_ref, y + 1, 0), scaled_ref[...])
    down_ref[...] = u1_ref[...] + nt(block(m_ref, y - 1, 1), scaled_ref[...])


def own_kernel(m_ref, scaled_ref, own_ref):
    own_ref[...] = nt(block(m_ref, lax.axis_index("cols")), scaled_ref[...])


def gather_kernel(own_ref, v0_ref, v1_ref, sum_ref):
    half = own_ref.shape[0] // 2
    sum_ref[:half] = own_ref[:half] + v1_ref[...]
    sum_ref[half:] = own_ref[half:] + v0_ref[...]


def finish_kernel(own_ref, w0_ref, w1_ref, out_ref, done_ref):
    done_ref[...] = jnp.zeros_like(done_ref)
    half = own_ref.shape[0] // 2
    out_ref[:half] = (own_ref[:half] + w0_ref[...]).astype(BF16)
    out_ref[half:] = (own_ref[half:] + w1_ref[...]).astype(BF16)


def a_kernel(factor, vec_ref, dy_ref, b_ref, x_ref, m_ref, *refs):
    outs, whole = refs[:-1], refs[-1]
    scale = vec_ref[2:3] * factor
    wide = b_ref[...].astype(F32) * scale
    p_t = fold(nt(hi_lo(wide), dy_ref[...]))
    left = hi_lo(p_t)
    right = hi_lo(wide * (vec_ref[3:4] / vec_ref[0:1]))
    rows = m_ref.shape[0]
    tile = 512
    for r in range(rows // tile):
        at = slice(r * tile, (r + 1) * tile)
        whole[:, at] = fold(nn(left, x_ref[:, at]) - nt(right, m_ref[at]))
    split(whole, outs, lax.axis_index("dp"), 1)


def split(whole, outs, index, axis):
    count = len(outs)
    size = whole.shape[axis] // count
    for k, ref in enumerate(outs):
        at = pl.ds(pl.multiple_of(lax.rem(index + k, count) * size, 128 if axis else 8), size)
        ref[...] = whole[:, at] if axis else whole[at]


def sum_kernel(*refs):
    refs[-1][...] = functools.reduce(jnp.add, [ref[...] for ref in refs[:-1]])


def add(*ins, after=()):
    return call(sum_kernel, [out(ins[0].shape)], [VMEM] * len(ins), *ins, after=after)[0]


def halve_kernel(position, left_ref, right_ref, keep_ref, send_ref, whole):
    whole[...] = left_ref[...] + right_ref[...]
    split(whole, [keep_ref, send_ref], position(), 0)


def halve(left, right, position, after=()):
    rows, cols = left.shape
    return call(
        functools.partial(halve_kernel, position),
        [out((rows // 2, cols))] * 2,
        [VMEM] * 2,
        left, right,
        scratch=[pltpu.VMEM((rows, cols), F32)],
        after=after,
    )


def join_kernel(position, axis, *refs):
    ins, whole = refs[:-1], refs[-1]
    count = len(ins)
    size = ins[0].shape[axis]
    for k, ref in enumerate(ins):
        start = lax.rem(position() + count - k, count) * size
        at = pl.ds(pl.multiple_of(start, 128 if axis else 8), size)
        if axis:
            whole[:, at] = ref[...]
        else:
            whole[at] = ref[...]


def join(ins, position, axis, after=()):
    shape = list(ins[0].shape)
    shape[axis] *= len(ins)
    return call(
        functools.partial(join_kernel, position, axis),
        [out(tuple(shape))],
        [VMEM] * len(ins),
        *ins,
        after=after,
    )[0]


def b_kernel(factor, vec_ref, bq_ref, am_ref, keep_ref, send_ref, whole):
    ratio = vec_ref[3:4] / vec_ref[0:1]
    whole[...] = (vec_ref[2:3] * factor) * (bq_ref[...] - ratio * am_ref[...])
    split(whole, [keep_ref, send_ref], core_bit(), 0)


def add_halves_kernel(left_ref, right_ref, top_ref, bottom_ref):
    half = top_ref.shape[0]
    top_ref[...] = left_ref[:half] + right_ref[:half]
    bottom_ref[...] = left_ref[half:] + right_ref[half:]


def pair_kernel(top_ref, top_more_ref, bottom_ref, bottom_more_ref, top_out_ref, bottom_out_ref):
    half = top_ref.shape[0]
    top_out_ref[:half] = top_ref[...]
    top_out_ref[half:] = top_more_ref[...]
    bottom_out_ref[:half] = bottom_ref[...]
    bottom_out_ref[half:] = bottom_more_ref[...]


def a_join_kernel(top_ref, top_more_ref, bottom_ref, bottom_more_ref, whole, done_ref):
    done_ref[...] = jnp.zeros_like(done_ref)
    z = dp_index()
    first = z + 1 - 2 * lax.rem(z, 2)
    second = 3 - z
    half, size = top_ref.shape[0] // 2, top_ref.shape[1]
    for row, ref, near, far in (
        (0, top_ref, z, second),
        (0, top_more_ref, first, 3 - first),
        (half, bottom_ref, z, first),
        (half, bottom_more_ref, second, 3 - first),
    ):
        whole[row:row + half, pl.ds(pl.multiple_of(near * size, 128), size)] = ref[:half]
        whole[row:row + half, pl.ds(pl.multiple_of(far * size, 128), size)] = ref[half:]


def b_stack_kernel(left_ref, right_ref, vec_ref, out_ref):
    rows = left_ref.shape[0]
    out_ref[:rows] = left_ref[...] + right_ref[...]
    out_ref[rows:] = jnp.broadcast_to(vec_ref[3:4], left_ref.shape)


def b_unstack_kernel(factor, left_ref, right_ref, vec_ref, b_ref, mag_ref):
    rows = b_ref.shape[0]
    total = left_ref[...] + right_ref[...]
    b_ref[...] = total[:rows]
    mag_ref[...] = factor * total[rows:rows + 1] / vec_ref[1:2]


def core_bit():
    return lax.rem(lax.axis_index("rows"), 2)


def near_bit():
    return lax.rem(lax.div(lax.div(lax.axis_index("rows"), 2) + 1, 2), 2)


def far_bit():
    return lax.div(lax.axis_index("rows"), 4)


def dp_index():
    return lax.axis_index("dp")


def ring(value, axis, k, count=4):
    return lax.ppermute(value, axis, [(i, (i + k) % count) for i in range(count)])


def ring_x(value, k, count=8):
    return lax.ppermute(value, "rows", [(i, (i + 2 * k) % count) for i in range(count)])


def swap(value, axis, step):
    return lax.ppermute(value, axis, [(i, i ^ 1 if step == 0 else 3 - i) for i in range(4)])


def swap_x(value, step):
    return lax.ppermute(value, "rows", [(i, i ^ 2 if step == 0 else 6 - 2 * (i // 2) + i % 2) for i in range(8)])


def swap_core(value, count=8):
    return lax.ppermute(value, "rows", [(i, i ^ 1) for i in range(count)])


def shards(x, dy, w, a, b, mag):
    rows, cols = w.shape
    toks, rank = x.shape[0], a.shape[1]
    groups, full_rows = 4, rows * 8
    gamma = float(toks * groups) ** (-0.5)
    mag = mag.reshape(1, cols)
    m, stat, bq, am = merge(w, x, a.T, b, dy)

    m = pltpu.with_memory_space_constraint(m, pltpu.VMEM)
    stat = stat + swap_core(stat)
    far = rows // 8
    vec, scaled, h0, h1 = call(
        far_kernel,
        [out((4, cols)), out((toks, cols), BF16), out((far, toks)), out((far, toks))],
        [VMEM] * 7,
        stat, ring_x(stat, 1), ring_x(stat, 2), ring_x(stat, 3), mag, dy, m,
    )
    u0, u1 = ring(h0, "cols", 1), ring(h1, "cols", 3)
    keep, send = call(
        functools.partial(b_kernel, 2.0 * gamma),
        [out((rank // 2, cols))] * 2,
        [VMEM] * 3,
        vec, bq, am,
        scratch=[pltpu.VMEM((rank, cols), F32)],
    )
    half = [out((far, toks))] * 2
    up, down = call(near_kernel, half, [VMEM] * 2, m, scaled, after=[send])
    v0, v1 = ring(up, "cols", 1), ring(down, "cols", 3)
    keep, send = halve(keep, swap_core(send), near_bit, after=[up])
    pieces = call(
        functools.partial(a_kernel, 2.0 * gamma),
        [out((rank, rows // 4))] * 4,
        [VMEM] * 5,
        vec, dy, b, x, m,
        scratch=[pltpu.VMEM((rank, rows), F32)],
        after=[send],
    )
    keep, send = halve(keep, swap_x(send, 0), far_bit, after=[pieces[0]])
    pieces = [pieces[0]] + [ring(pieces[k], "dp", k) for k in (2, 1, 3)]
    own = call(own_kernel, [out((rows // 4, toks))], [VMEM] * 2, m, scaled, after=[send, u0, u1])[0]
    up, down = call(relay_kernel, half, [VMEM] * 4, m, scaled, u0, u1, after=[own])
    own = call(gather_kernel, [out((rows // 4, toks))], [VMEM] * 3, own, v0, v1, after=[up])[0]

    piece = add(*pieces, after=[own])
    stack = call(
        b_stack_kernel, [out((rank // 4, cols))], [VMEM] * 3, keep, swap_x(send, 1), vec, after=[piece]
    )[0]
    piece = add(piece, swap(piece, "cols", 0), after=[stack])
    last = (piece, swap(piece, "cols", 1))
    stack = add(stack, swap(stack, "dp", 0), after=[piece])
    up, down = hold([up, down], [stack])
    w0, w1 = ring(up, "cols", 1), ring(down, "cols", 3)
    piece = [out((rank // 2, rows // 4))] * 2
    top, bottom = call(add_halves_kernel, piece, [VMEM] * 2, *last, after=[up])
    b_part, mag_grad = call(
        functools.partial(b_unstack_kernel, gamma / float(full_rows) ** 0.5),
        [out((rank // 8, cols)), out((1, cols))],
        [VMEM] * 3,
        stack, swap(stack, "dp", 1), vec,
        after=[top],
    )
    b_part = join([b_part, swap_x(b_part, 1)], far_bit, 0)
    top, bottom = call(
        pair_kernel,
        [out((rank, rows // 4))] * 2,
        [VMEM] * 4,
        top, swap(top, "dp", 1), bottom, swap(bottom, "dp", 0),
        after=[b_part],
    )
    grad, done = call(
        finish_kernel, [out((rows // 4, toks), BF16), out((8, 128))], [VMEM] * 3, own, w0, w1, after=[top]
    )
    a_grad, done = call(
        a_join_kernel,
        [out((rank, rows)), out((8, 128))],
        [VMEM] * 4,
        top, swap(top, "dp", 0), bottom, swap(bottom, "dp", 1),
        after=[done],
    )
    b_part = join([b_part, swap_x(b_part, 0)], near_bit, 0, after=[done])
    b_grad = join([b_part, swap_core(b_part)], core_bit, 0)
    return grad, a_grad.T, b_grad, mag_grad.reshape(cols)


def solution(mesh):
    return jax.shard_map(
        shards,
        mesh=mesh,
        in_specs=(
            P("dp", "rows"),
            P("dp", "cols"),
            P("rows", "cols"),
            P("rows", None),
            P(None, "cols"),
            P("cols"),
        ),
        out_specs=(P(("rows", "cols"), "dp"), P("rows", None), P(None, "cols"), P("cols")),
        check_vma=False,
    )
```

```python
import functools

import jax
import jax.numpy as jnp
from jax import lax
from jax.experimental import pallas as pl
from jax.experimental.pallas import tpu as pltpu
from jax.sharding import PartitionSpec as P

EPS = 1e-06
F32 = jnp.float32
BF16 = jnp.bfloat16
MIB = 1024 * 1024

ANY = pl.BlockSpec(memory_space=pl.ANY)
VMEM = pl.BlockSpec(memory_space=pltpu.VMEM)
HBM = pl.BlockSpec(memory_space=pltpu.HBM)


def nn(a, b):
    return lax.dot_general(a, b, (((1,), (0,)), ((), ())), preferred_element_type=F32)


def nt(a, b):
    return lax.dot_general(a, b, (((1,), (1,)), ((), ())), preferred_element_type=F32)


def tn(a, b):
    return lax.dot_general(a, b, (((0,), (0,)), ((), ())), preferred_element_type=F32)


def hi_lo(value):
    hi = value.astype(BF16)
    lo = (value - hi.astype(F32)).astype(BF16)
    return jnp.concatenate([hi, lo], axis=0)


def fold(value):
    half = value.shape[0] // 2
    return value[:half] + value[half:]


def call(kernel, outs, specs, *args, scratch=(), vmem=16, flops=1, data=1, after=()):
    used = len(args)

    def body(*refs):
        kernel(*refs[:used], *refs[used + len(after):])

    return pl.pallas_call(
        body,
        out_shape=outs,
        in_specs=list(specs) + [ANY] * len(after),
        out_specs=[VMEM for _ in outs],
        scratch_shapes=list(scratch),
        compiler_params=pltpu.CompilerParams(vmem_limit_bytes=vmem * MIB),
        cost_estimate=pl.CostEstimate(flops=flops, bytes_accessed=data, transcendentals=0),
    )(*args, *after)


def hold(values, after):
    count = len(values)
    return pl.pallas_call(
        lambda *refs: None,
        out_shape=[out(value.shape, value.dtype) for value in values],
        in_specs=[ANY] * (count + len(after)),
        out_specs=[ANY] * count,
        input_output_aliases={k: k for k in range(count)},
        compiler_params=pltpu.CompilerParams(vmem_limit_bytes=MIB),
    )(*values, *after)


def out(shape, dtype=F32):
    return jax.ShapeDtypeStruct(shape, dtype)


def merge_kernel(
    steps, w_ref, x_ref, a_ref, b_ref, dy_ref, m_ref, stat_ref, am_ref,
    xa, b2, dy, acc, sq, w_sem, x_sem, a_sem, b_sem, dy_sem,
):
    rows, cols = w_ref.shape
    toks = x_ref.shape[0]
    step = rows // steps
    tile = 2048
    b_copy = pltpu.make_async_copy(b_ref, b2, b_sem)
    dy_copy = pltpu.make_async_copy(dy_ref, dy, dy_sem)
    a_copy = pltpu.make_async_copy(a_ref, xa.at[toks:], a_sem)

    def w_copy(i):
        part = pl.ds(pl.multiple_of(i * step, step), step)
        return pltpu.make_async_copy(w_ref.at[part], m_ref.at[part], w_sem.at[i])

    x_copy = pltpu.make_async_copy(x_ref, xa.at[:toks], x_sem)
    b_copy.start()
    a_copy.start()
    w_copy(0).start()
    x_copy.start()
    for i in range(1, steps):
        w_copy(i).start()
    dy_copy.start()
    acc[...] = jnp.zeros_like(acc)
    sq[...] = jnp.zeros_like(sq)
    b_copy.wait()
    a_copy.wait()
    x_copy.wait()
    b2[...] = b2[...] + b2[...]

    @pl.loop(0, steps)
    def _(i):
        w_copy(i).wait()
        part = pl.ds(pl.multiple_of(i * step, step), step)
        xa_part = xa[:, part]
        a_part = xa_part[toks:]
        for c in range(cols // tile):
            at = slice(c * tile, (c + 1) * tile)
            m = (m_ref[part, at].astype(F32) + tn(a_part, b2[:, at])).astype(BF16)
            m_ref[part, at] = m
            wide = m.astype(F32)
            sq[:, at] += jnp.sum((wide * wide).reshape(step // 8, 8, tile), axis=0)
            acc[:, at] += nn(xa_part, m)

    dy_copy.wait()
    am_ref[...] = acc[toks:]
    stat_ref[0:1] = jnp.sum(sq[...], axis=0, keepdims=True)
    stat_ref[1:2] = jnp.sum(acc[:toks] * dy[...].astype(F32), axis=0, keepdims=True)


def merge(w, x, a_t, b, dy):
    rows, cols = w.shape
    toks = x.shape[0]
    rank = b.shape[0]
    steps = rows // 512
    dma = pltpu.SemaphoreType.DMA
    return call(
        functools.partial(merge_kernel, steps),
        [pltpu.VMEM((rows, cols), BF16), out((2, cols)), out((rank, cols))],
        [HBM] * 5,
        *[pltpu.with_memory_space_constraint(value, pltpu.HBM) for value in (w, x, a_t, b, dy)],
        scratch=[
            pltpu.VMEM((toks + rank, rows), BF16),
            pltpu.VMEM((rank, cols), BF16),
            pltpu.VMEM((toks, cols), BF16),
            pltpu.VMEM((toks + rank, cols), F32),
            pltpu.VMEM((8, cols), F32),
            dma((steps,)), dma, dma, dma, dma,
        ],
        vmem=32,
        flops=2 * rows * cols * (toks + 2 * rank),
        data=rows * cols * 2,
    )


def q_kernel(a_ref, x_ref, dy_ref, bq_ref):
    bq_ref[...] = fold(nn(hi_lo(nt(a_ref[...], x_ref[...])), dy_ref[...]))


def block(m_ref, index, half=None, count=4):
    size = m_ref.shape[0] // count
    start = lax.rem(index + count, count) * size
    if half is not None:
        size //= 2
        start += half * size
    return m_ref[pl.ds(pl.multiple_of(start, 64), size)]


def far_kernel(stat_ref, r1_ref, r2_ref, r3_ref, mag_ref, dy_ref, m_ref, vec_ref, scaled_ref, h0_ref, h1_ref):
    total = (stat_ref[...] + r2_ref[...]) + (r1_ref[...] + r3_ref[...])
    squares = total[0:1] + EPS
    norms = jnp.sqrt(squares)
    scale = mag_ref[...] / norms
    vec_ref[...] = jnp.concatenate([squares, norms, scale, total[1:2]], axis=0)
    scaled = (dy_ref[...].astype(F32) * scale).astype(BF16)
    scaled_ref[...] = scaled
    y = lax.axis_index("cols")
    h0_ref[...] = nt(block(m_ref, y + 2, 0), scaled)
    h1_ref[...] = nt(block(m_ref, y + 2, 1), scaled)


def near_kernel(m_ref, scaled_ref, up_ref, down_ref):
    y = lax.axis_index("cols")
    up_ref[...] = nt(block(m_ref, y + 1, 1), scaled_ref[...])
    down_ref[...] = nt(block(m_ref, y - 1, 0), scaled_ref[...])


def relay_kernel(m_ref, scaled_ref, u0_ref, u1_ref, up_ref, down_ref):
    y = lax.axis_index("cols")
    up_ref[...] = u0_ref[...] + nt(block(m_ref, y + 1, 0), scaled_ref[...])
    down_ref[...] = u1_ref[...] + nt(block(m_ref, y - 1, 1), scaled_ref[...])


def own_kernel(m_ref, scaled_ref, own_ref):
    own_ref[...] = nt(block(m_ref, lax.axis_index("cols")), scaled_ref[...])


def gather_kernel(own_ref, v0_ref, v1_ref, sum_ref):
    half = own_ref.shape[0] // 2
    sum_ref[:half] = own_ref[:half] + v1_ref[...]
    sum_ref[half:] = own_ref[half:] + v0_ref[...]


def finish_kernel(own_ref, w0_ref, w1_ref, out_ref, done_ref):
    done_ref[...] = jnp.zeros_like(done_ref)
    half = own_ref.shape[0] // 2
    out_ref[:half] = (own_ref[:half] + w0_ref[...]).astype(BF16)
    out_ref[half:] = (own_ref[half:] + w1_ref[...]).astype(BF16)


def a_kernel(factor, vec_ref, dy_ref, b_ref, x_ref, m_ref, *refs):
    outs, whole = refs[:-1], refs[-1]
    scale = vec_ref[2:3] * factor
    wide = b_ref[...].astype(F32) * scale
    p_t = fold(nt(hi_lo(wide), dy_ref[...]))
    left = hi_lo(p_t)
    right = hi_lo(wide * (vec_ref[3:4] / vec_ref[0:1]))
    rows = m_ref.shape[0]
    tile = 512
    for r in range(rows // tile):
        at = slice(r * tile, (r + 1) * tile)
        whole[:, at] = fold(nn(left, x_ref[:, at]) - nt(right, m_ref[at]))
    split(whole, outs, lax.axis_index("dp"), 1)


def split(whole, outs, index, axis):
    count = len(outs)
    size = whole.shape[axis] // count
    for k, ref in enumerate(outs):
        at = pl.ds(pl.multiple_of(lax.rem(index + k, count) * size, 128 if axis else 8), size)
        ref[...] = whole[:, at] if axis else whole[at]


def sum_kernel(*refs):
    refs[-1][...] = functools.reduce(jnp.add, [ref[...] for ref in refs[:-1]])


def add(*ins, after=()):
    return call(sum_kernel, [out(ins[0].shape)], [VMEM] * len(ins), *ins, after=after)[0]


def halve_kernel(position, left_ref, right_ref, keep_ref, send_ref, whole):
    whole[...] = left_ref[...] + right_ref[...]
    split(whole, [keep_ref, send_ref], position(), 0)


def halve(left, right, position, after=()):
    rows, cols = left.shape
    return call(
        functools.partial(halve_kernel, position),
        [out((rows // 2, cols))] * 2,
        [VMEM] * 2,
        left, right,
        scratch=[pltpu.VMEM((rows, cols), F32)],
        after=after,
    )


def join_kernel(position, axis, *refs):
    ins, whole = refs[:-1], refs[-1]
    count = len(ins)
    size = ins[0].shape[axis]
    for k, ref in enumerate(ins):
        start = lax.rem(position() + count - k, count) * size
        at = pl.ds(pl.multiple_of(start, 128 if axis else 8), size)
        if axis:
            whole[:, at] = ref[...]
        else:
            whole[at] = ref[...]


def join(ins, position, axis, after=()):
    shape = list(ins[0].shape)
    shape[axis] *= len(ins)
    return call(
        functools.partial(join_kernel, position, axis),
        [out(tuple(shape))],
        [VMEM] * len(ins),
        *ins,
        after=after,
    )[0]


def b_kernel(factor, vec_ref, bq_ref, am_ref, keep_ref, send_ref, whole):
    ratio = vec_ref[3:4] / vec_ref[0:1]
    whole[...] = (vec_ref[2:3] * factor) * (bq_ref[...] - ratio * am_ref[...])
    split(whole, [keep_ref, send_ref], core_bit(), 0)


def add_halves_kernel(left_ref, right_ref, top_ref, bottom_ref):
    half = top_ref.shape[0]
    top_ref[...] = left_ref[:half] + right_ref[:half]
    bottom_ref[...] = left_ref[half:] + right_ref[half:]


def pair_kernel(top_ref, top_more_ref, bottom_ref, bottom_more_ref, top_out_ref, bottom_out_ref):
    half = top_ref.shape[0]
    top_out_ref[:half] = top_ref[...]
    top_out_ref[half:] = top_more_ref[...]
    bottom_out_ref[:half] = bottom_ref[...]
    bottom_out_ref[half:] = bottom_more_ref[...]


def a_join_kernel(top_ref, top_more_ref, bottom_ref, bottom_more_ref, whole):
    z = dp_index()
    first = z + 1 - 2 * lax.rem(z, 2)
    second = 3 - z
    half, size = top_ref.shape[0] // 2, top_ref.shape[1]
    for row, ref, near, far in (
        (0, top_ref, z, second),
        (0, top_more_ref, first, 3 - first),
        (half, bottom_ref, z, first),
        (half, bottom_more_ref, second, 3 - first),
    ):
        whole[row:row + half, pl.ds(pl.multiple_of(near * size, 128), size)] = ref[:half]
        whole[row:row + half, pl.ds(pl.multiple_of(far * size, 128), size)] = ref[half:]


def b_stack_kernel(left_ref, right_ref, vec_ref, out_ref):
    rows = left_ref.shape[0]
    out_ref[:rows] = left_ref[...] + right_ref[...]
    out_ref[rows:] = jnp.broadcast_to(vec_ref[3:4], left_ref.shape)


def b_unstack_kernel(factor, left_ref, right_ref, vec_ref, b_ref, mag_ref):
    rows = b_ref.shape[0]
    total = left_ref[...] + right_ref[...]
    b_ref[...] = total[:rows]
    mag_ref[...] = factor * total[rows:rows + 1] / vec_ref[1:2]


def core_bit():
    return lax.rem(lax.axis_index("rows"), 2)


def near_bit():
    return lax.rem(lax.div(lax.div(lax.axis_index("rows"), 2) + 1, 2), 2)


def far_bit():
    return lax.div(lax.axis_index("rows"), 4)


def dp_index():
    return lax.axis_index("dp")


def ring(value, axis, k, count=4):
    return lax.ppermute(value, axis, [(i, (i + k) % count) for i in range(count)])


def ring_x(value, k, count=8):
    return lax.ppermute(value, "rows", [(i, (i + 2 * k) % count) for i in range(count)])


def swap(value, axis, step):
    return lax.ppermute(value, axis, [(i, i ^ 1 if step == 0 else 3 - i) for i in range(4)])


def swap_x(value, step):
    return lax.ppermute(value, "rows", [(i, i ^ 2 if step == 0 else 6 - 2 * (i // 2) + i % 2) for i in range(8)])


def swap_core(value, count=8):
    return lax.ppermute(value, "rows", [(i, i ^ 1) for i in range(count)])


def shards(x, dy, w, a, b, mag):
    rows, cols = w.shape
    toks, rank = x.shape[0], a.shape[1]
    groups, full_rows = 4, rows * 8
    gamma = float(toks * groups) ** (-0.5)
    mag = mag.reshape(1, cols)
    m, stat, am = merge(w, x, a.T, b, dy)
    bq = call(q_kernel, [out((rank, cols))], [VMEM] * 3, a.T, x, dy, after=[stat])[0]

    m = pltpu.with_memory_space_constraint(m, pltpu.VMEM)
    stat = stat + swap_core(stat)
    far = rows // 8
    vec, scaled, h0, h1 = call(
        far_kernel,
        [out((4, cols)), out((toks, cols), BF16), out((far, toks)), out((far, toks))],
        [VMEM] * 7,
        stat, ring_x(stat, 1), ring_x(stat, 2), ring_x(stat, 3), mag, dy, m,
        after=[bq],
    )
    u0, u1 = ring(h0, "cols", 1), ring(h1, "cols", 3)
    keep, send = call(
        functools.partial(b_kernel, 2.0 * gamma),
        [out((rank // 2, cols))] * 2,
        [VMEM] * 3,
        vec, bq, am,
        scratch=[pltpu.VMEM((rank, cols), F32)],
    )
    half = [out((far, toks))] * 2
    up, down = call(near_kernel, half, [VMEM] * 2, m, scaled, after=[send])
    v0, v1 = ring(up, "cols", 1), ring(down, "cols", 3)
    keep, send = halve(keep, swap_core(send), near_bit, after=[up])
    pieces = call(
        functools.partial(a_kernel, 2.0 * gamma),
        [out((rank, rows // 4))] * 4,
        [VMEM] * 5,
        vec, dy, b, x, m,
        scratch=[pltpu.VMEM((rank, rows), F32)],
        after=[send],
    )
    keep, send = halve(keep, swap_x(send, 0), far_bit, after=[pieces[0]])
    pieces = [pieces[0]] + [ring(pieces[k], "dp", k) for k in (2, 1, 3)]
    own = call(own_kernel, [out((rows // 4, toks))], [VMEM] * 2, m, scaled, after=[send, u0, u1])[0]
    up, down = call(relay_kernel, half, [VMEM] * 4, m, scaled, u0, u1, after=[own])
    own = call(gather_kernel, [out((rows // 4, toks))], [VMEM] * 3, own, v0, v1, after=[up])[0]

    piece = add(*pieces, after=[own])
    stack = call(
        b_stack_kernel, [out((rank // 4, cols))], [VMEM] * 3, keep, swap_x(send, 1), vec, after=[piece]
    )[0]
    piece = add(piece, swap(piece, "cols", 0), after=[stack])
    last = (piece, swap(piece, "cols", 1))
    stack = add(stack, swap(stack, "dp", 0), after=[piece])
    up, down = hold([up, down], [stack])
    w0, w1 = ring(up, "cols", 1), ring(down, "cols", 3)
    piece = [out((rank // 2, rows // 4))] * 2
    top, bottom = call(add_halves_kernel, piece, [VMEM] * 2, *last, after=[up])
    b_part, mag_grad = call(
        functools.partial(b_unstack_kernel, gamma / float(full_rows) ** 0.5),
        [out((rank // 8, cols)), out((1, cols))],
        [VMEM] * 3,
        stack, swap(stack, "dp", 1), vec,
        after=[top],
    )
    b_part = join([b_part, swap_x(b_part, 1)], far_bit, 0)
    top, bottom = call(
        pair_kernel,
        [out((rank, rows // 4))] * 2,
        [VMEM] * 4,
        top, swap(top, "dp", 1), bottom, swap(bottom, "dp", 0),
        after=[b_part],
    )
    grad, done = call(
        finish_kernel, [out((rows // 4, toks), BF16), out((8, 128))], [VMEM] * 3, own, w0, w1, after=[top]
    )
    top_more, bottom_more = hold([swap(top, "dp", 0), swap(bottom, "dp", 1)], [done])
    b_part = join([b_part, swap_x(b_part, 0)], near_bit, 0, after=[top_more])
    a_grad = call(a_join_kernel, [out((rank, rows))], [VMEM] * 4, top, top_more, bottom, bottom_more, after=[b_part])[0]
    b_grad = join([b_part, swap_core(b_part)], core_bit, 0)
    return grad, a_grad.T, b_grad, mag_grad.reshape(cols)


def solution(mesh):
    return jax.shard_map(
        shards,
        mesh=mesh,
        in_specs=(
            P("dp", "rows"),
            P("dp", "cols"),
            P("rows", "cols"),
            P("rows", None),
            P(None, "cols"),
            P("cols"),
        ),
        out_specs=(P(("rows", "cols"), "dp"), P("rows", None), P(None, "cols"), P("cols")),
        check_vma=False,
    )
```

```python
import functools

import jax
import jax.numpy as jnp
from jax import lax
from jax.experimental import pallas as pl
from jax.experimental.pallas import tpu as pltpu
from jax.sharding import PartitionSpec as P

EPS = 1e-06
F32 = jnp.float32
BF16 = jnp.bfloat16
MIB = 1024 * 1024

ANY = pl.BlockSpec(memory_space=pl.ANY)
VMEM = pl.BlockSpec(memory_space=pltpu.VMEM)
HBM = pl.BlockSpec(memory_space=pltpu.HBM)


def nn(a, b):
    return lax.dot_general(a, b, (((1,), (0,)), ((), ())), preferred_element_type=F32)


def nt(a, b):
    return lax.dot_general(a, b, (((1,), (1,)), ((), ())), preferred_element_type=F32)


def tn(a, b):
    return lax.dot_general(a, b, (((0,), (0,)), ((), ())), preferred_element_type=F32)


def hi_lo(value):
    hi = value.astype(BF16)
    lo = (value - hi.astype(F32)).astype(BF16)
    return jnp.concatenate([hi, lo], axis=0)


def fold(value):
    half = value.shape[0] // 2
    return value[:half] + value[half:]


def call(kernel, outs, specs, *args, scratch=(), vmem=16, flops=1, data=1, after=()):
    used = len(args)

    def body(*refs):
        kernel(*refs[:used], *refs[used + len(after):])

    return pl.pallas_call(
        body,
        out_shape=outs,
        in_specs=list(specs) + [ANY] * len(after),
        out_specs=[VMEM for _ in outs],
        scratch_shapes=list(scratch),
        compiler_params=pltpu.CompilerParams(vmem_limit_bytes=vmem * MIB),
        cost_estimate=pl.CostEstimate(flops=flops, bytes_accessed=data, transcendentals=0),
    )(*args, *after)


def hold(values, after):
    count = len(values)
    return pl.pallas_call(
        lambda *refs: None,
        out_shape=[out(value.shape, value.dtype) for value in values],
        in_specs=[ANY] * (count + len(after)),
        out_specs=[ANY] * count,
        input_output_aliases={k: k for k in range(count)},
        compiler_params=pltpu.CompilerParams(vmem_limit_bytes=MIB),
    )(*values, *after)


def out(shape, dtype=F32):
    return jax.ShapeDtypeStruct(shape, dtype)


def merge_kernel(
    steps, w_ref, x_ref, a_ref, b_ref, dy_ref, m_ref, stat_ref, am_ref,
    xa, b2, dy, acc, sq, w_sem, x_sem, a_sem, b_sem, dy_sem,
):
    rows, cols = w_ref.shape
    toks = x_ref.shape[0]
    step = rows // steps
    tile = 2048
    b_copy = pltpu.make_async_copy(b_ref, b2, b_sem)
    dy_copy = pltpu.make_async_copy(dy_ref, dy, dy_sem)
    a_copy = pltpu.make_async_copy(a_ref, xa.at[toks:], a_sem)

    def w_copy(i):
        part = pl.ds(pl.multiple_of(i * step, step), step)
        return pltpu.make_async_copy(w_ref.at[part], m_ref.at[part], w_sem.at[i])

    x_copy = pltpu.make_async_copy(x_ref, xa.at[:toks], x_sem)
    b_copy.start()
    a_copy.start()
    w_copy(0).start()
    x_copy.start()
    for i in range(1, steps):
        w_copy(i).start()
    dy_copy.start()
    acc[...] = jnp.zeros_like(acc)
    sq[...] = jnp.zeros_like(sq)
    b_copy.wait()
    a_copy.wait()
    x_copy.wait()
    b2[...] = b2[...] + b2[...]

    @pl.loop(0, steps)
    def _(i):
        w_copy(i).wait()
        part = pl.ds(pl.multiple_of(i * step, step), step)
        xa_part = xa[:, part]
        a_part = xa_part[toks:]
        for c in range(cols // tile):
            at = slice(c * tile, (c + 1) * tile)
            m = (m_ref[part, at].astype(F32) + tn(a_part, b2[:, at])).astype(BF16)
            m_ref[part, at] = m
            wide = m.astype(F32)
            sq[:, at] += jnp.sum((wide * wide).reshape(step // 8, 8, tile), axis=0)
            acc[:, at] += nn(xa_part, m)

    dy_copy.wait()
    am_ref[...] = acc[toks:]
    stat_ref[0:1] = jnp.sum(sq[...], axis=0, keepdims=True)
    stat_ref[1:2] = jnp.sum(acc[:toks] * dy[...].astype(F32), axis=0, keepdims=True)


def merge(w, x, a_t, b, dy):
    rows, cols = w.shape
    toks = x.shape[0]
    rank = b.shape[0]
    steps = rows // 512
    dma = pltpu.SemaphoreType.DMA
    return call(
        functools.partial(merge_kernel, steps),
        [pltpu.VMEM((rows, cols), BF16), out((2, cols)), out((rank, cols))],
        [HBM] * 5,
        *[pltpu.with_memory_space_constraint(value, pltpu.HBM) for value in (w, x, a_t, b, dy)],
        scratch=[
            pltpu.VMEM((toks + rank, rows), BF16),
            pltpu.VMEM((rank, cols), BF16),
            pltpu.VMEM((toks, cols), BF16),
            pltpu.VMEM((toks + rank, cols), F32),
            pltpu.VMEM((8, cols), F32),
            dma((steps,)), dma, dma, dma, dma,
        ],
        vmem=32,
        flops=2 * rows * cols * (toks + 2 * rank),
        data=rows * cols * 2,
    )


def q_kernel(a_ref, x_ref, dy_ref, bq_ref):
    bq_ref[...] = fold(nn(hi_lo(nt(a_ref[...], x_ref[...])), dy_ref[...]))


def block(m_ref, index, half=None, count=4):
    size = m_ref.shape[0] // count
    start = lax.rem(index + count, count) * size
    if half is not None:
        size //= 2
        start += half * size
    return m_ref[pl.ds(pl.multiple_of(start, 64), size)]


def far_kernel(*refs):
    stats, (mag_ref, dy_ref, m_ref, vec_ref, scaled_ref, h0_ref, h1_ref) = refs[:8], refs[8:]
    chips = [stats[k][...] + stats[k + 4][...] for k in range(4)]
    total = (chips[0] + chips[2]) + (chips[1] + chips[3])
    squares = total[0:1] + EPS
    norms = jnp.sqrt(squares)
    scale = mag_ref[...] / norms
    vec_ref[...] = jnp.concatenate([squares, norms, scale, total[1:2]], axis=0)
    scaled = (dy_ref[...].astype(F32) * scale).astype(BF16)
    scaled_ref[...] = scaled
    y = lax.axis_index("cols")
    h0_ref[...] = nt(block(m_ref, y + 2, 0), scaled)
    h1_ref[...] = nt(block(m_ref, y + 2, 1), scaled)


def near_kernel(m_ref, scaled_ref, up_ref, down_ref):
    y = lax.axis_index("cols")
    up_ref[...] = nt(block(m_ref, y + 1, 1), scaled_ref[...])
    down_ref[...] = nt(block(m_ref, y - 1, 0), scaled_ref[...])


def relay_kernel(m_ref, scaled_ref, u0_ref, u1_ref, up_ref, down_ref):
    y = lax.axis_index("cols")
    up_ref[...] = u0_ref[...] + nt(block(m_ref, y + 1, 0), scaled_ref[...])
    down_ref[...] = u1_ref[...] + nt(block(m_ref, y - 1, 1), scaled_ref[...])


def own_kernel(m_ref, scaled_ref, own_ref):
    own_ref[...] = nt(block(m_ref, lax.axis_index("cols")), scaled_ref[...])


def gather_kernel(own_ref, v0_ref, v1_ref, sum_ref):
    half = own_ref.shape[0] // 2
    sum_ref[:half] = own_ref[:half] + v1_ref[...]
    sum_ref[half:] = own_ref[half:] + v0_ref[...]


def finish_kernel(own_ref, w0_ref, w1_ref, out_ref, done_ref):
    done_ref[...] = jnp.zeros_like(done_ref)
    half = own_ref.shape[0] // 2
    out_ref[:half] = (own_ref[:half] + w0_ref[...]).astype(BF16)
    out_ref[half:] = (own_ref[half:] + w1_ref[...]).astype(BF16)


def a_kernel(factor, vec_ref, dy_ref, b_ref, x_ref, m_ref, *refs):
    outs, whole = refs[:-1], refs[-1]
    scale = vec_ref[2:3] * factor
    wide = b_ref[...].astype(F32) * scale
    p_t = fold(nt(hi_lo(wide), dy_ref[...]))
    left = hi_lo(p_t)
    right = hi_lo(wide * (vec_ref[3:4] / vec_ref[0:1]))
    rows = m_ref.shape[0]
    tile = 512
    for r in range(rows // tile):
        at = slice(r * tile, (r + 1) * tile)
        whole[:, at] = fold(nn(left, x_ref[:, at]) - nt(right, m_ref[at]))
    split(whole, outs, lax.axis_index("dp"), 1)


def split(whole, outs, index, axis):
    count = len(outs)
    size = whole.shape[axis] // count
    for k, ref in enumerate(outs):
        at = pl.ds(pl.multiple_of(lax.rem(index + k, count) * size, 128 if axis else 8), size)
        ref[...] = whole[:, at] if axis else whole[at]


def sum_kernel(*refs):
    refs[-1][...] = functools.reduce(jnp.add, [ref[...] for ref in refs[:-1]])


def add(*ins, after=()):
    return call(sum_kernel, [out(ins[0].shape)], [VMEM] * len(ins), *ins, after=after)[0]


def halve_kernel(position, left_ref, right_ref, keep_ref, send_ref, whole):
    whole[...] = left_ref[...] + right_ref[...]
    split(whole, [keep_ref, send_ref], position(), 0)


def halve(left, right, position, after=()):
    rows, cols = left.shape
    return call(
        functools.partial(halve_kernel, position),
        [out((rows // 2, cols))] * 2,
        [VMEM] * 2,
        left, right,
        scratch=[pltpu.VMEM((rows, cols), F32)],
        after=after,
    )


def join_kernel(position, axis, *refs):
    ins, whole = refs[:-1], refs[-1]
    count = len(ins)
    size = ins[0].shape[axis]
    for k, ref in enumerate(ins):
        start = lax.rem(position() + count - k, count) * size
        at = pl.ds(pl.multiple_of(start, 128 if axis else 8), size)
        if axis:
            whole[:, at] = ref[...]
        else:
            whole[at] = ref[...]


def join(ins, position, axis, after=()):
    shape = list(ins[0].shape)
    shape[axis] *= len(ins)
    return call(
        functools.partial(join_kernel, position, axis),
        [out(tuple(shape))],
        [VMEM] * len(ins),
        *ins,
        after=after,
    )[0]


def b_kernel(factor, vec_ref, bq_ref, am_ref, keep_ref, send_ref, whole):
    ratio = vec_ref[3:4] / vec_ref[0:1]
    whole[...] = (vec_ref[2:3] * factor) * (bq_ref[...] - ratio * am_ref[...])
    split(whole, [keep_ref, send_ref], core_bit(), 0)


def add_halves_kernel(left_ref, right_ref, top_ref, bottom_ref):
    half = top_ref.shape[0]
    top_ref[...] = left_ref[:half] + right_ref[:half]
    bottom_ref[...] = left_ref[half:] + right_ref[half:]


def pair_kernel(top_ref, top_more_ref, bottom_ref, bottom_more_ref, top_out_ref, bottom_out_ref):
    half = top_ref.shape[0]
    top_out_ref[:half] = top_ref[...]
    top_out_ref[half:] = top_more_ref[...]
    bottom_out_ref[:half] = bottom_ref[...]
    bottom_out_ref[half:] = bottom_more_ref[...]


def a_join_kernel(top_ref, top_more_ref, bottom_ref, bottom_more_ref, whole):
    z = dp_index()
    first = z + 1 - 2 * lax.rem(z, 2)
    second = 3 - z
    half, size = top_ref.shape[0] // 2, top_ref.shape[1]
    for row, ref, near, far in (
        (0, top_ref, z, second),
        (0, top_more_ref, first, 3 - first),
        (half, bottom_ref, z, first),
        (half, bottom_more_ref, second, 3 - first),
    ):
        whole[row:row + half, pl.ds(pl.multiple_of(near * size, 128), size)] = ref[:half]
        whole[row:row + half, pl.ds(pl.multiple_of(far * size, 128), size)] = ref[half:]


def b_stack_kernel(left_ref, right_ref, vec_ref, out_ref):
    rows = left_ref.shape[0]
    out_ref[:rows] = left_ref[...] + right_ref[...]
    out_ref[rows:] = jnp.broadcast_to(vec_ref[3:4], left_ref.shape)


def b_unstack_kernel(factor, left_ref, right_ref, vec_ref, b_ref, mag_ref):
    rows = b_ref.shape[0]
    total = left_ref[...] + right_ref[...]
    b_ref[...] = total[:rows]
    mag_ref[...] = factor * total[rows:rows + 1] / vec_ref[1:2]


def core_bit():
    return lax.rem(lax.axis_index("rows"), 2)


def near_bit():
    return lax.rem(lax.div(lax.div(lax.axis_index("rows"), 2) + 1, 2), 2)


def far_bit():
    return lax.div(lax.axis_index("rows"), 4)


def dp_index():
    return lax.axis_index("dp")


def ring(value, axis, k, count=4):
    return lax.ppermute(value, axis, [(i, (i + k) % count) for i in range(count)])


def ring_x(value, k, core=0, count=8):
    return lax.ppermute(value, "rows", [(i, (i + 2 * k) % count ^ core) for i in range(count)])


def swap(value, axis, step):
    return lax.ppermute(value, axis, [(i, i ^ 1 if step == 0 else 3 - i) for i in range(4)])


def swap_x(value, step):
    return lax.ppermute(value, "rows", [(i, i ^ 2 if step == 0 else 6 - 2 * (i // 2) + i % 2) for i in range(8)])


def swap_core(value, count=8):
    return lax.ppermute(value, "rows", [(i, i ^ 1) for i in range(count)])


def shards(x, dy, w, a, b, mag):
    rows, cols = w.shape
    toks, rank = x.shape[0], a.shape[1]
    groups, full_rows = 4, rows * 8
    gamma = float(toks * groups) ** (-0.5)
    mag = mag.reshape(1, cols)
    m, stat, am = merge(w, x, a.T, b, dy)
    bq = call(q_kernel, [out((rank, cols))], [VMEM] * 3, a.T, x, dy, after=[stat])[0]

    m = pltpu.with_memory_space_constraint(m, pltpu.VMEM)
    stats = [stat] + [ring_x(stat, k) for k in (1, 2, 3)] + [ring_x(stat, k, 1) for k in range(4)]
    far = rows // 8
    vec, scaled, h0, h1 = call(
        far_kernel,
        [out((4, cols)), out((toks, cols), BF16), out((far, toks)), out((far, toks))],
        [VMEM] * 11,
        *stats, mag, dy, m,
        after=[bq],
    )
    u0, u1 = ring(h0, "cols", 1), ring(h1, "cols", 3)
    keep, send = call(
        functools.partial(b_kernel, 2.0 * gamma),
        [out((rank // 2, cols))] * 2,
        [VMEM] * 3,
        vec, bq, am,
        scratch=[pltpu.VMEM((rank, cols), F32)],
    )
    half = [out((far, toks))] * 2
    up, down = call(near_kernel, half, [VMEM] * 2, m, scaled, after=[send])
    v0, v1 = ring(up, "cols", 1), ring(down, "cols", 3)
    keep, send = halve(keep, swap_core(send), near_bit, after=[up])
    pieces = call(
        functools.partial(a_kernel, 2.0 * gamma),
        [out((rank, rows // 4))] * 4,
        [VMEM] * 5,
        vec, dy, b, x, m,
        scratch=[pltpu.VMEM((rank, rows), F32)],
        after=[send],
    )
    keep, send = halve(keep, swap_x(send, 0), far_bit, after=[pieces[0]])
    pieces = [pieces[0]] + [ring(pieces[k], "dp", k) for k in (2, 1, 3)]
    own = call(own_kernel, [out((rows // 4, toks))], [VMEM] * 2, m, scaled, after=[send, u0, u1])[0]
    up, down = call(relay_kernel, half, [VMEM] * 4, m, scaled, u0, u1, after=[own])
    own = call(gather_kernel, [out((rows // 4, toks))], [VMEM] * 3, own, v0, v1, after=[up])[0]

    piece = add(*pieces, after=[own])
    stack = call(
        b_stack_kernel, [out((rank // 4, cols))], [VMEM] * 3, keep, swap_x(send, 1), vec, after=[piece]
    )[0]
    piece = add(piece, swap(piece, "cols", 0), after=[stack])
    last = (piece, swap(piece, "cols", 1))
    stack = add(stack, swap(stack, "dp", 0), after=[piece])
    up, down = hold([up, down], [stack])
    w0, w1 = ring(up, "cols", 1), ring(down, "cols", 3)
    piece = [out((rank // 2, rows // 4))] * 2
    top, bottom = call(add_halves_kernel, piece, [VMEM] * 2, *last, after=[up])
    b_part, mag_grad = call(
        functools.partial(b_unstack_kernel, gamma / float(full_rows) ** 0.5),
        [out((rank // 8, cols)), out((1, cols))],
        [VMEM] * 3,
        stack, swap(stack, "dp", 1), vec,
        after=[top],
    )
    b_part = join([b_part, swap_x(b_part, 1)], far_bit, 0)
    top, bottom = call(
        pair_kernel,
        [out((rank, rows // 4))] * 2,
        [VMEM] * 4,
        top, swap(top, "dp", 1), bottom, swap(bottom, "dp", 0),
        after=[b_part],
    )
    grad, done = call(
        finish_kernel, [out((rows // 4, toks), BF16), out((8, 128))], [VMEM] * 3, own, w0, w1, after=[top]
    )
    top_more, bottom_more = hold([swap(top, "dp", 0), swap(bottom, "dp", 1)], [done])
    b_part = join([b_part, swap_x(b_part, 0)], near_bit, 0, after=[top_more])
    a_grad = call(a_join_kernel, [out((rank, rows))], [VMEM] * 4, top, top_more, bottom, bottom_more, after=[b_part])[0]
    b_grad = join([b_part, swap_core(b_part)], core_bit, 0)
    return grad, a_grad.T, b_grad, mag_grad.reshape(cols)


def solution(mesh):
    return jax.shard_map(
        shards,
        mesh=mesh,
        in_specs=(
            P("dp", "rows"),
            P("dp", "cols"),
            P("rows", "cols"),
            P("rows", None),
            P(None, "cols"),
            P("cols"),
        ),
        out_specs=(P(("rows", "cols"), "dp"), P("rows", None), P(None, "cols"), P("cols")),
        check_vma=False,
    )
```

```python
import functools

import jax
import jax.numpy as jnp
from jax import lax
from jax.experimental import pallas as pl
from jax.experimental.pallas import tpu as pltpu
from jax.sharding import PartitionSpec as P

EPS = 1e-06
F32 = jnp.float32
BF16 = jnp.bfloat16
MIB = 1024 * 1024

ANY = pl.BlockSpec(memory_space=pl.ANY)
VMEM = pl.BlockSpec(memory_space=pltpu.VMEM)
HBM = pl.BlockSpec(memory_space=pltpu.HBM)


def nn(a, b):
    return lax.dot_general(a, b, (((1,), (0,)), ((), ())), preferred_element_type=F32)


def nt(a, b):
    return lax.dot_general(a, b, (((1,), (1,)), ((), ())), preferred_element_type=F32)


def tn(a, b):
    return lax.dot_general(a, b, (((0,), (0,)), ((), ())), preferred_element_type=F32)


def hi_lo(value):
    hi = value.astype(BF16)
    lo = (value - hi.astype(F32)).astype(BF16)
    return jnp.concatenate([hi, lo], axis=0)


def fold(value):
    half = value.shape[0] // 2
    return value[:half] + value[half:]


def call(kernel, outs, specs, *args, scratch=(), vmem=16, flops=1, data=1, after=()):
    used = len(args)

    def body(*refs):
        kernel(*refs[:used], *refs[used + len(after):])

    return pl.pallas_call(
        body,
        out_shape=outs,
        in_specs=list(specs) + [ANY] * len(after),
        out_specs=[VMEM for _ in outs],
        scratch_shapes=list(scratch),
        compiler_params=pltpu.CompilerParams(vmem_limit_bytes=vmem * MIB),
        cost_estimate=pl.CostEstimate(flops=flops, bytes_accessed=data, transcendentals=0),
    )(*args, *after)


def hold(values, after):
    count = len(values)
    return pl.pallas_call(
        lambda *refs: None,
        out_shape=[out(value.shape, value.dtype) for value in values],
        in_specs=[ANY] * (count + len(after)),
        out_specs=[ANY] * count,
        input_output_aliases={k: k for k in range(count)},
        compiler_params=pltpu.CompilerParams(vmem_limit_bytes=MIB),
    )(*values, *after)


def out(shape, dtype=F32):
    return jax.ShapeDtypeStruct(shape, dtype)


def merge_kernel(
    steps, w_ref, x_ref, a_ref, b_ref, dy_ref, m_ref, stat_ref, am_ref,
    xa, b2, dy, acc, sq, w_sem, x_sem, a_sem, b_sem, dy_sem,
):
    rows, cols = w_ref.shape
    toks = x_ref.shape[0]
    step = rows // steps
    tile = 2048
    b_copy = pltpu.make_async_copy(b_ref, b2, b_sem)
    dy_copy = pltpu.make_async_copy(dy_ref, dy, dy_sem)
    a_copy = pltpu.make_async_copy(a_ref, xa.at[toks:], a_sem)

    def w_copy(i):
        part = pl.ds(pl.multiple_of(i * step, step), step)
        return pltpu.make_async_copy(w_ref.at[part], m_ref.at[part], w_sem.at[i])

    x_copy = pltpu.make_async_copy(x_ref, xa.at[:toks], x_sem)
    b_copy.start()
    a_copy.start()
    w_copy(0).start()
    x_copy.start()
    for i in range(1, steps):
        w_copy(i).start()
    dy_copy.start()
    acc[...] = jnp.zeros_like(acc)
    sq[...] = jnp.zeros_like(sq)
    b_copy.wait()
    a_copy.wait()
    x_copy.wait()
    b2[...] = b2[...] + b2[...]

    @pl.loop(0, steps)
    def _(i):
        w_copy(i).wait()
        part = pl.ds(pl.multiple_of(i * step, step), step)
        xa_part = xa[:, part]
        a_part = xa_part[toks:]
        for c in range(cols // tile):
            at = slice(c * tile, (c + 1) * tile)
            m = (m_ref[part, at].astype(F32) + tn(a_part, b2[:, at])).astype(BF16)
            m_ref[part, at] = m
            wide = m.astype(F32)
            sq[:, at] += jnp.sum((wide * wide).reshape(step // 8, 8, tile), axis=0)
            acc[:, at] += nn(xa_part, m)

    dy_copy.wait()
    am_ref[...] = acc[toks:]
    stat_ref[0:1] = jnp.sum(sq[...], axis=0, keepdims=True)
    stat_ref[1:2] = jnp.sum(acc[:toks] * dy[...].astype(F32), axis=0, keepdims=True)


def merge(w, x, a_t, b, dy):
    rows, cols = w.shape
    toks = x.shape[0]
    rank = b.shape[0]
    steps = rows // 512
    dma = pltpu.SemaphoreType.DMA
    return call(
        functools.partial(merge_kernel, steps),
        [pltpu.VMEM((rows, cols), BF16), out((2, cols)), out((rank, cols))],
        [HBM] * 5,
        *[pltpu.with_memory_space_constraint(value, pltpu.HBM) for value in (w, x, a_t, b, dy)],
        scratch=[
            pltpu.VMEM((toks + rank, rows), BF16),
            pltpu.VMEM((rank, cols), BF16),
            pltpu.VMEM((toks, cols), BF16),
            pltpu.VMEM((toks + rank, cols), F32),
            pltpu.VMEM((8, cols), F32),
            dma((steps,)), dma, dma, dma, dma,
        ],
        vmem=32,
        flops=2 * rows * cols * (toks + 2 * rank),
        data=rows * cols * 2,
    )


def q_kernel(a_ref, x_ref, dy_ref, bq_ref):
    bq_ref[...] = fold(nn(hi_lo(nt(a_ref[...], x_ref[...])), dy_ref[...]))


def block(m_ref, index, half=None, count=4):
    size = m_ref.shape[0] // count
    start = lax.rem(index + count, count) * size
    if half is not None:
        size //= 2
        start += half * size
    return m_ref[pl.ds(pl.multiple_of(start, 64), size)]


def far_kernel(stat_ref, r1_ref, r2_ref, r3_ref, mag_ref, dy_ref, m_ref, vec_ref, scaled_ref, h0_ref, h1_ref):
    total = (stat_ref[...] + r2_ref[...]) + (r1_ref[...] + r3_ref[...])
    squares = total[0:1] + EPS
    norms = jnp.sqrt(squares)
    scale = mag_ref[...] / norms
    vec_ref[...] = jnp.concatenate([squares, norms, scale, total[1:2]], axis=0)
    scaled = (dy_ref[...].astype(F32) * scale).astype(BF16)
    scaled_ref[...] = scaled
    y = lax.axis_index("cols")
    h0_ref[...] = nt(block(m_ref, y + 2, 0), scaled)
    h1_ref[...] = nt(block(m_ref, y + 2, 1), scaled)


def near_kernel(m_ref, scaled_ref, up_ref, down_ref):
    y = lax.axis_index("cols")
    up_ref[...] = nt(block(m_ref, y + 1, 1), scaled_ref[...])
    down_ref[...] = nt(block(m_ref, y - 1, 0), scaled_ref[...])


def relay_kernel(m_ref, scaled_ref, u0_ref, u1_ref, up_ref, down_ref):
    y = lax.axis_index("cols")
    up_ref[...] = u0_ref[...] + nt(block(m_ref, y + 1, 0), scaled_ref[...])
    down_ref[...] = u1_ref[...] + nt(block(m_ref, y - 1, 1), scaled_ref[...])


def own_kernel(m_ref, scaled_ref, own_ref):
    own_ref[...] = nt(block(m_ref, lax.axis_index("cols")), scaled_ref[...])


def gather_kernel(own_ref, v0_ref, v1_ref, sum_ref):
    half = own_ref.shape[0] // 2
    sum_ref[:half] = own_ref[:half] + v1_ref[...]
    sum_ref[half:] = own_ref[half:] + v0_ref[...]


def finish_kernel(own_ref, w0_ref, w1_ref, out_ref, done_ref):
    done_ref[...] = jnp.zeros_like(done_ref)
    half = own_ref.shape[0] // 2
    out_ref[:half] = (own_ref[:half] + w0_ref[...]).astype(BF16)
    out_ref[half:] = (own_ref[half:] + w1_ref[...]).astype(BF16)


def a_kernel(factor, vec_ref, dy_ref, b_ref, x_ref, m_ref, *refs):
    outs, whole = refs[:-1], refs[-1]
    scale = vec_ref[2:3] * factor
    wide = b_ref[...].astype(F32) * scale
    p_t = fold(nt(hi_lo(wide), dy_ref[...]))
    left = hi_lo(p_t)
    right = hi_lo(wide * (vec_ref[3:4] / vec_ref[0:1]))
    rows = m_ref.shape[0]
    tile = 512
    for r in range(rows // tile):
        at = slice(r * tile, (r + 1) * tile)
        whole[:, at] = fold(nn(left, x_ref[:, at]) - nt(right, m_ref[at]))
    split(whole, outs, lax.axis_index("dp"), 1)


def split(whole, outs, index, axis):
    count = len(outs)
    size = whole.shape[axis] // count
    for k, ref in enumerate(outs):
        at = pl.ds(pl.multiple_of(lax.rem(index + k, count) * size, 128 if axis else 8), size)
        ref[...] = whole[:, at] if axis else whole[at]


def sum_kernel(*refs):
    refs[-1][...] = functools.reduce(jnp.add, [ref[...] for ref in refs[:-1]])


def add(*ins, after=()):
    return call(sum_kernel, [out(ins[0].shape)], [VMEM] * len(ins), *ins, after=after)[0]


def halve_kernel(position, left_ref, right_ref, keep_ref, send_ref, whole):
    whole[...] = left_ref[...] + right_ref[...]
    split(whole, [keep_ref, send_ref], position(), 0)


def halve(left, right, position, after=()):
    rows, cols = left.shape
    return call(
        functools.partial(halve_kernel, position),
        [out((rows // 2, cols))] * 2,
        [VMEM] * 2,
        left, right,
        scratch=[pltpu.VMEM((rows, cols), F32)],
        after=after,
    )


def join_kernel(position, axis, *refs):
    ins, whole = refs[:-1], refs[-1]
    count = len(ins)
    size = ins[0].shape[axis]
    for k, ref in enumerate(ins):
        start = lax.rem(position() + count - k, count) * size
        at = pl.ds(pl.multiple_of(start, 128 if axis else 8), size)
        if axis:
            whole[:, at] = ref[...]
        else:
            whole[at] = ref[...]


def join(ins, position, axis, after=()):
    shape = list(ins[0].shape)
    shape[axis] *= len(ins)
    return call(
        functools.partial(join_kernel, position, axis),
        [out(tuple(shape))],
        [VMEM] * len(ins),
        *ins,
        after=after,
    )[0]


def b_kernel(factor, vec_ref, bq_ref, am_ref, keep_ref, send_ref, whole):
    ratio = vec_ref[3:4] / vec_ref[0:1]
    whole[...] = (vec_ref[2:3] * factor) * (bq_ref[...] - ratio * am_ref[...])
    split(whole, [keep_ref, send_ref], core_bit(), 0)


def add_halves_kernel(left_ref, right_ref, top_ref, bottom_ref):
    half = top_ref.shape[0]
    top_ref[...] = left_ref[:half] + right_ref[:half]
    bottom_ref[...] = left_ref[half:] + right_ref[half:]


def pair_kernel(top_ref, top_more_ref, bottom_ref, bottom_more_ref, top_out_ref, bottom_out_ref):
    half = top_ref.shape[0]
    top_out_ref[:half] = top_ref[...]
    top_out_ref[half:] = top_more_ref[...]
    bottom_out_ref[:half] = bottom_ref[...]
    bottom_out_ref[half:] = bottom_more_ref[...]


def a_join_kernel(top_ref, top_more_ref, bottom_ref, bottom_more_ref, whole):
    z = dp_index()
    first = z + 1 - 2 * lax.rem(z, 2)
    second = 3 - z
    half, size = top_ref.shape[0] // 2, top_ref.shape[1]
    for row, ref, near, far in (
        (0, top_ref, z, second),
        (0, top_more_ref, first, 3 - first),
        (half, bottom_ref, z, first),
        (half, bottom_more_ref, second, 3 - first),
    ):
        whole[row:row + half, pl.ds(pl.multiple_of(near * size, 128), size)] = ref[:half]
        whole[row:row + half, pl.ds(pl.multiple_of(far * size, 128), size)] = ref[half:]


def b_stack_kernel(left_ref, right_ref, vec_ref, out_ref):
    rows = left_ref.shape[0]
    out_ref[:rows] = left_ref[...] + right_ref[...]
    out_ref[rows:] = jnp.broadcast_to(vec_ref[3:4], left_ref.shape)


def b_unstack_kernel(factor, left_ref, right_ref, vec_ref, b_ref, mag_ref):
    rows = b_ref.shape[0]
    total = left_ref[...] + right_ref[...]
    b_ref[...] = total[:rows]
    mag_ref[...] = factor * total[rows:rows + 1] / vec_ref[1:2]


def core_bit():
    return lax.rem(lax.axis_index("rows"), 2)


def near_bit():
    return lax.rem(lax.div(lax.div(lax.axis_index("rows"), 2) + 1, 2), 2)


def far_bit():
    return lax.div(lax.axis_index("rows"), 4)


def dp_index():
    return lax.axis_index("dp")


def ring(value, axis, k, count=4):
    return lax.ppermute(value, axis, [(i, (i + k) % count) for i in range(count)])


def ring_x(value, k, count=8):
    return lax.ppermute(value, "rows", [(i, (i + 2 * k) % count) for i in range(count)])


def swap(value, axis, step):
    return lax.ppermute(value, axis, [(i, i ^ 1 if step == 0 else 3 - i) for i in range(4)])


def swap_x(value, step):
    return lax.ppermute(value, "rows", [(i, i ^ 2 if step == 0 else 6 - 2 * (i // 2) + i % 2) for i in range(8)])


def swap_core(value, count=8):
    return lax.ppermute(value, "rows", [(i, i ^ 1) for i in range(count)])


def shards(x, dy, w, a, b, mag):
    rows, cols = w.shape
    toks, rank = x.shape[0], a.shape[1]
    groups, full_rows = 4, rows * 8
    gamma = float(toks * groups) ** (-0.5)
    mag = mag.reshape(1, cols)
    m, stat, am = merge(w, x, a.T, b, dy)
    bq = call(q_kernel, [out((rank, cols))], [VMEM] * 3, a.T, x, dy, after=[stat])[0]

    m = pltpu.with_memory_space_constraint(m, pltpu.VMEM)
    stat = stat + swap_core(stat)
    far = rows // 8
    vec, scaled, h0, h1 = call(
        far_kernel,
        [out((4, cols)), out((toks, cols), BF16), out((far, toks)), out((far, toks))],
        [VMEM] * 7,
        stat, ring_x(stat, 1), ring_x(stat, 2), ring_x(stat, 3), mag, dy, m,
        after=[bq],
    )
    u0, u1 = ring(h0, "cols", 1), ring(h1, "cols", 3)
    keep, send = call(
        functools.partial(b_kernel, 2.0 * gamma),
        [out((rank // 2, cols))] * 2,
        [VMEM] * 3,
        vec, bq, am,
        scratch=[pltpu.VMEM((rank, cols), F32)],
    )
    keep, send = halve(keep, swap_core(send), near_bit)
    pieces = call(
        functools.partial(a_kernel, 2.0 * gamma),
        [out((rank, rows // 4))] * 4,
        [VMEM] * 5,
        vec, dy, b, x, m,
        scratch=[pltpu.VMEM((rank, rows), F32)],
        after=[send],
    )
    keep, send = halve(keep, swap_x(send, 0), far_bit, after=[pieces[0]])
    pieces = [pieces[0]] + [ring(pieces[k], "dp", k) for k in (2, 1, 3)]
    half = [out((far, toks))] * 2
    v_up, v_down = call(near_kernel, half, [VMEM] * 2, m, scaled, after=[send])
    own = call(own_kernel, [out((rows // 4, toks))], [VMEM] * 2, m, scaled, after=[v_up])[0]
    v_up, v_down = hold([v_up, v_down], [own, u0, u1])
    v0, v1 = ring(v_up, "cols", 1), ring(v_down, "cols", 3)
    up, down = call(relay_kernel, half, [VMEM] * 4, m, scaled, u0, u1, after=[v_up])

    piece = add(*pieces, after=[up])
    stack = call(
        b_stack_kernel, [out((rank // 4, cols))], [VMEM] * 3, keep, swap_x(send, 1), vec, after=[piece]
    )[0]
    own = call(gather_kernel, [out((rows // 4, toks))], [VMEM] * 3, own, v0, v1, after=[stack])[0]
    piece = add(piece, swap(piece, "cols", 0), after=[own])
    last = (piece, swap(piece, "cols", 1))
    stack = add(stack, swap(stack, "dp", 0), after=[piece])
    up, down = hold([up, down], [stack])
    w0, w1 = ring(up, "cols", 1), ring(down, "cols", 3)
    piece = [out((rank // 2, rows // 4))] * 2
    top, bottom = call(add_halves_kernel, piece, [VMEM] * 2, *last, after=[up])
    b_part, mag_grad = call(
        functools.partial(b_unstack_kernel, gamma / float(full_rows) ** 0.5),
        [out((rank // 8, cols)), out((1, cols))],
        [VMEM] * 3,
        stack, swap(stack, "dp", 1), vec,
        after=[top],
    )
    b_part = join([b_part, swap_x(b_part, 1)], far_bit, 0)
    top, bottom = call(
        pair_kernel,
        [out((rank, rows // 4))] * 2,
        [VMEM] * 4,
        top, swap(top, "dp", 1), bottom, swap(bottom, "dp", 0),
        after=[b_part],
    )
    grad, done = call(
        finish_kernel, [out((rows // 4, toks), BF16), out((8, 128))], [VMEM] * 3, own, w0, w1, after=[top]
    )
    top_more, bottom_more = hold([swap(top, "dp", 0), swap(bottom, "dp", 1)], [done])
    b_part = join([b_part, swap_x(b_part, 0)], near_bit, 0, after=[top_more])
    a_grad = call(a_join_kernel, [out((rank, rows))], [VMEM] * 4, top, top_more, bottom, bottom_more, after=[b_part])[0]
    b_grad = join([b_part, swap_core(b_part)], core_bit, 0)
    return grad, a_grad.T, b_grad, mag_grad.reshape(cols)


def solution(mesh):
    return jax.shard_map(
        shards,
        mesh=mesh,
        in_specs=(
            P("dp", "rows"),
            P("dp", "cols"),
            P("rows", "cols"),
            P("rows", None),
            P(None, "cols"),
            P("cols"),
        ),
        out_specs=(P(("rows", "cols"), "dp"), P("rows", None), P(None, "cols"), P("cols")),
        check_vma=False,
    )
```

```python
import functools

import jax
import jax.numpy as jnp
from jax import lax
from jax.experimental import pallas as pl
from jax.experimental.pallas import tpu as pltpu
from jax.sharding import PartitionSpec as P

EPS = 1e-06
F32 = jnp.float32
BF16 = jnp.bfloat16
MIB = 1024 * 1024

ANY = pl.BlockSpec(memory_space=pl.ANY)
VMEM = pl.BlockSpec(memory_space=pltpu.VMEM)
HBM = pl.BlockSpec(memory_space=pltpu.HBM)


def nn(a, b):
    return lax.dot_general(a, b, (((1,), (0,)), ((), ())), preferred_element_type=F32)


def nt(a, b):
    return lax.dot_general(a, b, (((1,), (1,)), ((), ())), preferred_element_type=F32)


def tn(a, b):
    return lax.dot_general(a, b, (((0,), (0,)), ((), ())), preferred_element_type=F32)


def hi_lo(value):
    hi = value.astype(BF16)
    lo = (value - hi.astype(F32)).astype(BF16)
    return jnp.concatenate([hi, lo], axis=0)


def fold(value):
    half = value.shape[0] // 2
    return value[:half] + value[half:]


def call(kernel, outs, specs, *args, scratch=(), vmem=16, flops=1, data=1, after=()):
    used = len(args)

    def body(*refs):
        kernel(*refs[:used], *refs[used + len(after):])

    return pl.pallas_call(
        body,
        out_shape=outs,
        in_specs=list(specs) + [ANY] * len(after),
        out_specs=[VMEM for _ in outs],
        scratch_shapes=list(scratch),
        compiler_params=pltpu.CompilerParams(vmem_limit_bytes=vmem * MIB),
        cost_estimate=pl.CostEstimate(flops=flops, bytes_accessed=data, transcendentals=0),
    )(*args, *after)


def hold(values, after):
    count = len(values)
    return pl.pallas_call(
        lambda *refs: None,
        out_shape=[out(value.shape, value.dtype) for value in values],
        in_specs=[ANY] * (count + len(after)),
        out_specs=[ANY] * count,
        input_output_aliases={k: k for k in range(count)},
        compiler_params=pltpu.CompilerParams(vmem_limit_bytes=MIB),
    )(*values, *after)


def out(shape, dtype=F32):
    return jax.ShapeDtypeStruct(shape, dtype)


def merge_kernel(
    steps, w_ref, x_ref, a_ref, b_ref, dy_ref, m_ref, stat_ref, am_ref,
    xa, b2, dy, acc, sq, w_sem, x_sem, a_sem, b_sem, dy_sem,
):
    rows, cols = w_ref.shape
    toks = x_ref.shape[0]
    step = rows // steps
    tile = 2048
    b_copy = pltpu.make_async_copy(b_ref, b2, b_sem)
    dy_copy = pltpu.make_async_copy(dy_ref, dy, dy_sem)
    a_copy = pltpu.make_async_copy(a_ref, xa.at[toks:], a_sem)

    def w_copy(i):
        part = pl.ds(pl.multiple_of(i * step, step), step)
        return pltpu.make_async_copy(w_ref.at[part], m_ref.at[part], w_sem.at[i])

    x_copy = pltpu.make_async_copy(x_ref, xa.at[:toks], x_sem)
    b_copy.start()
    a_copy.start()
    w_copy(0).start()
    x_copy.start()
    for i in range(1, steps):
        w_copy(i).start()
    dy_copy.start()
    acc[...] = jnp.zeros_like(acc)
    sq[...] = jnp.zeros_like(sq)
    b_copy.wait()
    a_copy.wait()
    x_copy.wait()
    b2[...] = b2[...] + b2[...]

    @pl.loop(0, steps)
    def _(i):
        w_copy(i).wait()
        part = pl.ds(pl.multiple_of(i * step, step), step)
        xa_part = xa[:, part]
        a_part = xa_part[toks:]
        for c in range(cols // tile):
            at = slice(c * tile, (c + 1) * tile)
            m = (m_ref[part, at].astype(F32) + tn(a_part, b2[:, at])).astype(BF16)
            m_ref[part, at] = m
            wide = m.astype(F32)
            sq[:, at] += jnp.sum((wide * wide).reshape(step // 8, 8, tile), axis=0)
            acc[:, at] += nn(xa_part, m)

    dy_copy.wait()
    am_ref[...] = acc[toks:]
    stat_ref[0:1] = jnp.sum(sq[...], axis=0, keepdims=True)
    stat_ref[1:2] = jnp.sum(acc[:toks] * dy[...].astype(F32), axis=0, keepdims=True)


def merge(w, x, a_t, b, dy):
    rows, cols = w.shape
    toks = x.shape[0]
    rank = b.shape[0]
    steps = rows // 512
    dma = pltpu.SemaphoreType.DMA
    return call(
        functools.partial(merge_kernel, steps),
        [pltpu.VMEM((rows, cols), BF16), out((2, cols)), out((rank, cols))],
        [HBM] * 5,
        *[pltpu.with_memory_space_constraint(value, pltpu.HBM) for value in (w, x, a_t, b, dy)],
        scratch=[
            pltpu.VMEM((toks + rank, rows), BF16),
            pltpu.VMEM((rank, cols), BF16),
            pltpu.VMEM((toks, cols), BF16),
            pltpu.VMEM((toks + rank, cols), F32),
            pltpu.VMEM((8, cols), F32),
            dma((steps,)), dma, dma, dma, dma,
        ],
        vmem=32,
        flops=2 * rows * cols * (toks + 2 * rank),
        data=rows * cols * 2,
    )


def q_kernel(a_ref, x_ref, dy_ref, bq_ref):
    bq_ref[...] = fold(nn(hi_lo(nt(a_ref[...], x_ref[...])), dy_ref[...]))


def block(m_ref, index, half=None, count=4):
    size = m_ref.shape[0] // count
    start = lax.rem(index + count, count) * size
    if half is not None:
        size //= 2
        start += half * size
    return m_ref[pl.ds(pl.multiple_of(start, 64), size)]


def far_kernel(stat_ref, r1_ref, r2_ref, r3_ref, mag_ref, dy_ref, m_ref, vec_ref, scaled_ref, h0_ref, h1_ref):
    total = (stat_ref[...] + r2_ref[...]) + (r1_ref[...] + r3_ref[...])
    squares = total[0:1] + EPS
    norms = jnp.sqrt(squares)
    scale = mag_ref[...] / norms
    vec_ref[...] = jnp.concatenate([squares, norms, scale, total[1:2]], axis=0)
    scaled = (dy_ref[...].astype(F32) * scale).astype(BF16)
    scaled_ref[...] = scaled
    y = lax.axis_index("cols")
    h0_ref[...] = nt(block(m_ref, y + 2, 0), scaled)
    h1_ref[...] = nt(block(m_ref, y + 2, 1), scaled)


def near_kernel(m_ref, scaled_ref, up_ref, down_ref):
    y = lax.axis_index("cols")
    up_ref[...] = nt(block(m_ref, y + 1, 1), scaled_ref[...])
    down_ref[...] = nt(block(m_ref, y - 1, 0), scaled_ref[...])


def relay_kernel(m_ref, scaled_ref, u0_ref, u1_ref, up_ref, down_ref):
    y = lax.axis_index("cols")
    up_ref[...] = u0_ref[...] + nt(block(m_ref, y + 1, 0), scaled_ref[...])
    down_ref[...] = u1_ref[...] + nt(block(m_ref, y - 1, 1), scaled_ref[...])


def own_kernel(m_ref, scaled_ref, own_ref):
    own_ref[...] = nt(block(m_ref, lax.axis_index("cols")), scaled_ref[...])


def gather_kernel(own_ref, v0_ref, v1_ref, sum_ref):
    half = own_ref.shape[0] // 2
    sum_ref[:half] = own_ref[:half] + v1_ref[...]
    sum_ref[half:] = own_ref[half:] + v0_ref[...]


def finish_kernel(own_ref, w0_ref, w1_ref, out_ref, done_ref):
    done_ref[...] = jnp.zeros_like(done_ref)
    half = own_ref.shape[0] // 2
    out_ref[:half] = (own_ref[:half] + w0_ref[...]).astype(BF16)
    out_ref[half:] = (own_ref[half:] + w1_ref[...]).astype(BF16)


def a_kernel(factor, vec_ref, dy_ref, b_ref, x_ref, m_ref, *refs):
    outs, whole = refs[:-1], refs[-1]
    scale = vec_ref[2:3] * factor
    wide = b_ref[...].astype(F32) * scale
    p_t = fold(nt(hi_lo(wide), dy_ref[...]))
    left = hi_lo(p_t)
    right = hi_lo(wide * (vec_ref[3:4] / vec_ref[0:1]))
    rows = m_ref.shape[0]
    tile = 512
    for r in range(rows // tile):
        at = slice(r * tile, (r + 1) * tile)
        whole[:, at] = fold(nn(left, x_ref[:, at]) - nt(right, m_ref[at]))
    split(whole, outs, lax.axis_index("dp"), 1)


def split(whole, outs, index, axis):
    count = len(outs)
    size = whole.shape[axis] // count
    for k, ref in enumerate(outs):
        at = pl.ds(pl.multiple_of(lax.rem(index + k, count) * size, 128 if axis else 8), size)
        ref[...] = whole[:, at] if axis else whole[at]


def sum_kernel(*refs):
    refs[-1][...] = functools.reduce(jnp.add, [ref[...] for ref in refs[:-1]])


def add(*ins, after=()):
    return call(sum_kernel, [out(ins[0].shape)], [VMEM] * len(ins), *ins, after=after)[0]


def halve_kernel(position, left_ref, right_ref, keep_ref, send_ref, whole):
    whole[...] = left_ref[...] + right_ref[...]
    split(whole, [keep_ref, send_ref], position(), 0)


def halve(left, right, position, after=()):
    rows, cols = left.shape
    return call(
        functools.partial(halve_kernel, position),
        [out((rows // 2, cols))] * 2,
        [VMEM] * 2,
        left, right,
        scratch=[pltpu.VMEM((rows, cols), F32)],
        after=after,
    )


def join_kernel(position, axis, *refs):
    ins, whole = refs[:-1], refs[-1]
    count = len(ins)
    size = ins[0].shape[axis]
    for k, ref in enumerate(ins):
        start = lax.rem(position() + count - k, count) * size
        at = pl.ds(pl.multiple_of(start, 128 if axis else 8), size)
        if axis:
            whole[:, at] = ref[...]
        else:
            whole[at] = ref[...]


def join(ins, position, axis, after=()):
    shape = list(ins[0].shape)
    shape[axis] *= len(ins)
    return call(
        functools.partial(join_kernel, position, axis),
        [out(tuple(shape))],
        [VMEM] * len(ins),
        *ins,
        after=after,
    )[0]


def b_kernel(factor, vec_ref, bq_ref, am_ref, keep_ref, send_ref, whole):
    ratio = vec_ref[3:4] / vec_ref[0:1]
    whole[...] = (vec_ref[2:3] * factor) * (bq_ref[...] - ratio * am_ref[...])
    split(whole, [keep_ref, send_ref], core_bit(), 0)


def add_halves_kernel(left_ref, right_ref, top_ref, bottom_ref):
    half = top_ref.shape[0]
    top_ref[...] = left_ref[:half] + right_ref[:half]
    bottom_ref[...] = left_ref[half:] + right_ref[half:]


def pair_kernel(top_ref, top_more_ref, bottom_ref, bottom_more_ref, top_out_ref, bottom_out_ref):
    half = top_ref.shape[0]
    top_out_ref[:half] = top_ref[...]
    top_out_ref[half:] = top_more_ref[...]
    bottom_out_ref[:half] = bottom_ref[...]
    bottom_out_ref[half:] = bottom_more_ref[...]


def a_join_kernel(top_ref, top_more_ref, bottom_ref, bottom_more_ref, whole):
    z = dp_index()
    first = z + 1 - 2 * lax.rem(z, 2)
    second = 3 - z
    half, size = top_ref.shape[0] // 2, top_ref.shape[1]
    for row, ref, near, far in (
        (0, top_ref, z, second),
        (0, top_more_ref, first, 3 - first),
        (half, bottom_ref, z, first),
        (half, bottom_more_ref, second, 3 - first),
    ):
        whole[row:row + half, pl.ds(pl.multiple_of(near * size, 128), size)] = ref[:half]
        whole[row:row + half, pl.ds(pl.multiple_of(far * size, 128), size)] = ref[half:]


def b_stack_kernel(left_ref, right_ref, vec_ref, out_ref):
    rows = left_ref.shape[0]
    out_ref[:rows] = left_ref[...] + right_ref[...]
    out_ref[rows:] = jnp.broadcast_to(vec_ref[3:4], left_ref.shape)


def b_unstack_kernel(factor, left_ref, right_ref, vec_ref, b_ref, mag_ref):
    rows = b_ref.shape[0]
    total = left_ref[...] + right_ref[...]
    b_ref[...] = total[:rows]
    mag_ref[...] = factor * total[rows:rows + 1] / vec_ref[1:2]


def core_bit():
    return lax.rem(lax.axis_index("rows"), 2)


def near_bit():
    return lax.rem(lax.div(lax.div(lax.axis_index("rows"), 2) + 1, 2), 2)


def far_bit():
    return lax.div(lax.axis_index("rows"), 4)


def dp_index():
    return lax.axis_index("dp")


def ring(value, axis, k, count=4):
    return lax.ppermute(value, axis, [(i, (i + k) % count) for i in range(count)])


def ring_x(value, k, count=8):
    return lax.ppermute(value, "rows", [(i, (i + 2 * k) % count) for i in range(count)])


def swap(value, axis, step):
    return lax.ppermute(value, axis, [(i, i ^ 1 if step == 0 else 3 - i) for i in range(4)])


def swap_x(value, step):
    return lax.ppermute(value, "rows", [(i, i ^ 2 if step == 0 else 6 - 2 * (i // 2) + i % 2) for i in range(8)])


def swap_core(value, count=8):
    return lax.ppermute(value, "rows", [(i, i ^ 1) for i in range(count)])


def shards(x, dy, w, a, b, mag):
    rows, cols = w.shape
    toks, rank = x.shape[0], a.shape[1]
    groups, full_rows = 4, rows * 8
    gamma = float(toks * groups) ** (-0.5)
    mag = mag.reshape(1, cols)
    m, stat, am = merge(w, x, a.T, b, dy)
    bq = call(q_kernel, [out((rank, cols))], [VMEM] * 3, a.T, x, dy, after=[stat])[0]

    m = pltpu.with_memory_space_constraint(m, pltpu.VMEM)
    stat = stat + swap_core(stat)
    far = rows // 8
    vec, scaled, h0, h1 = call(
        far_kernel,
        [out((4, cols)), out((toks, cols), BF16), out((far, toks)), out((far, toks))],
        [VMEM] * 7,
        stat, ring_x(stat, 1), ring_x(stat, 2), ring_x(stat, 3), mag, dy, m,
        after=[bq],
    )
    u0, u1 = ring(h0, "cols", 1), ring(h1, "cols", 3)
    keep, send = call(
        functools.partial(b_kernel, 2.0 * gamma),
        [out((rank // 2, cols))] * 2,
        [VMEM] * 3,
        vec, bq, am,
        scratch=[pltpu.VMEM((rank, cols), F32)],
    )
    keep, send = halve(keep, swap_core(send), near_bit)
    pieces = call(
        functools.partial(a_kernel, 2.0 * gamma),
        [out((rank, rows // 4))] * 4,
        [VMEM] * 5,
        vec, dy, b, x, m,
        scratch=[pltpu.VMEM((rank, rows), F32)],
        after=[send],
    )
    keep, send = halve(keep, swap_x(send, 0), far_bit, after=[pieces[0]])
    pieces = [pieces[0]] + [ring(pieces[k], "dp", k) for k in (1, 3, 2)]
    half = [out((far, toks))] * 2
    v_up, v_down = call(near_kernel, half, [VMEM] * 2, m, scaled, after=[send])
    v_up, v_down = hold([v_up, v_down], [u0, u1])
    v0, v1 = ring(v_up, "cols", 1), ring(v_down, "cols", 3)
    own = call(own_kernel, [out((rows // 4, toks))], [VMEM] * 2, m, scaled, after=[v_up])[0]
    up, down = call(relay_kernel, half, [VMEM] * 4, m, scaled, u0, u1, after=[own])

    piece = add(*pieces, after=[up])
    stack = call(
        b_stack_kernel, [out((rank // 4, cols))], [VMEM] * 3, keep, swap_x(send, 1), vec, after=[piece]
    )[0]
    own = call(gather_kernel, [out((rows // 4, toks))], [VMEM] * 3, own, v0, v1, after=[stack])[0]
    piece = add(piece, swap(piece, "cols", 0), after=[own])
    last = (piece, swap(piece, "cols", 1))
    stack = add(stack, swap(stack, "dp", 0), after=[piece])
    up, down = hold([up, down], [stack])
    w0, w1 = ring(up, "cols", 1), ring(down, "cols", 3)
    piece = [out((rank // 2, rows // 4))] * 2
    top, bottom = call(add_halves_kernel, piece, [VMEM] * 2, *last, after=[up])
    b_part, mag_grad = call(
        functools.partial(b_unstack_kernel, gamma / float(full_rows) ** 0.5),
        [out((rank // 8, cols)), out((1, cols))],
        [VMEM] * 3,
        stack, swap(stack, "dp", 1), vec,
        after=[top],
    )
    b_part = join([b_part, swap_x(b_part, 1)], far_bit, 0)
    top, bottom = call(
        pair_kernel,
        [out((rank, rows // 4))] * 2,
        [VMEM] * 4,
        top, swap(top, "dp", 1), bottom, swap(bottom, "dp", 0),
        after=[b_part],
    )
    grad, done = call(
        finish_kernel, [out((rows // 4, toks), BF16), out((8, 128))], [VMEM] * 3, own, w0, w1, after=[top]
    )
    top_more, bottom_more = hold([swap(top, "dp", 0), swap(bottom, "dp", 1)], [done])
    b_part = join([b_part, swap_x(b_part, 0)], near_bit, 0, after=[top_more])
    a_grad = call(a_join_kernel, [out((rank, rows))], [VMEM] * 4, top, top_more, bottom, bottom_more, after=[b_part])[0]
    b_grad = join([b_part, swap_core(b_part)], core_bit, 0)
    return grad, a_grad.T, b_grad, mag_grad.reshape(cols)


def solution(mesh):
    return jax.shard_map(
        shards,
        mesh=mesh,
        in_specs=(
            P("dp", "rows"),
            P("dp", "cols"),
            P("rows", "cols"),
            P("rows", None),
            P(None, "cols"),
            P("cols"),
        ),
        out_specs=(P(("rows", "cols"), "dp"), P("rows", None), P(None, "cols"), P("cols")),
        check_vma=False,
    )
```

```python
import functools

import jax
import jax.numpy as jnp
from jax import lax
from jax.experimental import pallas as pl
from jax.experimental.pallas import tpu as pltpu
from jax.sharding import PartitionSpec as P

EPS = 1e-06
F32 = jnp.float32
BF16 = jnp.bfloat16
MIB = 1024 * 1024

ANY = pl.BlockSpec(memory_space=pl.ANY)
VMEM = pl.BlockSpec(memory_space=pltpu.VMEM)
HBM = pl.BlockSpec(memory_space=pltpu.HBM)


def nn(a, b):
    return lax.dot_general(a, b, (((1,), (0,)), ((), ())), preferred_element_type=F32)


def nt(a, b):
    return lax.dot_general(a, b, (((1,), (1,)), ((), ())), preferred_element_type=F32)


def tn(a, b):
    return lax.dot_general(a, b, (((0,), (0,)), ((), ())), preferred_element_type=F32)


def hi_lo(value):
    hi = value.astype(BF16)
    lo = (value - hi.astype(F32)).astype(BF16)
    return jnp.concatenate([hi, lo], axis=0)


def fold(value):
    half = value.shape[0] // 2
    return value[:half] + value[half:]


def call(kernel, outs, specs, *args, scratch=(), vmem=16, flops=1, data=1, after=()):
    used = len(args)

    def body(*refs):
        kernel(*refs[:used], *refs[used + len(after):])

    return pl.pallas_call(
        body,
        out_shape=outs,
        in_specs=list(specs) + [ANY] * len(after),
        out_specs=[VMEM for _ in outs],
        scratch_shapes=list(scratch),
        compiler_params=pltpu.CompilerParams(vmem_limit_bytes=vmem * MIB),
        cost_estimate=pl.CostEstimate(flops=flops, bytes_accessed=data, transcendentals=0),
    )(*args, *after)


def hold(values, after):
    count = len(values)
    return pl.pallas_call(
        lambda *refs: None,
        out_shape=[out(value.shape, value.dtype) for value in values],
        in_specs=[ANY] * (count + len(after)),
        out_specs=[ANY] * count,
        input_output_aliases={k: k for k in range(count)},
        compiler_params=pltpu.CompilerParams(vmem_limit_bytes=MIB),
    )(*values, *after)


def out(shape, dtype=F32):
    return jax.ShapeDtypeStruct(shape, dtype)


def merge_kernel(
    steps, w_ref, x_ref, a_ref, b_ref, dy_ref, m_ref, stat_ref, am_ref,
    xa, b2, dy, acc, sq, w_sem, x_sem, a_sem, b_sem, dy_sem,
):
    rows, cols = w_ref.shape
    toks = x_ref.shape[0]
    step = rows // steps
    tile = 2048
    b_copy = pltpu.make_async_copy(b_ref, b2, b_sem)
    dy_copy = pltpu.make_async_copy(dy_ref, dy, dy_sem)
    a_copy = pltpu.make_async_copy(a_ref, xa.at[toks:], a_sem)

    def w_copy(i):
        part = pl.ds(pl.multiple_of(i * step, step), step)
        return pltpu.make_async_copy(w_ref.at[part], m_ref.at[part], w_sem.at[i])

    x_copy = pltpu.make_async_copy(x_ref, xa.at[:toks], x_sem)
    b_copy.start()
    a_copy.start()
    w_copy(0).start()
    x_copy.start()
    for i in range(1, steps):
        w_copy(i).start()
    dy_copy.start()
    acc[...] = jnp.zeros_like(acc)
    sq[...] = jnp.zeros_like(sq)
    b_copy.wait()
    a_copy.wait()
    x_copy.wait()
    b2[...] = b2[...] + b2[...]

    @pl.loop(0, steps)
    def _(i):
        w_copy(i).wait()
        part = pl.ds(pl.multiple_of(i * step, step), step)
        xa_part = xa[:, part]
        a_part = xa_part[toks:]
        for c in range(cols // tile):
            at = slice(c * tile, (c + 1) * tile)
            m = (m_ref[part, at].astype(F32) + tn(a_part, b2[:, at])).astype(BF16)
            m_ref[part, at] = m
            wide = m.astype(F32)
            sq[:, at] += jnp.sum((wide * wide).reshape(step // 8, 8, tile), axis=0)
            acc[:, at] += nn(xa_part, m)

    dy_copy.wait()
    am_ref[...] = acc[toks:]
    stat_ref[0:1] = jnp.sum(sq[...], axis=0, keepdims=True)
    stat_ref[1:2] = jnp.sum(acc[:toks] * dy[...].astype(F32), axis=0, keepdims=True)


def merge(w, x, a_t, b, dy):
    rows, cols = w.shape
    toks = x.shape[0]
    rank = b.shape[0]
    steps = rows // 512
    dma = pltpu.SemaphoreType.DMA
    return call(
        functools.partial(merge_kernel, steps),
        [pltpu.VMEM((rows, cols), BF16), out((2, cols)), out((rank, cols))],
        [HBM] * 5,
        *[pltpu.with_memory_space_constraint(value, pltpu.HBM) for value in (w, x, a_t, b, dy)],
        scratch=[
            pltpu.VMEM((toks + rank, rows), BF16),
            pltpu.VMEM((rank, cols), BF16),
            pltpu.VMEM((toks, cols), BF16),
            pltpu.VMEM((toks + rank, cols), F32),
            pltpu.VMEM((8, cols), F32),
            dma((steps,)), dma, dma, dma, dma,
        ],
        vmem=32,
        flops=2 * rows * cols * (toks + 2 * rank),
        data=rows * cols * 2,
    )


def q_kernel(a_ref, x_ref, dy_ref, bq_ref):
    bq_ref[...] = fold(nn(hi_lo(nt(a_ref[...], x_ref[...])), dy_ref[...]))


def block(m_ref, index, half=None, count=4):
    size = m_ref.shape[0] // count
    start = lax.rem(index + count, count) * size
    if half is not None:
        size //= 2
        start += half * size
    return m_ref[pl.ds(pl.multiple_of(start, 64), size)]


def far_kernel(stat_ref, r1_ref, r2_ref, r3_ref, mag_ref, dy_ref, m_ref, vec_ref, scaled_ref, h0_ref, h1_ref):
    total = (stat_ref[...] + r2_ref[...]) + (r1_ref[...] + r3_ref[...])
    squares = total[0:1] + EPS
    norms = jnp.sqrt(squares)
    scale = mag_ref[...] / norms
    vec_ref[...] = jnp.concatenate([squares, norms, scale, total[1:2]], axis=0)
    scaled = (dy_ref[...].astype(F32) * scale).astype(BF16)
    scaled_ref[...] = scaled
    y = lax.axis_index("cols")
    h0_ref[...] = nt(block(m_ref, y + 2, 0), scaled)
    h1_ref[...] = nt(block(m_ref, y + 2, 1), scaled)


def near_kernel(m_ref, scaled_ref, up_ref, down_ref):
    y = lax.axis_index("cols")
    up_ref[...] = nt(block(m_ref, y + 1, 1), scaled_ref[...])
    down_ref[...] = nt(block(m_ref, y - 1, 0), scaled_ref[...])


def relay_kernel(m_ref, scaled_ref, u0_ref, u1_ref, up_ref, down_ref):
    y = lax.axis_index("cols")
    up_ref[...] = u0_ref[...] + nt(block(m_ref, y + 1, 0), scaled_ref[...])
    down_ref[...] = u1_ref[...] + nt(block(m_ref, y - 1, 1), scaled_ref[...])


def own_kernel(m_ref, scaled_ref, own_ref):
    own_ref[...] = nt(block(m_ref, lax.axis_index("cols")), scaled_ref[...])


def gather_kernel(own_ref, v0_ref, v1_ref, sum_ref):
    half = own_ref.shape[0] // 2
    sum_ref[:half] = own_ref[:half] + v1_ref[...]
    sum_ref[half:] = own_ref[half:] + v0_ref[...]


def finish_kernel(own_ref, w0_ref, w1_ref, out_ref, done_ref):
    done_ref[...] = jnp.zeros_like(done_ref)
    half = own_ref.shape[0] // 2
    out_ref[:half] = (own_ref[:half] + w0_ref[...]).astype(BF16)
    out_ref[half:] = (own_ref[half:] + w1_ref[...]).astype(BF16)


def a_kernel(factor, vec_ref, dy_ref, b_ref, x_ref, m_ref, *refs):
    outs, whole = refs[:-1], refs[-1]
    scale = vec_ref[2:3] * factor
    wide = b_ref[...].astype(F32) * scale
    p_t = fold(nt(hi_lo(wide), dy_ref[...]))
    left = hi_lo(p_t)
    right = hi_lo(wide * (vec_ref[3:4] / vec_ref[0:1]))
    rows = m_ref.shape[0]
    tile = 512
    for r in range(rows // tile):
        at = slice(r * tile, (r + 1) * tile)
        whole[:, at] = fold(nn(left, x_ref[:, at]) - nt(right, m_ref[at]))
    split(whole, outs, lax.axis_index("dp"), 1)


def split(whole, outs, index, axis):
    count = len(outs)
    size = whole.shape[axis] // count
    for k, ref in enumerate(outs):
        at = pl.ds(pl.multiple_of(lax.rem(index + k, count) * size, 128 if axis else 8), size)
        ref[...] = whole[:, at] if axis else whole[at]


def sum_kernel(*refs):
    refs[-1][...] = functools.reduce(jnp.add, [ref[...] for ref in refs[:-1]])


def add(*ins, after=()):
    return call(sum_kernel, [out(ins[0].shape)], [VMEM] * len(ins), *ins, after=after)[0]


def halve_kernel(position, left_ref, right_ref, keep_ref, send_ref, whole):
    whole[...] = left_ref[...] + right_ref[...]
    split(whole, [keep_ref, send_ref], position(), 0)


def halve(left, right, position, after=()):
    rows, cols = left.shape
    return call(
        functools.partial(halve_kernel, position),
        [out((rows // 2, cols))] * 2,
        [VMEM] * 2,
        left, right,
        scratch=[pltpu.VMEM((rows, cols), F32)],
        after=after,
    )


def join_kernel(position, axis, *refs):
    ins, whole = refs[:-1], refs[-1]
    count = len(ins)
    size = ins[0].shape[axis]
    for k, ref in enumerate(ins):
        start = lax.rem(position() + count - k, count) * size
        at = pl.ds(pl.multiple_of(start, 128 if axis else 8), size)
        if axis:
            whole[:, at] = ref[...]
        else:
            whole[at] = ref[...]


def join(ins, position, axis, after=()):
    shape = list(ins[0].shape)
    shape[axis] *= len(ins)
    return call(
        functools.partial(join_kernel, position, axis),
        [out(tuple(shape))],
        [VMEM] * len(ins),
        *ins,
        after=after,
    )[0]


def b_kernel(factor, vec_ref, bq_ref, am_ref, keep_ref, send_ref, whole):
    ratio = vec_ref[3:4] / vec_ref[0:1]
    whole[...] = (vec_ref[2:3] * factor) * (bq_ref[...] - ratio * am_ref[...])
    split(whole, [keep_ref, send_ref], core_bit(), 0)


def add_halves_kernel(left_ref, right_ref, top_ref, bottom_ref):
    half = top_ref.shape[0]
    top_ref[...] = left_ref[:half] + right_ref[:half]
    bottom_ref[...] = left_ref[half:] + right_ref[half:]


def pair_kernel(top_ref, top_more_ref, bottom_ref, bottom_more_ref, top_out_ref, bottom_out_ref):
    half = top_ref.shape[0]
    top_out_ref[:half] = top_ref[...]
    top_out_ref[half:] = top_more_ref[...]
    bottom_out_ref[:half] = bottom_ref[...]
    bottom_out_ref[half:] = bottom_more_ref[...]


def a_join_kernel(top_ref, top_more_ref, bottom_ref, bottom_more_ref, whole):
    z = dp_index()
    first = z + 1 - 2 * lax.rem(z, 2)
    second = 3 - z
    half, size = top_ref.shape[0] // 2, top_ref.shape[1]
    for row, ref, near, far in (
        (0, top_ref, z, second),
        (0, top_more_ref, first, 3 - first),
        (half, bottom_ref, z, first),
        (half, bottom_more_ref, second, 3 - first),
    ):
        whole[row:row + half, pl.ds(pl.multiple_of(near * size, 128), size)] = ref[:half]
        whole[row:row + half, pl.ds(pl.multiple_of(far * size, 128), size)] = ref[half:]


def b_stack_kernel(left_ref, right_ref, vec_ref, out_ref):
    rows = left_ref.shape[0]
    out_ref[:rows] = left_ref[...] + right_ref[...]
    out_ref[rows:] = jnp.broadcast_to(vec_ref[3:4], left_ref.shape)


def b_unstack_kernel(factor, left_ref, right_ref, vec_ref, b_ref, mag_ref):
    rows = b_ref.shape[0]
    total = left_ref[...] + right_ref[...]
    b_ref[...] = total[:rows]
    mag_ref[...] = factor * total[rows:rows + 1] / vec_ref[1:2]


def core_bit():
    return lax.rem(lax.axis_index("rows"), 2)


def near_bit():
    return lax.rem(lax.div(lax.div(lax.axis_index("rows"), 2) + 1, 2), 2)


def far_bit():
    return lax.div(lax.axis_index("rows"), 4)


def dp_index():
    return lax.axis_index("dp")


def ring(value, axis, k, count=4):
    return lax.ppermute(value, axis, [(i, (i + k) % count) for i in range(count)])


def ring_x(value, k, count=8):
    return lax.ppermute(value, "rows", [(i, (i + 2 * k) % count) for i in range(count)])


def swap(value, axis, step):
    return lax.ppermute(value, axis, [(i, i ^ 1 if step == 0 else 3 - i) for i in range(4)])


def swap_x(value, step):
    return lax.ppermute(value, "rows", [(i, i ^ 2 if step == 0 else 6 - 2 * (i // 2) + i % 2) for i in range(8)])


def swap_core(value, count=8):
    return lax.ppermute(value, "rows", [(i, i ^ 1) for i in range(count)])


def shards(x, dy, w, a, b, mag):
    rows, cols = w.shape
    toks, rank = x.shape[0], a.shape[1]
    groups, full_rows = 4, rows * 8
    gamma = float(toks * groups) ** (-0.5)
    mag = mag.reshape(1, cols)
    m, stat, am = merge(w, x, a.T, b, dy)
    bq = call(q_kernel, [out((rank, cols))], [VMEM] * 3, a.T, x, dy, after=[stat])[0]

    m = pltpu.with_memory_space_constraint(m, pltpu.VMEM)
    stat = stat + swap_core(stat)
    far = rows // 8
    vec, scaled, h0, h1 = call(
        far_kernel,
        [out((4, cols)), out((toks, cols), BF16), out((far, toks)), out((far, toks))],
        [VMEM] * 7,
        stat, ring_x(stat, 1), ring_x(stat, 2), ring_x(stat, 3), mag, dy, m,
        after=[bq],
    )
    u0, u1 = ring(h0, "cols", 1), ring(h1, "cols", 3)
    keep, send = call(
        functools.partial(b_kernel, 2.0 * gamma),
        [out((rank // 2, cols))] * 2,
        [VMEM] * 3,
        vec, bq, am,
        scratch=[pltpu.VMEM((rank, cols), F32)],
    )
    half = [out((far, toks))] * 2
    v_up, v_down = call(near_kernel, half, [VMEM] * 2, m, scaled, after=[send])
    keep, send = halve(keep, swap_core(send), near_bit, after=[v_up])
    pieces = call(
        functools.partial(a_kernel, 2.0 * gamma),
        [out((rank, rows // 4))] * 4,
        [VMEM] * 5,
        vec, dy, b, x, m,
        scratch=[pltpu.VMEM((rank, rows), F32)],
        after=[send],
    )
    keep, send = halve(keep, swap_x(send, 0), far_bit, after=[pieces[0]])
    pieces = [pieces[0]] + [ring(pieces[k], "dp", k) for k in (1, 3, 2)]
    v_up, v_down = hold([v_up, v_down], [send, u0, u1])
    v0, v1 = ring(v_up, "cols", 1), ring(v_down, "cols", 3)
    own = call(own_kernel, [out((rows // 4, toks))], [VMEM] * 2, m, scaled, after=[v_up])[0]
    up, down = call(relay_kernel, half, [VMEM] * 4, m, scaled, u0, u1, after=[own])

    piece = add(*pieces, after=[up])
    stack = call(
        b_stack_kernel, [out((rank // 4, cols))], [VMEM] * 3, keep, swap_x(send, 1), vec, after=[piece]
    )[0]
    own = call(gather_kernel, [out((rows // 4, toks))], [VMEM] * 3, own, v0, v1, after=[stack])[0]
    piece = add(piece, swap(piece, "cols", 0), after=[own])
    last = (piece, swap(piece, "cols", 1))
    stack = add(stack, swap(stack, "dp", 0), after=[piece])
    up, down = hold([up, down], [stack])
    w0, w1 = ring(up, "cols", 1), ring(down, "cols", 3)
    piece = [out((rank // 2, rows // 4))] * 2
    top, bottom = call(add_halves_kernel, piece, [VMEM] * 2, *last, after=[up])
    b_part, mag_grad = call(
        functools.partial(b_unstack_kernel, gamma / float(full_rows) ** 0.5),
        [out((rank // 8, cols)), out((1, cols))],
        [VMEM] * 3,
        stack, swap(stack, "dp", 1), vec,
        after=[top],
    )
    b_part = join([b_part, swap_x(b_part, 1)], far_bit, 0)
    top, bottom = call(
        pair_kernel,
        [out((rank, rows // 4))] * 2,
        [VMEM] * 4,
        top, swap(top, "dp", 1), bottom, swap(bottom, "dp", 0),
        after=[b_part],
    )
    grad, done = call(
        finish_kernel, [out((rows // 4, toks), BF16), out((8, 128))], [VMEM] * 3, own, w0, w1, after=[top]
    )
    top_more, bottom_more = hold([swap(top, "dp", 0), swap(bottom, "dp", 1)], [done])
    b_part = join([b_part, swap_x(b_part, 0)], near_bit, 0, after=[top_more])
    a_grad = call(a_join_kernel, [out((rank, rows))], [VMEM] * 4, top, top_more, bottom, bottom_more, after=[b_part])[0]
    b_grad = join([b_part, swap_core(b_part)], core_bit, 0)
    return grad, a_grad.T, b_grad, mag_grad.reshape(cols)


def solution(mesh):
    return jax.shard_map(
        shards,
        mesh=mesh,
        in_specs=(
            P("dp", "rows"),
            P("dp", "cols"),
            P("rows", "cols"),
            P("rows", None),
            P(None, "cols"),
            P("cols"),
        ),
        out_specs=(P(("rows", "cols"), "dp"), P("rows", None), P(None, "cols"), P("cols")),
        check_vma=False,
    )
```

```python
import functools

import jax
import jax.numpy as jnp
from jax import lax
from jax.experimental import pallas as pl
from jax.experimental.pallas import tpu as pltpu
from jax.sharding import PartitionSpec as P

EPS = 1e-06
F32 = jnp.float32
BF16 = jnp.bfloat16
MIB = 1024 * 1024

ANY = pl.BlockSpec(memory_space=pl.ANY)
VMEM = pl.BlockSpec(memory_space=pltpu.VMEM)
HBM = pl.BlockSpec(memory_space=pltpu.HBM)


def nn(a, b):
    return lax.dot_general(a, b, (((1,), (0,)), ((), ())), preferred_element_type=F32)


def nt(a, b):
    return lax.dot_general(a, b, (((1,), (1,)), ((), ())), preferred_element_type=F32)


def tn(a, b):
    return lax.dot_general(a, b, (((0,), (0,)), ((), ())), preferred_element_type=F32)


def hi_lo(value):
    hi = value.astype(BF16)
    lo = (value - hi.astype(F32)).astype(BF16)
    return jnp.concatenate([hi, lo], axis=0)


def fold(value):
    half = value.shape[0] // 2
    return value[:half] + value[half:]


def call(kernel, outs, specs, *args, scratch=(), vmem=16, flops=1, data=1, after=()):
    used = len(args)

    def body(*refs):
        kernel(*refs[:used], *refs[used + len(after):])

    return pl.pallas_call(
        body,
        out_shape=outs,
        in_specs=list(specs) + [ANY] * len(after),
        out_specs=[VMEM for _ in outs],
        scratch_shapes=list(scratch),
        compiler_params=pltpu.CompilerParams(vmem_limit_bytes=vmem * MIB),
        cost_estimate=pl.CostEstimate(flops=flops, bytes_accessed=data, transcendentals=0),
    )(*args, *after)


def hold(values, after):
    count = len(values)
    return pl.pallas_call(
        lambda *refs: None,
        out_shape=[out(value.shape, value.dtype) for value in values],
        in_specs=[ANY] * (count + len(after)),
        out_specs=[ANY] * count,
        input_output_aliases={k: k for k in range(count)},
        compiler_params=pltpu.CompilerParams(vmem_limit_bytes=MIB),
    )(*values, *after)


def out(shape, dtype=F32):
    return jax.ShapeDtypeStruct(shape, dtype)


def merge_kernel(
    steps, w_ref, x_ref, a_ref, b_ref, dy_ref, m_ref, stat_ref, am_ref,
    xa, b2, dy, acc, sq, w_sem, x_sem, a_sem, b_sem, dy_sem,
):
    rows, cols = w_ref.shape
    toks = x_ref.shape[0]
    step = rows // steps
    tile = 2048
    b_copy = pltpu.make_async_copy(b_ref, b2, b_sem)
    dy_copy = pltpu.make_async_copy(dy_ref, dy, dy_sem)
    a_copy = pltpu.make_async_copy(a_ref, xa.at[toks:], a_sem)

    def w_copy(i):
        part = pl.ds(pl.multiple_of(i * step, step), step)
        return pltpu.make_async_copy(w_ref.at[part], m_ref.at[part], w_sem.at[i])

    x_copy = pltpu.make_async_copy(x_ref, xa.at[:toks], x_sem)
    b_copy.start()
    a_copy.start()
    w_copy(0).start()
    x_copy.start()
    for i in range(1, steps):
        w_copy(i).start()
    dy_copy.start()
    acc[...] = jnp.zeros_like(acc)
    sq[...] = jnp.zeros_like(sq)
    b_copy.wait()
    a_copy.wait()
    x_copy.wait()
    b2[...] = b2[...] + b2[...]

    @pl.loop(0, steps)
    def _(i):
        w_copy(i).wait()
        part = pl.ds(pl.multiple_of(i * step, step), step)
        xa_part = xa[:, part]
        a_part = xa_part[toks:]
        for c in range(cols // tile):
            at = slice(c * tile, (c + 1) * tile)
            m = (m_ref[part, at].astype(F32) + tn(a_part, b2[:, at])).astype(BF16)
            m_ref[part, at] = m
            wide = m.astype(F32)
            sq[:, at] += jnp.sum((wide * wide).reshape(step // 8, 8, tile), axis=0)
            acc[:, at] += nn(xa_part, m)

    dy_copy.wait()
    am_ref[...] = acc[toks:]
    stat_ref[0:1] = jnp.sum(sq[...], axis=0, keepdims=True)
    stat_ref[1:2] = jnp.sum(acc[:toks] * dy[...].astype(F32), axis=0, keepdims=True)


def merge(w, x, a_t, b, dy):
    rows, cols = w.shape
    toks = x.shape[0]
    rank = b.shape[0]
    steps = rows // 512
    dma = pltpu.SemaphoreType.DMA
    return call(
        functools.partial(merge_kernel, steps),
        [pltpu.VMEM((rows, cols), BF16), out((2, cols)), out((rank, cols))],
        [HBM] * 5,
        *[pltpu.with_memory_space_constraint(value, pltpu.HBM) for value in (w, x, a_t, b, dy)],
        scratch=[
            pltpu.VMEM((toks + rank, rows), BF16),
            pltpu.VMEM((rank, cols), BF16),
            pltpu.VMEM((toks, cols), BF16),
            pltpu.VMEM((toks + rank, cols), F32),
            pltpu.VMEM((8, cols), F32),
            dma((steps,)), dma, dma, dma, dma,
        ],
        vmem=32,
        flops=2 * rows * cols * (toks + 2 * rank),
        data=rows * cols * 2,
    )


def q_kernel(a_ref, x_ref, dy_ref, bq_ref):
    bq_ref[...] = fold(nn(hi_lo(nt(a_ref[...], x_ref[...])), dy_ref[...]))


def block(m_ref, index, half=None, count=4):
    size = m_ref.shape[0] // count
    start = lax.rem(index + count, count) * size
    if half is not None:
        size //= 2
        start += half * size
    return m_ref[pl.ds(pl.multiple_of(start, 64), size)]


def far_kernel(stat_ref, r1_ref, r2_ref, r3_ref, mag_ref, dy_ref, m_ref, vec_ref, scaled_ref, h0_ref, h1_ref):
    total = (stat_ref[...] + r2_ref[...]) + (r1_ref[...] + r3_ref[...])
    squares = total[0:1] + EPS
    norms = jnp.sqrt(squares)
    scale = mag_ref[...] / norms
    vec_ref[...] = jnp.concatenate([squares, norms, scale, total[1:2]], axis=0)
    scaled = (dy_ref[...].astype(F32) * scale).astype(BF16)
    scaled_ref[...] = scaled
    y = lax.axis_index("cols")
    h0_ref[...] = nt(block(m_ref, y + 2, 0), scaled)
    h1_ref[...] = nt(block(m_ref, y + 2, 1), scaled)


def near_kernel(m_ref, scaled_ref, up_ref, down_ref):
    y = lax.axis_index("cols")
    up_ref[...] = nt(block(m_ref, y + 1, 1), scaled_ref[...])
    down_ref[...] = nt(block(m_ref, y - 1, 0), scaled_ref[...])


def relay_kernel(m_ref, scaled_ref, u0_ref, u1_ref, up_ref, down_ref):
    y = lax.axis_index("cols")
    up_ref[...] = u0_ref[...] + nt(block(m_ref, y + 1, 0), scaled_ref[...])
    down_ref[...] = u1_ref[...] + nt(block(m_ref, y - 1, 1), scaled_ref[...])


def own_kernel(m_ref, scaled_ref, own_ref):
    own_ref[...] = nt(block(m_ref, lax.axis_index("cols")), scaled_ref[...])


def gather_kernel(own_ref, v0_ref, v1_ref, sum_ref):
    half = own_ref.shape[0] // 2
    sum_ref[:half] = own_ref[:half] + v1_ref[...]
    sum_ref[half:] = own_ref[half:] + v0_ref[...]


def finish_kernel(own_ref, w0_ref, w1_ref, out_ref, done_ref):
    done_ref[...] = jnp.zeros_like(done_ref)
    half = own_ref.shape[0] // 2
    out_ref[:half] = (own_ref[:half] + w0_ref[...]).astype(BF16)
    out_ref[half:] = (own_ref[half:] + w1_ref[...]).astype(BF16)


def a_kernel(factor, vec_ref, dy_ref, b_ref, x_ref, m_ref, *outs):
    scale = vec_ref[2:3] * factor
    wide = b_ref[...].astype(F32) * scale
    p_t = fold(nt(hi_lo(wide), dy_ref[...]))
    left = hi_lo(p_t)
    right = hi_lo(wide * (vec_ref[3:4] / vec_ref[0:1]))
    count = len(outs)
    size = m_ref.shape[0] // count
    for k, ref in enumerate(outs):
        start = pl.multiple_of(lax.rem(dp_index() + k, count) * size, 128)
        ref[...] = fold(nn(left, x_ref[:, pl.ds(start, size)]) - nt(right, m_ref[pl.ds(start, size)]))


def split(whole, outs, index, axis):
    count = len(outs)
    size = whole.shape[axis] // count
    for k, ref in enumerate(outs):
        at = pl.ds(pl.multiple_of(lax.rem(index + k, count) * size, 128 if axis else 8), size)
        ref[...] = whole[:, at] if axis else whole[at]


def sum_kernel(*refs):
    refs[-1][...] = functools.reduce(jnp.add, [ref[...] for ref in refs[:-1]])


def add(*ins, after=()):
    return call(sum_kernel, [out(ins[0].shape)], [VMEM] * len(ins), *ins, after=after)[0]


def halve_kernel(position, left_ref, right_ref, keep_ref, send_ref, whole):
    whole[...] = left_ref[...] + right_ref[...]
    split(whole, [keep_ref, send_ref], position(), 0)


def halve(left, right, position, after=()):
    rows, cols = left.shape
    return call(
        functools.partial(halve_kernel, position),
        [out((rows // 2, cols))] * 2,
        [VMEM] * 2,
        left, right,
        scratch=[pltpu.VMEM((rows, cols), F32)],
        after=after,
    )


def join_kernel(position, axis, *refs):
    ins, whole = refs[:-1], refs[-1]
    count = len(ins)
    size = ins[0].shape[axis]
    for k, ref in enumerate(ins):
        start = lax.rem(position() + count - k, count) * size
        at = pl.ds(pl.multiple_of(start, 128 if axis else 8), size)
        if axis:
            whole[:, at] = ref[...]
        else:
            whole[at] = ref[...]


def join(ins, position, axis, after=()):
    shape = list(ins[0].shape)
    shape[axis] *= len(ins)
    return call(
        functools.partial(join_kernel, position, axis),
        [out(tuple(shape))],
        [VMEM] * len(ins),
        *ins,
        after=after,
    )[0]


def b_kernel(factor, vec_ref, bq_ref, am_ref, keep_ref, send_ref, whole):
    ratio = vec_ref[3:4] / vec_ref[0:1]
    whole[...] = (vec_ref[2:3] * factor) * (bq_ref[...] - ratio * am_ref[...])
    split(whole, [keep_ref, send_ref], core_bit(), 0)


def add_halves_kernel(left_ref, right_ref, top_ref, bottom_ref):
    half = top_ref.shape[0]
    top_ref[...] = left_ref[:half] + right_ref[:half]
    bottom_ref[...] = left_ref[half:] + right_ref[half:]


def pair_kernel(top_ref, top_more_ref, bottom_ref, bottom_more_ref, top_out_ref, bottom_out_ref):
    half = top_ref.shape[0]
    top_out_ref[:half] = top_ref[...]
    top_out_ref[half:] = top_more_ref[...]
    bottom_out_ref[:half] = bottom_ref[...]
    bottom_out_ref[half:] = bottom_more_ref[...]


def a_join_kernel(top_ref, top_more_ref, bottom_ref, bottom_more_ref, whole):
    z = dp_index()
    first = z + 1 - 2 * lax.rem(z, 2)
    second = 3 - z
    half, size = top_ref.shape[0] // 2, top_ref.shape[1]
    for row, ref, near, far in (
        (0, top_ref, z, second),
        (0, top_more_ref, first, 3 - first),
        (half, bottom_ref, z, first),
        (half, bottom_more_ref, second, 3 - first),
    ):
        whole[row:row + half, pl.ds(pl.multiple_of(near * size, 128), size)] = ref[:half]
        whole[row:row + half, pl.ds(pl.multiple_of(far * size, 128), size)] = ref[half:]


def b_stack_kernel(left_ref, right_ref, vec_ref, out_ref):
    rows = left_ref.shape[0]
    out_ref[:rows] = left_ref[...] + right_ref[...]
    out_ref[rows:] = jnp.broadcast_to(vec_ref[3:4], left_ref.shape)


def b_unstack_kernel(factor, left_ref, right_ref, vec_ref, b_ref, mag_ref):
    rows = b_ref.shape[0]
    total = left_ref[...] + right_ref[...]
    b_ref[...] = total[:rows]
    mag_ref[...] = factor * total[rows:rows + 1] / vec_ref[1:2]


def core_bit():
    return lax.rem(lax.axis_index("rows"), 2)


def near_bit():
    return lax.rem(lax.div(lax.div(lax.axis_index("rows"), 2) + 1, 2), 2)


def far_bit():
    return lax.div(lax.axis_index("rows"), 4)


def dp_index():
    return lax.axis_index("dp")


def ring(value, axis, k, count=4):
    return lax.ppermute(value, axis, [(i, (i + k) % count) for i in range(count)])


def ring_x(value, k, count=8):
    return lax.ppermute(value, "rows", [(i, (i + 2 * k) % count) for i in range(count)])


def swap(value, axis, step):
    return lax.ppermute(value, axis, [(i, i ^ 1 if step == 0 else 3 - i) for i in range(4)])


def swap_x(value, step):
    return lax.ppermute(value, "rows", [(i, i ^ 2 if step == 0 else 6 - 2 * (i // 2) + i % 2) for i in range(8)])


def swap_core(value, count=8):
    return lax.ppermute(value, "rows", [(i, i ^ 1) for i in range(count)])


def shards(x, dy, w, a, b, mag):
    rows, cols = w.shape
    toks, rank = x.shape[0], a.shape[1]
    groups, full_rows = 4, rows * 8
    gamma = float(toks * groups) ** (-0.5)
    mag = mag.reshape(1, cols)
    m, stat, am = merge(w, x, a.T, b, dy)
    bq = call(q_kernel, [out((rank, cols))], [VMEM] * 3, a.T, x, dy, after=[stat])[0]

    m = pltpu.with_memory_space_constraint(m, pltpu.VMEM)
    stat = stat + swap_core(stat)
    far = rows // 8
    vec, scaled, h0, h1 = call(
        far_kernel,
        [out((4, cols)), out((toks, cols), BF16), out((far, toks)), out((far, toks))],
        [VMEM] * 7,
        stat, ring_x(stat, 1), ring_x(stat, 2), ring_x(stat, 3), mag, dy, m,
        after=[bq],
    )
    u0, u1 = ring(h0, "cols", 1), ring(h1, "cols", 3)
    keep, send = call(
        functools.partial(b_kernel, 2.0 * gamma),
        [out((rank // 2, cols))] * 2,
        [VMEM] * 3,
        vec, bq, am,
        scratch=[pltpu.VMEM((rank, cols), F32)],
    )
    half = [out((far, toks))] * 2
    v_up, v_down = call(near_kernel, half, [VMEM] * 2, m, scaled, after=[send])
    keep, send = halve(keep, swap_core(send), near_bit, after=[v_up])
    pieces = call(
        functools.partial(a_kernel, 2.0 * gamma),
        [out((rank, rows // 4))] * 4,
        [VMEM] * 5,
        vec, dy, b, x, m,
        after=[send],
    )
    keep, send = halve(keep, swap_x(send, 0), far_bit, after=[pieces[0]])
    pieces = [pieces[0]] + [ring(pieces[k], "dp", k) for k in (1, 3, 2)]
    v_up, v_down = hold([v_up, v_down], [send, u0, u1])
    v0, v1 = ring(v_up, "cols", 1), ring(v_down, "cols", 3)
    own = call(own_kernel, [out((rows // 4, toks))], [VMEM] * 2, m, scaled, after=[v_up])[0]
    up, down = call(relay_kernel, half, [VMEM] * 4, m, scaled, u0, u1, after=[own])

    piece = add(*pieces, after=[up])
    stack = call(
        b_stack_kernel, [out((rank // 4, cols))], [VMEM] * 3, keep, swap_x(send, 1), vec, after=[piece]
    )[0]
    own = call(gather_kernel, [out((rows // 4, toks))], [VMEM] * 3, own, v0, v1, after=[stack])[0]
    piece = add(piece, swap(piece, "cols", 0), after=[own])
    last = (piece, swap(piece, "cols", 1))
    stack = add(stack, swap(stack, "dp", 0), after=[piece])
    up, down = hold([up, down], [stack])
    w0, w1 = ring(up, "cols", 1), ring(down, "cols", 3)
    piece = [out((rank // 2, rows // 4))] * 2
    top, bottom = call(add_halves_kernel, piece, [VMEM] * 2, *last, after=[up])
    b_part, mag_grad = call(
        functools.partial(b_unstack_kernel, gamma / float(full_rows) ** 0.5),
        [out((rank // 8, cols)), out((1, cols))],
        [VMEM] * 3,
        stack, swap(stack, "dp", 1), vec,
        after=[top],
    )
    b_part = join([b_part, swap_x(b_part, 1)], far_bit, 0)
    top, bottom = call(
        pair_kernel,
        [out((rank, rows // 4))] * 2,
        [VMEM] * 4,
        top, swap(top, "dp", 1), bottom, swap(bottom, "dp", 0),
        after=[b_part],
    )
    grad, done = call(
        finish_kernel, [out((rows // 4, toks), BF16), out((8, 128))], [VMEM] * 3, own, w0, w1, after=[top]
    )
    top_more, bottom_more = hold([swap(top, "dp", 0), swap(bottom, "dp", 1)], [done])
    b_part = join([b_part, swap_x(b_part, 0)], near_bit, 0, after=[top_more])
    a_grad = call(a_join_kernel, [out((rank, rows))], [VMEM] * 4, top, top_more, bottom, bottom_more, after=[b_part])[0]
    b_grad = join([b_part, swap_core(b_part)], core_bit, 0)
    return grad, a_grad.T, b_grad, mag_grad.reshape(cols)


def solution(mesh):
    return jax.shard_map(
        shards,
        mesh=mesh,
        in_specs=(
            P("dp", "rows"),
            P("dp", "cols"),
            P("rows", "cols"),
            P("rows", None),
            P(None, "cols"),
            P("cols"),
        ),
        out_specs=(P(("rows", "cols"), "dp"), P("rows", None), P(None, "cols"), P("cols")),
        check_vma=False,
    )
```
